32 devices in a mesh: head: 4 (over y, x), tok: 8 (over z, core).
Axes of the slice: x: 2, y: 2, z: 4, core: 2. Of those that a mesh axis runs over, the one named last changes fastest.
Arguments:
- stretch_tokens: bfloat16 [8, 1024, 1792], P('tok', 'head'), may hold values from -6 to 6
- stretch_tail: bfloat16 [8, 2, 1792], P('tok'), may hold values from -6 to 6
- decode_tokens: bfloat16 [8, 32, 1792], P('tok'), may hold values from -6 to 6
- decode_tail: bfloat16 [8, 32, 2, 1792], P('tok'), may hold values from -6 to 6
- norm_gain: float32 [1792], replicated, may hold values from 0.1 to 1.9
- conv_taps: float32 [3, 1792], replicated, may hold values from -3 to 3
- qkv_weight: bfloat16 [1792, 16, 144], P(None, 'head'), may hold values from -0.125 to 0.125
- out_gain: float32 [1792], P('head'), may hold values from 0.1 to 1.9
- out_weight: bfloat16 [1792, 1792], P('head'), may hold values from -0.125 to 0.125
- state_cache: float32 [8, 16, 16, 112, 273], P('tok', None, 'head'), may hold values from -24 to 24
- stretch_len: int32 [8], P('tok'), may hold values from 1 to 1024, 4096 in all
- stretch_slot: int32 [8], P('tok'), may hold values from 0 to 15
- decode_slot: int32 [8, 32], P('tok'), may hold values from 0 to 15
- decode_owner: int32 [8, 32, 1], P('tok'), may hold values from 0 to 7; in each aligned block of 32 rows (0 to 31, 32 to 63, ..., all dimensions but the last counted through in order) at most 8 rows name the same one
Outputs:
- stretch_out: bfloat16 [8, 1024, 1792], P('tok', 'head')
- decode_out: bfloat16 [8, 32, 1792], P('tok', 'head')
- state_new: float32 [8, 16, 112, 273], P('tok', 'head')
The draws below stay inside these ranges and needn't reach their ends.
Inputs may be any that keep to these rules, and one draw needn't show every extreme that they name: `decode_owner`: in the 32 decoders of one group at most 8 name the same owner group, a bound that some block reaches of them. `stretch_len`: some group's stretch is full.
All inputs are finite; a program needn't handle non-finite values.
Results may differ from the reference program's by a relative error of at most 0.014.
Values may be sent and summed in bfloat16 or wider, within the bound.
No kernel may reach another device: no remote copies, remote signals or barrier semaphores. Data moves between devices by JAX's collectives and lax.ppermute only.
A program may use at most 64 MiB of HBM per device.

```python
import math
import jax
import jax.numpy as jnp
import numpy as np
from jax import lax

D = 1792
H = 16
DH = 112
F = 16
PHI = 273
STRETCH = 1024
DEC = 32
SLOTS = 16
GROUPS = 8
CAP = 8
N_HEAD = 4


def plant(values, rng, low, high):
    spot = [jax.random.randint(jax.random.fold_in(rng, axis), (), 0, length) for axis, length in enumerate(values.shape)]
    longest = values.shape.index(max(values.shape))
    next_to = spot[:longest] + [(spot[longest] + 1) % values.shape[longest]] + spot[longest + 1:]
    return values.at[tuple(spot)].set(low).at[tuple(next_to)].set(high)


def steps_of(stream_key, extent, split, least, high):
    level, own = 1.0, jax.random.fold_in(stream_key, 6)
    for dim, shards_of in split:
        steps = jnp.exp(jax.random.uniform(jax.random.fold_in(own, dim), (shards_of,), jnp.float32, least / len(split), high / len(split)))
        level = level * jnp.repeat(steps, extent[dim] // shards_of).reshape([-1 if axis == dim else 1 for axis in range(len(extent))])
    return level


def split_up(amount, total, reach, slope):
    weights = [(1 << 20) // math.isqrt(rank ** slope) + 1 for rank in range(2, amount + 1)]
    rest, counts = total - reach - (amount - 1), [1] * (amount - 1)
    while rest > 0:
        free = [i for i in range(amount - 1) if counts[i] < reach]
        pool, left = sum([weights[i] for i in free]), rest
        for i in free:
            addition = min(reach - counts[i], max(1, left * weights[i] // pool), rest)
            counts[i] = counts[i] + addition
            rest = rest - addition
    return np.array([reach] + counts)


def ragged(rng, count, total, limit, skew):
    if count == 2:
        one = jax.random.randint(rng, (), max(1, total - limit), min(limit, total - 1) + 1)
        return jnp.stack([one, total - one])
    tallies = jnp.asarray(split_up(count, total, limit, skew), jnp.int32)
    pairs = (count - 1) // 2
    giver, receiver = tallies[1:1 + 2 * pairs:2], tallies[2:2 + 2 * pairs:2]
    room = jnp.minimum(giver - 1, limit - receiver)
    shifted = jax.random.randint(jax.random.fold_in(rng, 1), (pairs,), 0, 1 << 20) % (room + 1)
    tallies = tallies.at[1:1 + 2 * pairs:2].set(giver - shifted).at[2:2 + 2 * pairs:2].set(receiver + shifted)
    return tallies[jax.random.permutation(jax.random.fold_in(rng, 2), count)]


def deal_out(stream_key, own, number, rows, number_of, top, limit, skew):
    sequence = jax.random.permutation(stream_key, number_of)
    heavy_load, usual = load_shares(number_of, rows * top, limit, skew, True), load_shares(number_of, rows * top, limit, skew, False)
    places = jnp.arange(number_of)

    def named(lengths, rotation):
        used = int((lengths > 0).sum())
        fixed = max(1, used // 4)
        passed = fixed + (places - fixed + rotation * (used - fixed)) % max(1, number_of - fixed)
        return jnp.zeros((number_of,), jnp.int32).at[sequence[jnp.where(places < fixed, places, passed)]].set(jnp.asarray(lengths, jnp.int32))

    lengths = jnp.where(number % 4 == 0, named(heavy_load, number // 4), named(usual, number - number // 4 - 1))
    mixed = jax.random.permutation(jax.random.fold_in(own, 3), number_of)
    source_of, sink = mixed[0:number_of // 2 * 2:2], mixed[1:number_of // 2 * 2:2]
    slack = jnp.minimum(lengths[source_of] - 1, limit - lengths[sink]) // 2
    slack = jnp.where((source_of == sequence[0]) | (sink == sequence[0]) | (lengths[sink] == 0), 0, jnp.maximum(slack, 0))
    passed = jax.random.randint(jax.random.fold_in(own, 4), (number_of // 2,), 0, 1 << 20) % (slack + 1)
    lengths = lengths.at[source_of].add(-passed).at[sink].add(passed)
    labels = jnp.searchsorted(jnp.cumsum(lengths), jnp.arange(rows * top), side="right").astype(jnp.int32)
    listing = labels.reshape(top, rows).T
    listing = listing[jax.random.permutation(jax.random.fold_in(own, 1), rows)]
    rotation = jax.random.randint(jax.random.fold_in(own, 2), (rows, 1), 0, top)
    return jnp.take_along_axis(listing, (jnp.arange(top)[None, :] + rotation) % top, axis=1)


def load_shares(count, total, most, lean, full):
    weights = [(1 << 20) // math.isqrt(standing ** lean) + 1 for standing in range(1, count + 1)]
    largest = most if full else min(most, max(-(-total // count), total * weights[0] // sum(weights)))
    least = 1 if total - largest >= count - 1 else 0
    given, spare = [largest] + [least] * (count - 1), total - largest - least * (count - 1)
    while spare > 0:
        candidates = [i for i in range(1, count) if given[i] < largest] or [i for i in range(1, count) if given[i] < most]
        pool, remaining = sum([weights[i] for i in candidates]), spare
        for i in candidates:
            more = min(most - given[i], max(1, remaining * weights[i] // pool), spare)
            given[i] = given[i] + more
            spare = spare - more
    return np.array(given)


def centred(key, dims, spread, most, split=(), kind=jnp.bfloat16):
    entries = jax.random.normal(key, dims, jnp.float32) * spread
    if len(split) > 0:
        entries = steps_of(key, dims, split, -0.22, 0.18) * entries
    return jnp.clip(entries, min=-most, max=most).astype(kind)


def setup_inputs(seed: int = 0) -> dict:
    arg_keys = jax.random.split(jax.random.key(seed), 15)
    stretch_tokens = centred(arg_keys[0], (GROUPS, STRETCH, D), 1.0, 6.0, ((0, 8), (1, 4)))
    stretch_tail = centred(arg_keys[1], (GROUPS, 2, D), 1.0, 6.0, ((0, 8),))
    decode_tokens = centred(arg_keys[2], (GROUPS, DEC, D), 1.0, 6.0, ((0, 8),))
    decode_tail = centred(arg_keys[3], (GROUPS, DEC, 2, D), 1.0, 6.0, ((0, 8),))
    norm_gain = jnp.clip(1.0 + 0.18 * jax.random.normal(arg_keys[4], (D,), jnp.float32), 0.1, 1.9)
    conv_taps = centred(arg_keys[5], (3, D), 0.6, 3.0, (), jnp.float32)
    qkv_weight = centred(arg_keys[6], (D, H, 2 * F + DH), D ** -0.5, 0.125, ((1, 4),))
    out_gain = jnp.clip(1.0 + 0.18 * jax.random.normal(arg_keys[7], (H * DH,), jnp.float32), 0.1, 1.9)
    out_weight = centred(arg_keys[8], (H * DH, D), (H * DH) ** -0.5, 0.125, ((0, 4),))
    state_cache = centred(arg_keys[9], (GROUPS, SLOTS, H, DH, PHI), 4.0, 24.0, ((0, 8), (2, 4)), jnp.float32)
    stretch_len = ragged(arg_keys[10], GROUPS, GROUPS * STRETCH // 2, STRETCH, 2).astype(jnp.int32)
    stretch_slot = plant(jax.random.randint(arg_keys[11], (GROUPS,), 0, SLOTS), jax.random.fold_in(arg_keys[11], 1), 0, SLOTS - 1).astype(jnp.int32)
    decode_slot = plant(jax.random.randint(arg_keys[12], (GROUPS, DEC), 0, SLOTS), jax.random.fold_in(arg_keys[12], 1), 0, SLOTS - 1).astype(jnp.int32)
    decode_owner_keys = jax.random.split(jax.random.fold_in(arg_keys[13], 1), GROUPS * DEC // DEC)
    decode_owner_turns = jax.random.permutation(jax.random.fold_in(arg_keys[13], 3), GROUPS * DEC // DEC)
    decode_owner = jax.vmap(lambda own, number: deal_out(jax.random.fold_in(arg_keys[13], 2), own, number, DEC, GROUPS, 1, CAP, 2))(decode_owner_keys, decode_owner_turns).reshape((GROUPS, DEC, 1))
    return dict(stretch_tokens=stretch_tokens, stretch_tail=stretch_tail, decode_tokens=decode_tokens, decode_tail=decode_tail, norm_gain=norm_gain, conv_taps=conv_taps, qkv_weight=qkv_weight, out_gain=out_gain, out_weight=out_weight, state_cache=state_cache, stretch_len=stretch_len, stretch_slot=stretch_slot, decode_slot=decode_slot, decode_owner=decode_owner)


def rms_rows(values, gain):
    values = values.astype(jnp.float32)
    factor = lax.rsqrt(lax.optimization_barrier(jnp.mean(values * values, axis=-1, keepdims=True)) + 1e-05)
    return values * factor * gain

def features(vectors):
    breadth = vectors.shape[-1]
    linear = vectors / math.sqrt(math.sqrt(breadth))
    outer = vectors[..., :, None] * vectors[..., None, :] / math.sqrt(2.0 * breadth)
    outer = outer.reshape(vectors.shape[:-1] + (breadth * breadth,))
    ones = jnp.ones(vectors.shape[:-1] + (1,), vectors.dtype)
    return jnp.concatenate([ones, linear, outer], axis=-1)

def convolve(tail, normed, conv_taps):
    joined = jnp.concatenate([tail, normed], axis=-2).astype(jnp.float32)
    span_rows = normed.shape[-2]
    total = conv_taps[0] * joined[..., 0:span_rows, :]
    total = total + conv_taps[1] * joined[..., 1:span_rows + 1, :]
    total = total + conv_taps[2] * joined[..., 2:span_rows + 2, :]
    return total.astype(jnp.bfloat16)

def project_out(attended, out_weight):
    row_total = attended.shape[0]
    share_width = H // N_HEAD * DH
    split_rows = attended.reshape(row_total, N_HEAD, share_width).astype(jnp.float32)
    grouped_weight = out_weight.reshape(N_HEAD, share_width, D).astype(jnp.float32)
    partial_value = jnp.einsum('ngk,gkd->gnd', split_rows, grouped_weight).astype(jnp.bfloat16)
    partial_value = lax.optimization_barrier(partial_value).astype(jnp.float32)
    return lax.optimization_barrier(jnp.sum(partial_value, axis=0)).astype(jnp.bfloat16)

def reference(stretch_tokens, stretch_tail, decode_tokens, decode_tail, norm_gain, conv_taps, qkv_weight, out_gain, out_weight, state_cache, stretch_len, stretch_slot, decode_slot, decode_owner):
    block_width = 2 * F + DH
    w_flat = qkv_weight.reshape(D, H * block_width)
    gains = out_gain.reshape(H, DH)

    def one_stretch(inputs):
        tokens, tail, length, slot_now, cache_group = inputs
        normed = rms_rows(tokens, norm_gain).astype(jnp.bfloat16)
        conved = convolve(tail, normed, conv_taps)
        qkv = jnp.dot(conved, w_flat, preferred_element_type=jnp.float32).astype(jnp.bfloat16)
        qkv = qkv.reshape(STRETCH, H, block_width).astype(jnp.float32)
        queries = qkv[:, :, :F]
        key_feats = qkv[:, :, F:2 * F]
        values = qkv[:, :, 2 * F:]
        positions = jnp.arange(STRETCH)
        valid_rows = positions < length
        state_old = lax.dynamic_index_in_dim(cache_group, slot_now.astype(jnp.int32), 0, keepdims=False)
        inner = jnp.einsum('ihf,jhf->hij', queries, key_feats) / math.sqrt(F)
        weights = 1.0 + inner + 0.5 * inner * inner
        allowed = (positions[None, :] <= positions[:, None]) & valid_rows[None, :]
        weights = jnp.where(allowed[None], weights, 0.0).astype(jnp.bfloat16)
        weights = lax.optimization_barrier(weights).astype(jnp.float32)
        local_sum = jnp.einsum('hij,jhd->ihd', weights, values)
        carried = jnp.einsum('ihp,hdp->ihd', features(queries), state_old, precision=lax.Precision.HIGHEST)
        attended = rms_rows(carried + local_sum, gains)
        attended = jnp.where(valid_rows[:, None, None], attended, 0.0).astype(jnp.bfloat16).reshape(STRETCH, H * DH)
        key_phi = jnp.where(valid_rows[:, None, None], features(key_feats), 0.0).astype(jnp.bfloat16)
        key_phi = lax.optimization_barrier(key_phi).astype(jnp.float32)
        state_next = state_old + jnp.einsum('jhd,jhp->hdp', values, key_phi, precision=lax.Precision.HIGHEST)
        return (project_out(attended, out_weight), state_next)
    stretch_out, state_new = lax.map(one_stretch, (stretch_tokens, stretch_tail, stretch_len, stretch_slot, state_cache))

    def one_decode(inputs):
        tokens, tail, owners, slots_now = inputs
        normed = rms_rows(tokens, norm_gain).astype(jnp.bfloat16)
        conved = convolve(tail, normed[:, None, :], conv_taps)[:, 0, :]
        qkv = jnp.dot(conved, w_flat, preferred_element_type=jnp.float32).astype(jnp.bfloat16)
        qkv = qkv.reshape(DEC, H, block_width).astype(jnp.float32)
        queries = qkv[:, :, :F]
        key_feats = qkv[:, :, F:2 * F]
        values = qkv[:, :, 2 * F:]
        states = state_cache[owners.astype(jnp.int32), slots_now.astype(jnp.int32)]
        carried = jnp.einsum('ehp,ehdp->ehd', features(queries), states, precision=lax.Precision.HIGHEST)
        inner = lax.optimization_barrier(jnp.sum(queries * key_feats, axis=-1)) / math.sqrt(F)
        own_term = (1.0 + inner + 0.5 * inner * inner)[..., None] * values
        attended = rms_rows(carried + own_term, gains).astype(jnp.bfloat16).reshape(DEC, H * DH)
        return project_out(attended, out_weight)
    decode_out = lax.map(one_decode, (decode_tokens, decode_tail, decode_owner[:, :, 0], decode_slot))
    return (stretch_out, decode_out, state_new)
```

```python
import functools
import math

import jax
import jax.numpy as jnp
import numpy as np
from jax import lax
from jax.experimental import pallas as pl
from jax.experimental.pallas import tpu as pltpu
from jax.sharding import PartitionSpec as P

D = 1792
DH = 112
F = 16
STRETCH = 1024
DEC = 32
PHI = 1 + F + F * F
WIDE = 128
PHI_WIDE = 384
MIB = 1 << 20


def selectors():
    first = np.zeros((F, PHI_WIDE), np.float32)
    second = np.zeros((F, PHI_WIDE), np.float32)
    for a in range(F):
        first[a, 1 + a] = 1.0
        for b in range(F):
            first[a, 1 + F + a * F + b] = 1.0
            second[b, 1 + F + a * F + b] = 1.0
    return jnp.asarray(first, jnp.bfloat16), jnp.asarray(second, jnp.bfloat16)


def dot(left, right, contract=((1,), (0,))):
    return lax.dot_general(left, right, (contract, ((), ())), preferred_element_type=jnp.float32)


def phi_of(vectors, first, second):
    a = dot(vectors, first)
    b = dot(vectors, second)
    lane = lax.broadcasted_iota(jnp.int32, a.shape, 1)
    scale = jnp.where(lane <= F, 1.0 / math.sqrt(math.sqrt(F)), b * (1.0 / math.sqrt(2.0 * F)))
    return jnp.where(lane == 0, 1.0, a * scale)


def unit_rows(values):
    values = values.astype(jnp.float32)
    total = jnp.sum(values * values, axis=-1, keepdims=True)
    return values, lax.rsqrt(total * (1.0 / D) + 1e-05)


def conv_kernel(first_ref, tokens_ref, rim_ref, tail_ref, gain_ref, taps_ref, out_ref):
    rows = tokens_ref.shape[0]
    _, factor = unit_rows(tokens_ref[...])
    rim, rim_factor = unit_rows(rim_ref[...])
    rim = (rim * rim_factor * gain_ref[...]).astype(jnp.bfloat16).astype(jnp.float32)
    rim = jnp.where(first_ref[0] == 0, tail_ref[...].astype(jnp.float32), rim)
    step = 256
    row = lax.broadcasted_iota(jnp.int32, (rows, step), 0)
    for at in range(0, D, step):
        cols = slice(at, at + step)
        normed = tokens_ref[:, cols].astype(jnp.float32) * factor * gain_ref[:, cols]
        normed = normed.astype(jnp.bfloat16).astype(jnp.float32)
        one = jnp.where(row == 0, rim[1:2, cols], pltpu.roll(normed, 1, 0))
        two = pltpu.roll(normed, 2, 0)
        two = jnp.where(row == 0, rim[0:1, cols], jnp.where(row == 1, rim[1:2, cols], two))
        total = taps_ref[0:1, cols] * two + taps_ref[1:2, cols] * one + taps_ref[2:3, cols] * normed
        out_ref[:, cols] = total.astype(jnp.bfloat16)


def block_kernel(slot, heads, meta_ref, conved_ref, w_ref, a_ref, b_ref, q_ref, local_ref, sums_ref):
    rows = conved_ref.shape[0]
    qkv = dot(conved_ref[...], w_ref[...]).astype(jnp.bfloat16)
    q_ref[...] = qkv[:, : heads * F]
    live = meta_ref[1] - rows * (meta_ref[2] ^ slot)
    row = lax.broadcasted_iota(jnp.int32, (rows, rows), 0)
    col = lax.broadcasted_iota(jnp.int32, (rows, rows), 1)
    allowed = (col <= row) & (col < live)
    live_row = lax.broadcasted_iota(jnp.int32, (rows, PHI_WIDE), 0) < live
    for head in range(heads):
        q = qkv[:, head * F : head * F + F]
        k = qkv[:, (heads + head) * F : (heads + head) * F + F]
        at = 2 * heads * F + head * WIDE
        v = qkv[:, at : at + WIDE]
        inner = dot(q, k, ((1,), (1,))) * (1.0 / math.sqrt(F))
        weights = jnp.where(allowed, 1.0 + inner + 0.5 * inner * inner, 0.0).astype(jnp.bfloat16)
        local_ref[:, head * WIDE : (head + 1) * WIDE] = dot(weights, v)
        key_phi = phi_of(k, a_ref[...], b_ref[...])
        key_phi = jnp.where(live_row, key_phi, 0.0).astype(jnp.bfloat16)
        total = dot(v, key_phi, ((0,), (0,)))
        sums_ref[head] = total[:DH, :PHI]


def finish_kernel(slots, heads, keep, meta_ref, *refs):
    q_refs = refs[: len(slots)]
    local_refs = refs[len(slots) : 2 * len(slots)]
    sums_refs = refs[2 * len(slots) : 2 * len(slots) + 4]
    old_ref, a_ref, b_ref, gain_ref, w_ref = refs[2 * len(slots) + 4 : 2 * len(slots) + 9]
    outs = refs[2 * len(slots) + 9 :]
    state = outs[-1]
    mine = meta_ref[2]
    rows = q_refs[0].shape[0]
    state[...] = jnp.zeros_like(state)
    for order, slot in enumerate(slots):
        block = mine ^ slot
        live = meta_ref[1] - rows * block
        live_row = lax.broadcasted_iota(jnp.int32, (rows, WIDE), 0) < live
        parts = []
        for head in range(heads):
            before = old_ref[0, 0, head]
            for other in range(4):
                if other != slot:
                    use = ((mine ^ other) < block).astype(jnp.float32)
                    before = before + use * sums_refs[other][head]
            state[head, :DH, :PHI] = before.astype(jnp.bfloat16)
            q = q_refs[order][:, head * F : head * F + F]
            query_phi = phi_of(q, a_ref[...], b_ref[...]).astype(jnp.bfloat16)
            total = local_refs[order][:, head * WIDE : (head + 1) * WIDE]
            total = total + dot(query_phi, state[head], ((1,), (1,)))
            square = jnp.sum(total * total, axis=-1, keepdims=True)
            total = total * lax.rsqrt(square * (1.0 / DH) + 1e-05) * gain_ref[head : head + 1, :]
            parts.append(jnp.where(live_row, total, 0.0).astype(jnp.bfloat16))
        attended = jnp.concatenate(parts, axis=1)
        outs[order][...] = dot(attended, w_ref[...]).astype(jnp.bfloat16)
    if keep:
        for head in range(heads):
            after = old_ref[0, 0, head]
            for other in range(4):
                after = after + sums_refs[other][head]
            outs[len(slots)][0, head] = after


def send_kernel(
    heads, capacity, tokens_ref, tail0_ref, tail1_ref, gain_ref, taps_ref, w_ref, col_ref, row_ref, slot_ref, out_ref
):
    tokens, factor = unit_rows(tokens_ref[...])
    normed = (tokens * factor * gain_ref[...]).astype(jnp.bfloat16).astype(jnp.float32)
    conved = taps_ref[0:1, :] * tail0_ref[...].astype(jnp.float32)
    conved = conved + taps_ref[1:2, :] * tail1_ref[...].astype(jnp.float32)
    conved = (conved + taps_ref[2:3, :] * normed).astype(jnp.bfloat16)
    qkv = dot(conved, w_ref[...]).astype(jnp.bfloat16)
    owners = row_ref[...]
    m = lax.broadcasted_iota(jnp.int32, (DEC, DEC), 0)
    n = lax.broadcasted_iota(jnp.int32, (DEC, DEC), 1)
    rank = jnp.sum(jnp.where((m < n) & (col_ref[...] == owners), 1, 0), axis=0, keepdims=True)
    target = owners * capacity + rank
    total = out_ref.shape[0]
    placing = lax.broadcasted_iota(jnp.int32, (total, DEC), 0) == target
    sent = dot(jnp.where(placing, 1.0, 0.0).astype(jnp.bfloat16), qkv)
    cache_slot = jnp.sum(jnp.where(placing, slot_ref[...] + 1, 0), axis=1, keepdims=True) - 1
    lane = lax.broadcasted_iota(jnp.int32, sent.shape, 1)
    mark = 2 * heads * F + DH
    out_ref[...] = jnp.where(lane == mark, cache_slot.astype(jnp.float32), sent).astype(jnp.bfloat16)


def serve_kernel(heads, items_ref, cache_ref, a_ref, b_ref, gain_ref, out_ref, phis, total, slots):
    step = pl.program_id(0)
    count = items_ref.shape[0]

    @pl.when(step == 0)
    def _():
        total[...] = jnp.zeros_like(total)
        for head in range(heads):
            q = items_ref[:, head * F : head * F + F]
            phis[head] = phi_of(q, a_ref[...], b_ref[...]).astype(jnp.bfloat16)
        slab = items_ref[:, 2 * heads * F : 2 * heads * F + WIDE].astype(jnp.float32)
        slots[...] = slab.T[DH : DH + 1, :]

    here = slots[...] == step.astype(jnp.float32)
    for head in range(heads):
        state = cache_ref[0, 0, head].astype(jnp.bfloat16)
        table = dot(state, phis[head][:, :PHI], ((1,), (1,)))
        total[head, :DH, :] += jnp.where(here, table, 0.0)

    @pl.when(step == pl.num_programs(0) - 1)
    def _():
        lane = lax.broadcasted_iota(jnp.int32, (count, WIDE), 1)
        for head in range(heads):
            q = items_ref[:, head * F : head * F + F].astype(jnp.float32)
            k = items_ref[:, (heads + head) * F : (heads + head) * F + F].astype(jnp.float32)
            at = 2 * heads * F + head * WIDE
            v = items_ref[:, at : at + WIDE].astype(jnp.float32)
            inner = jnp.sum(q * k, axis=-1, keepdims=True) * (1.0 / math.sqrt(F))
            value = total[head].T + (1.0 + inner + 0.5 * inner * inner) * v
            value = jnp.where(lane < DH, value, 0.0)
            square = jnp.sum(value * value, axis=-1, keepdims=True)
            value = value * lax.rsqrt(square * (1.0 / DH) + 1e-05) * gain_ref[head : head + 1, :]
            out_ref[:, head * WIDE : (head + 1) * WIDE] = value.astype(jnp.bfloat16)


def return_kernel(capacity, items_ref, col_ref, row_ref, w_ref, out_ref):
    owners = col_ref[...]
    n = lax.broadcasted_iota(jnp.int32, (DEC, DEC), 0)
    m = lax.broadcasted_iota(jnp.int32, (DEC, DEC), 1)
    rank = jnp.sum(jnp.where((m < n) & (row_ref[...] == owners), 1, 0), axis=1, keepdims=True)
    target = owners * capacity + rank
    placing = lax.broadcasted_iota(jnp.int32, (DEC, items_ref.shape[0]), 1) == target
    attended = dot(jnp.where(placing, 1.0, 0.0).astype(jnp.bfloat16), items_ref[...]).astype(jnp.bfloat16)
    out_ref[...] = dot(attended, w_ref[...]).astype(jnp.bfloat16)


def whole(count):
    return [pl.BlockSpec(memory_space=pltpu.VMEM)] * count


def call(kernel, outs, flops, size, smem=0, scratch=(), vmem=24):
    def run(*args):
        many = isinstance(outs, (list, tuple))
        return pl.pallas_call(
            kernel,
            out_shape=outs,
            in_specs=[pl.BlockSpec(memory_space=pltpu.SMEM)] * smem + whole(len(args) - smem),
            out_specs=whole(len(outs)) if many else whole(1)[0],
            scratch_shapes=list(scratch),
            compiler_params=pltpu.CompilerParams(vmem_limit_bytes=vmem * MIB),
            cost_estimate=pl.CostEstimate(flops=flops, bytes_accessed=size, transcendentals=0),
        )(*args)

    return run


def shape(*dims, dtype=jnp.bfloat16):
    return jax.ShapeDtypeStruct(dims, dtype)


def across(array, by):
    return lax.ppermute(array, "head", [(i, i ^ by) for i in range(4)])


def local_square(
    stretch_tokens,
    stretch_tail,
    decode_tokens,
    decode_tail,
    norm_gain,
    conv_taps,
    qkv_weight,
    out_gain,
    out_weight,
    state_cache,
    stretch_len,
    stretch_slot,
    decode_slot,
    decode_owner,
):
    heads = qkv_weight.shape[1]
    rows = stretch_tokens.shape[1]
    half = rows // 2
    me = lax.axis_index("head")
    meta = jnp.stack([stretch_slot[0], stretch_len[0], me]).astype(jnp.int32)
    gain = norm_gain.reshape(1, D)
    first, second = selectors()

    rim = from_behind(stretch_tokens[0, rows - 2 :], "head", 1)

    w_qk = [qkv_weight[:, :, :F].reshape(D, heads * F), qkv_weight[:, :, F : 2 * F].reshape(D, heads * F)]
    w_v = jnp.pad(qkv_weight[:, :, 2 * F :], ((0, 0), (0, 0), (0, WIDE - DH))).reshape(D, heads * WIDE)
    w_in = jnp.concatenate(w_qk + [w_v], axis=1)
    wide = w_in.shape[1]
    w_out = jnp.pad(out_weight.reshape(heads, DH, D), ((0, 0), (0, WIDE - DH), (0, 0))).reshape(heads * WIDE, D)
    gains = jnp.pad(out_gain.reshape(heads, DH), ((0, 0), (0, WIDE - DH)))

    conved = call(conv_kernel, shape(rows, D), 20 * rows * D, 4 * rows * D, smem=1)(
        me.reshape(1), stretch_tokens[0], rim, stretch_tail[0], gain, conv_taps
    )
    from_x = across(conved, 1)
    from_y = across(conved, 2)

    groups = lax.axis_size("tok")
    capacity = max(2, 2 * DEC // groups)
    count = groups * capacity
    owner_col = decode_owner[0]
    owner_row = owner_col.reshape(1, DEC)
    sent = call(functools.partial(send_kernel, heads, capacity), shape(count, wide), 2 * DEC * D * wide, 2 * D * wide)(
        decode_tokens[0], decode_tail[0, :, 0], decode_tail[0, :, 1], gain, conv_taps, w_in, owner_col, owner_row, decode_slot
    )
    items = lax.all_to_all(sent.reshape(groups, capacity, wide), "tok", split_axis=0, concat_axis=0, tiled=True)
    items = items.reshape(count, wide)
    cache_slots = state_cache.shape[1]
    served = pl.pallas_call(
        functools.partial(serve_kernel, heads),
        grid=(cache_slots,),
        in_specs=[
            pl.BlockSpec((count, wide), lambda i: (0, 0)),
            pl.BlockSpec((1, 1, heads, DH, PHI), lambda i: (0, i, 0, 0, 0)),
            pl.BlockSpec((F, PHI_WIDE), lambda i: (0, 0)),
            pl.BlockSpec((F, PHI_WIDE), lambda i: (0, 0)),
            pl.BlockSpec((heads, WIDE), lambda i: (0, 0)),
        ],
        out_specs=pl.BlockSpec((count, heads * WIDE), lambda i: (0, 0)),
        out_shape=shape(count, heads * WIDE),
        scratch_shapes=[
            pltpu.VMEM((heads, count, PHI_WIDE), jnp.bfloat16),
            pltpu.VMEM((heads, WIDE, count), jnp.float32),
            pltpu.VMEM((1, count), jnp.float32),
        ],
        compiler_params=pltpu.CompilerParams(vmem_limit_bytes=24 * MIB),
        cost_estimate=pl.CostEstimate(
            flops=2 * cache_slots * heads * DH * PHI * count, bytes_accessed=4 * cache_slots * heads * DH * PHI_WIDE, transcendentals=0
        ),
    )(items, state_cache, first, second, gains)
    returned = lax.all_to_all(
        served.reshape(groups, capacity, heads * WIDE), "tok", split_axis=0, concat_axis=0, tiled=True
    ).reshape(count, heads * WIDE)

    def block(slot, block_rows):
        return call(
            functools.partial(block_kernel, slot, heads),
            [shape(rows, heads * F), shape(rows, heads * WIDE, dtype=jnp.float32), shape(heads, DH, PHI, dtype=jnp.float32)],
            2 * rows * D * wide + 6 * heads * rows * rows * WIDE,
            2 * (rows * D + D * wide),
            smem=1,
        )(meta, block_rows, w_in, first, second)

    blocks = [block(0, conved), block(1, from_x), block(2, from_y)]
    from_xy = jnp.concatenate([across(from_x[:half], 2), across(from_y[half:], 1)], axis=0)
    blocks.append(block(3, from_xy))

    def finish(slots, keep=False):
        outs = [shape(rows, D)] * len(slots)
        if keep:
            outs = outs + [shape(1, heads, DH, PHI, dtype=jnp.float32)]
        args = [blocks[s][0] for s in slots] + [blocks[s][1] for s in slots] + [b[2] for b in blocks]
        args = args + [state_cache, first, second, gains, w_out]

        def fixed(dims):
            return pl.BlockSpec(dims, lambda i, meta_ref: (0,) * len(dims))

        specs = [fixed(a.shape) for a in args]
        specs[-5] = pl.BlockSpec((1, 1, heads, DH, PHI), lambda i, meta_ref: (0, meta_ref[0], 0, 0, 0))
        return pl.pallas_call(
            functools.partial(finish_kernel, slots, heads, keep),
            grid_spec=pltpu.PrefetchScalarGridSpec(
                num_scalar_prefetch=1,
                grid=(1,),
                in_specs=specs,
                out_specs=[fixed(o.shape) for o in outs],
                scratch_shapes=[pltpu.VMEM((heads, WIDE, PHI_WIDE), jnp.bfloat16)],
            ),
            out_shape=outs,
            compiler_params=pltpu.CompilerParams(vmem_limit_bytes=40 * MIB),
            cost_estimate=pl.CostEstimate(
                flops=len(slots) * 2 * rows * heads * WIDE * (D + PHI_WIDE), bytes_accessed=2 * rows * D * len(slots), transcendentals=0
            ),
        )(meta, *args)

    (p3,) = finish((3,))
    via_x = across(p3[:half], 1)
    via_y = across(p3[half:], 2)
    p1, p2 = finish((1, 2))
    top_x = across(p1[:half], 1)
    low_y = across(p2[half:], 2)
    p0, state_next = finish((0,), keep=True)
    f32 = jnp.float32
    top_y = across((p2[:half].astype(f32) + via_x.astype(f32)).astype(jnp.bfloat16), 2)
    low_x = across((p1[half:].astype(f32) + via_y.astype(f32)).astype(jnp.bfloat16), 1)
    top = p0[:half].astype(f32) + top_x.astype(f32) + top_y.astype(f32)
    low = p0[half:].astype(f32) + low_x.astype(f32) + low_y.astype(f32)
    stretch_out = jnp.concatenate([top, low], axis=0).astype(jnp.bfloat16)

    part = call(functools.partial(return_kernel, capacity), shape(DEC, D), 2 * DEC * heads * WIDE * D, 2 * heads * WIDE * D)(
        returned, owner_col, owner_row, w_out
    )
    shares = lax.all_to_all(part.reshape(4, DEC // 4, D), "head", split_axis=0, concat_axis=0, tiled=True)
    decode_out = jnp.sum(shares.astype(f32), axis=0).astype(jnp.bfloat16)
    return (stretch_out[None], decode_out[None], state_next)


def from_behind(array, axis, by):
    peers = lax.axis_size(axis)
    pairs = [(i, i + by) for i in range(peers) if 0 <= i + by < peers]
    return lax.ppermute(array, axis, pairs)


def rms_rows(values, gain):
    values = values.astype(jnp.float32)
    factor = lax.rsqrt(jnp.mean(values * values, axis=-1, keepdims=True) + 1e-05)
    return values * factor * gain


def features(vectors):
    breadth = vectors.shape[-1]
    linear = vectors / math.sqrt(math.sqrt(breadth))
    outer = vectors[..., :, None] * vectors[..., None, :] / math.sqrt(2.0 * breadth)
    outer = outer.reshape(vectors.shape[:-1] + (breadth * breadth,))
    ones = jnp.ones(vectors.shape[:-1] + (1,), vectors.dtype)
    return jnp.concatenate([ones, linear, outer], axis=-1)


def convolve(tail, normed, conv_taps):
    joined = jnp.concatenate([tail, normed], axis=-2).astype(jnp.float32)
    span_rows = normed.shape[-2]
    total = conv_taps[0] * joined[..., 0:span_rows, :]
    total = total + conv_taps[1] * joined[..., 1 : span_rows + 1, :]
    total = total + conv_taps[2] * joined[..., 2 : span_rows + 2, :]
    return total.astype(jnp.bfloat16)


def decode_items(items, slot_items, cache_own, out_gain, head_count):
    item_count = items.shape[0]
    shaped = items.reshape(item_count, head_count, 2 * F + DH).astype(jnp.float32)
    queries = shaped[:, :, :F]
    key_feats = shaped[:, :, F : 2 * F]
    values = shaped[:, :, 2 * F :]
    slot_total = cache_own.shape[0]
    table = jnp.einsum(
        "nhp,shdp->nshd", features(queries), cache_own, precision=lax.Precision.HIGHEST
    )
    picker = (slot_items[:, None] == jnp.arange(slot_total)[None, :]).astype(jnp.float32)
    carried = jnp.einsum("ns,nshd->nhd", picker, table, precision=lax.Precision.HIGHEST)
    inner = jnp.sum(queries * key_feats, axis=-1) / math.sqrt(F)
    own_term = (1.0 + inner + 0.5 * inner * inner)[..., None] * values
    attended = rms_rows(carried + own_term, out_gain.reshape(head_count, DH))
    return attended.astype(jnp.bfloat16).reshape(item_count, head_count * DH)


def local(
    stretch_tokens,
    stretch_tail,
    decode_tokens,
    decode_tail,
    norm_gain,
    conv_taps,
    qkv_weight,
    out_gain,
    out_weight,
    state_cache,
    stretch_len,
    stretch_slot,
    decode_slot,
    decode_owner,
):
    head_count = qkv_weight.shape[1]
    block_width = qkv_weight.shape[2]
    rows_own = stretch_tokens.shape[1]
    w_flat = qkv_weight.reshape(D, head_count * block_width)
    gains = out_gain.reshape(head_count, DH)
    normed = rms_rows(stretch_tokens[0], norm_gain).astype(jnp.bfloat16)
    rim_rows = from_behind(normed[rows_own - 2 :], "head", 1)
    first_dev = lax.axis_index("head") == 0
    rim_rows = jnp.where(first_dev, stretch_tail[0], rim_rows)
    conved = convolve(rim_rows, normed, conv_taps)
    grouped = jnp.dot(
        lax.all_gather(conved, "head", axis=0, tiled=True),
        w_flat,
        preferred_element_type=jnp.float32,
    ).astype(jnp.bfloat16)
    grouped = grouped.reshape(STRETCH, head_count, block_width)
    queries = grouped[:, :, :F]
    key_feats = grouped[:, :, F : 2 * F]
    values = grouped[:, :, 2 * F :]
    length = stretch_len[0]
    positions = jnp.arange(STRETCH)
    valid_rows = positions < length
    state_old = lax.dynamic_index_in_dim(state_cache[0], stretch_slot[0], 0, keepdims=False)
    carried = jnp.einsum(
        "ihp,hdp->ihd",
        features(queries.astype(jnp.float32)),
        state_old,
        precision=lax.Precision.HIGHEST,
    )
    block_rows = min(512, STRETCH)
    pieces = []
    for anchor in range(0, STRETCH, block_rows):
        finish = anchor + block_rows
        inner = jnp.einsum(
            "ihf,jhf->hij",
            queries[anchor:finish],
            key_feats[:finish],
            preferred_element_type=jnp.float32,
        ) / math.sqrt(F)
        weights = 1.0 + inner + 0.5 * inner * inner
        allowed = (positions[None, :finish] <= positions[anchor:finish, None]) & valid_rows[
            None, :finish
        ]
        weights = jnp.where(allowed[None], weights, 0.0).astype(jnp.bfloat16)
        pieces.append(
            jnp.einsum("hij,jhd->ihd", weights, values[:finish], preferred_element_type=jnp.float32)
        )
    local_sum = jnp.concatenate(pieces, axis=0)
    attended = rms_rows(carried + local_sum, gains)
    attended = (
        jnp.where(valid_rows[:, None, None], attended, 0.0)
        .astype(jnp.bfloat16)
        .reshape(STRETCH, head_count * DH)
    )
    key_phi = jnp.where(
        valid_rows[:, None, None], features(key_feats.astype(jnp.float32)), 0.0
    ).astype(jnp.bfloat16)
    state_next = state_old + jnp.einsum(
        "jhd,jhp->hdp", values, key_phi, preferred_element_type=jnp.float32
    )
    part_rows = attended
    stretch_out = lax.psum_scatter(
        jnp.dot(part_rows, out_weight, preferred_element_type=jnp.float32).astype(jnp.bfloat16),
        "head",
        scatter_dimension=0,
        tiled=True,
    )
    dec_normed = rms_rows(decode_tokens[0], norm_gain).astype(jnp.bfloat16)
    dec_conved = convolve(decode_tail[0], dec_normed[:, None, :], conv_taps)[:, 0, :]
    dec_qkv = jnp.dot(dec_conved, w_flat, preferred_element_type=jnp.float32).astype(jnp.bfloat16)
    owners = decode_owner[0, :, 0]
    slots_here = decode_slot[0]
    groups = lax.axis_size("tok")
    capacity = max(2, 2 * DEC // groups)
    earlier = jnp.arange(DEC)[None, :] < jnp.arange(DEC)[:, None]
    same_owner = owners[None, :] == owners[:, None]
    rank_in = jnp.sum(earlier & same_owner, axis=1)
    target = owners * capacity + rank_in
    placing = jnp.arange(groups * capacity)[:, None] == target[None, :]
    sent_rows = jnp.dot(
        placing.astype(jnp.bfloat16), dec_qkv, preferred_element_type=jnp.float32
    ).astype(jnp.bfloat16)
    sent_rows = sent_rows.reshape(groups, capacity, head_count * block_width)
    sent_slots = jnp.sum(jnp.where(placing, slots_here[None, :] + 1, 0), axis=1) - 1
    sent_slots = sent_slots.reshape(groups, capacity)
    item_rows = lax.all_to_all(sent_rows, "tok", split_axis=0, concat_axis=0, tiled=True)
    item_slots = lax.all_to_all(sent_slots, "tok", split_axis=0, concat_axis=0, tiled=True)
    item_count = item_rows.shape[1]
    flat_out = decode_items(
        item_rows.reshape(groups * item_count, head_count * block_width),
        item_slots.reshape(groups * item_count),
        state_cache[0],
        out_gain,
        head_count,
    )
    served = flat_out.reshape(groups, item_count, head_count * DH)
    returned = lax.all_to_all(served, "tok", split_axis=0, concat_axis=0, tiled=True)
    dec_attended = jnp.dot(
        jnp.transpose(placing).astype(jnp.bfloat16),
        returned.reshape(groups * capacity, head_count * DH),
        preferred_element_type=jnp.float32,
    ).astype(jnp.bfloat16)
    part_rows = dec_attended
    decode_out = lax.psum_scatter(
        jnp.dot(part_rows, out_weight, preferred_element_type=jnp.float32).astype(jnp.bfloat16),
        "head",
        scatter_dimension=0,
        tiled=True,
    )
    return (stretch_out[None], decode_out[None], state_next[None])


def solution(mesh):
    in_specs = (
        P("tok", "head", None),
        P("tok", None, None),
        P("tok", None, None),
        P("tok", None, None, None),
        P(),
        P(),
        P(None, "head", None),
        P("head"),
        P("head", None),
        P("tok", None, "head", None, None),
        P("tok"),
        P("tok"),
        P("tok", None),
        P("tok", None, None),
    )
    out_specs = (P("tok", "head", None), P("tok", "head", None), P("tok", "head", None, None))
    chosen = local_square if mesh.shape["head"] == 4 else local
    return jax.shard_map(chosen, mesh=mesh, in_specs=in_specs, out_specs=out_specs, check_vma=False)
```

```python
import functools
import math

import jax
import jax.numpy as jnp
import numpy as np
from jax import lax
from jax.experimental import pallas as pl
from jax.experimental.pallas import tpu as pltpu
from jax.sharding import PartitionSpec as P

D = 1792
DH = 112
F = 16
STRETCH = 1024
DEC = 32
QUAD = F * F
PHI = 1 + F + QUAD
WIDE = 128
PHI_WIDE = QUAD + 128
MIB = 1 << 20
BF = jnp.bfloat16
F32 = jnp.float32


def lanes_of(size):
    return lax.broadcasted_iota(jnp.int32, (F, size), 1), lax.broadcasted_iota(jnp.int32, (F, size), 0)


def ones_where(mask):
    return jnp.where(mask, 1.0, 0.0).astype(BF)


def spreader():
    lane, entry = lanes_of(PHI_WIDE)
    return ones_where(jnp.where(lane < QUAD, lane >> 4, lane & (F - 1)) == entry)


def dot(left, right, contract=((1,), (0,))):
    return lax.dot_general(left, right, (contract, ((), ())), preferred_element_type=F32)


def phi_of(vectors, pick):
    spread = dot(vectors, pick)
    a, b = spread[:, :QUAD], spread[:, QUAD:]
    quad = a * jnp.concatenate([b] * (QUAD // 128), axis=1) * (1.0 / math.sqrt(2.0 * F))
    lane = lax.broadcasted_iota(jnp.int32, b.shape, 1)
    rest = jnp.where(lane < F, b * (1.0 / math.sqrt(math.sqrt(F))), jnp.where(lane == F, 1.0, 0.0))
    return jnp.concatenate([quad, rest], axis=1)


def unit_rows(values):
    values = values.astype(F32)
    total = jnp.sum(values * values, axis=-1, keepdims=True)
    return values, lax.rsqrt(total * (1.0 / D) + 1e-05)


def column(row):
    size = row.shape[1]
    same = lax.broadcasted_iota(jnp.int32, (size, size), 0) == lax.broadcasted_iota(jnp.int32, (size, size), 1)
    return jnp.sum(jnp.where(same, row, 0), axis=1, keepdims=True)


def projection(w_ref, heads):
    pieces = [w_ref[h, :F, :] for h in range(heads)] + [w_ref[h, F : 2 * F, :] for h in range(heads)]
    for h in range(heads):
        pieces += [w_ref[h, 2 * F :, :], jnp.zeros((WIDE - DH, D), w_ref.dtype)]
    return jnp.concatenate(pieces, axis=0)


def out_projection(w_ref, heads):
    pieces = []
    for h in range(heads):
        pieces += [w_ref[h * DH : (h + 1) * DH, :], jnp.zeros((WIDE - DH, D), w_ref.dtype)]
    return jnp.concatenate(pieces, axis=0)


def conv_kernel(tokens_ref, tail_ref, gain_ref, taps_ref, low, top, begin, end):
    rows = tokens_ref.shape[0]
    half = rows // 2
    gain = gain_ref[...].reshape(1, D)
    taps = taps_ref[...]
    _, factor = unit_rows(tokens_ref[...])
    step = 256
    row = lax.broadcasted_iota(jnp.int32, (rows, step), 0)
    for at in range(0, D, step):
        cols = slice(at, at + step)
        normed = tokens_ref[:, cols].astype(F32) * factor * gain[:, cols]
        normed = normed.astype(BF)
        begin[:, cols] = normed[:16]
        end[:, cols] = normed[rows - 16 :]
        normed = normed.astype(F32)
        tail = tail_ref[:, cols].astype(F32)
        one = jnp.where(row == 0, tail[1:2], pltpu.roll(normed, 1, 0))
        two = pltpu.roll(normed, 2, 0)
        two = jnp.where(row == 0, tail[0:1], jnp.where(row == 1, tail[1:2], two))
        total = taps[0:1, cols] * two + taps[1:2, cols] * one + taps[2:3, cols] * normed
        total = total.astype(BF)
        top[:, cols] = total[:half]
        low[:, cols] = total[half:]


def rim_kernel(first_ref, top_ref, begin_ref, end_ref, taps_ref, out_ref, begin, end, taps, rows, sem):
    copies = [
        pltpu.make_async_copy(src, place, sem.at[n])
        for n, (src, place) in enumerate([(begin_ref, begin), (end_ref, end), (taps_ref, taps)])
    ]
    for copy in copies:
        copy.start()
    for copy in copies:
        copy.wait()
    now = begin[...].astype(F32)
    last = end[...].astype(F32)
    row = lax.broadcasted_iota(jnp.int32, now.shape, 0)
    one = jnp.where(row == 0, last[15:16], pltpu.roll(now, 1, 0))
    two = jnp.where(row == 0, last[14:15], jnp.where(row == 1, last[15:16], pltpu.roll(now, 2, 0)))
    rows[...] = (taps[0:1, :] * two + taps[1:2, :] * one + taps[2:3, :] * now).astype(BF)

    @pl.when(first_ref[0] != 0)
    def _():
        back = pltpu.make_async_copy(rows, out_ref.at[:16], sem.at[3])
        back.start()
        back.wait()


def block_part(slot, heads, length, conved, w_ref, sums, own, queries):
    rows = conved.shape[0]
    qkv = dot(conved, projection(w_ref, heads), ((1,), (1,))).astype(BF)
    queries[...] = qkv[:, : heads * F]
    live = length - rows * (lax.axis_index("head") ^ slot)
    row = lax.broadcasted_iota(jnp.int32, (rows, rows), 0)
    col = lax.broadcasted_iota(jnp.int32, (rows, rows), 1)
    allowed = (col <= row) & (col < live)
    live_row = lax.broadcasted_iota(jnp.int32, (rows, WIDE), 0) < live
    pick = spreader()
    for head in range(heads):
        q = qkv[:, head * F : head * F + F]
        k = qkv[:, (heads + head) * F : (heads + head) * F + F]
        at = 2 * heads * F + head * WIDE
        v = qkv[:, at : at + WIDE]
        key_phi = phi_of(k, pick).astype(BF)
        v_live = jnp.where(live_row, v.astype(F32), 0.0).astype(BF)
        sums[head] = dot(key_phi, v_live, ((0,), (0,)))
        inner = dot(q, k, ((1,), (1,))) * (1.0 / math.sqrt(F))
        weights = jnp.where(allowed, 1.0 + inner + 0.5 * inner * inner, 0.0).astype(BF)
        own[head] = dot(weights, v)


def finish_part(slot, heads, length, states, own, queries, gain_ref, w_ref, top, low):
    rows = queries.shape[0]
    half = rows // 2
    live = length - rows * (lax.axis_index("head") ^ slot)
    live_row = lax.broadcasted_iota(jnp.int32, (rows, WIDE), 0) < live
    pick = spreader()
    gains = gain_ref[...].reshape(1, heads * DH)
    zeros = jnp.zeros((1, WIDE - DH), F32)
    parts = []
    for head in range(heads):
        query_phi = phi_of(queries[:, head * F : head * F + F], pick).astype(BF)
        total = own[head] + dot(query_phi, states[head])
        square = jnp.sum(total * total, axis=-1, keepdims=True)
        gain = jnp.concatenate([gains[:, head * DH : (head + 1) * DH], zeros], axis=1)
        total = total * lax.rsqrt(square * (1.0 / DH) + 1e-05) * gain
        parts.append(jnp.where(live_row, total, 0.0).astype(BF))
    attended = jnp.concatenate(parts, axis=1)
    w_out = out_projection(w_ref, heads)
    top[...] = dot(attended[:half], w_out).astype(BF)
    top.push()
    low[...] = dot(attended[half:], w_out).astype(BF)
    low.push()


def first_kernel(heads, len_ref, low, top, w_ref, sums, own, queries):
    conved = jnp.concatenate([top[...], low[...]], axis=0)
    block_part(0, heads, len_ref[0], conved, w_ref, sums, own, queries)


def second_kernel(heads, len_ref, low1, top1, w_ref, low2, top2, sums1, own1, queries1, sums2, own2, queries2):
    conved = jnp.concatenate([top1[...], low1[...]], axis=0)
    block_part(1, heads, len_ref[0], conved, w_ref, sums1, own1, queries1)
    for out in (sums1, own1, queries1):
        out.push()
    conved = jnp.concatenate([top2[...], low2[...]], axis=0)
    block_part(2, heads, len_ref[0], conved, w_ref, sums2, own2, queries2)


def third_kernel(heads, capacity, len_ref, low, top, w_ref, cache_ref, sums0, sums1, sums2, gain_ref, out_w_ref, items_ref, owner_ref,
                 top3, low3, part, states, state_next, sums3, own3, queries3, states3):
    length = len_ref[0]
    mine = lax.axis_index("head")
    conved = jnp.concatenate([top[...], low[...]], axis=0)
    block_part(3, heads, length, conved, w_ref, sums3, own3, queries3)
    sums = [sums0, sums1, sums2, sums3]
    olds = []
    pad = jnp.zeros((PHI_WIDE - PHI, DH), F32)
    for head in range(heads):
        old = [cache_ref[F + 1 :, head, :], cache_ref[1 : F + 1, head, :], cache_ref[0:1, head, :], pad]
        old = jnp.concatenate([jnp.concatenate(old, axis=0), jnp.zeros((PHI_WIDE, WIDE - DH), F32)], axis=1)
        olds.append(old)

    def prefix(slot, head):
        before = olds[head]
        for other in range(4):
            if other != slot:
                before = before + ((mine ^ other) < (mine ^ slot)).astype(F32) * sums[other][head]
        return before.astype(BF)

    for head in range(heads):
        states3[head] = prefix(3, head)
    finish_part(3, heads, length, states3, own3, queries3, gain_ref, out_w_ref, top3, low3)
    for slot in range(3):
        for head in range(heads):
            states[slot, head] = prefix(slot, head)
    states.push()
    return_part(heads, capacity, items_ref, owner_ref, out_w_ref, part)
    part.push()
    for head in range(heads):
        total = olds[head] + (sums0[head] + sums1[head]) + (sums2[head] + sums3[head])
        total = total[:, :DH]
        state_next[0, F + 1 :, head, :] = total[:QUAD]
        state_next[0, 1 : F + 1, head, :] = total[QUAD : QUAD + F]
        state_next[0, 0:1, head, :] = total[QUAD + F : QUAD + F + 1]


def fourth_kernel(heads, len_ref, states, queries1, own1, gain_ref, out_w_ref, queries2, own2, top1, low1, top2, low2):
    finish_part(1, heads, len_ref[0], states.part(1), own1, queries1, gain_ref, out_w_ref, top1, low1)
    finish_part(2, heads, len_ref[0], states.part(2), own2, queries2, gain_ref, out_w_ref, top2, low2)


def fifth_kernel(heads, len_ref, states, queries0, own0, gain_ref, out_w_ref, top0, low0):
    finish_part(0, heads, len_ref[0], states.part(0), own0, queries0, gain_ref, out_w_ref, top0, low0)


def add_kernel(a_ref, b_ref, c_ref, d_ref, ab_ref, cd_ref):
    ab_ref[...] = (a_ref[...].astype(F32) + b_ref[...].astype(F32)).astype(BF)
    cd_ref[...] = (c_ref[...].astype(F32) + d_ref[...].astype(F32)).astype(BF)


def total_kernel(*refs):
    parts, out_ref = refs[:-1], refs[-1]
    half = out_ref.shape[1] // 2
    for order in range(2):
        mine = [part[...].astype(F32) for part in parts[order::2]]
        out_ref[0, order * half : (order + 1) * half, :] = functools.reduce(lambda a, b: a + b, mine).astype(BF)


def placing_rank(owners_row, axis):
    down = lax.broadcasted_iota(jnp.int32, (DEC, DEC), 0)
    along = lax.broadcasted_iota(jnp.int32, (DEC, DEC), 1)
    earlier = down < along if axis == 0 else along < down
    return jnp.sum(jnp.where(earlier & (column(owners_row) == owners_row), 1, 0), axis=axis, keepdims=True)


def send_kernel(heads, capacity, tokens_ref, tail_ref, gain_ref, taps_ref, owner_ref, slot_ref, w_ref, out):
    tokens, factor = unit_rows(tokens_ref[...])
    normed = (tokens * factor * gain_ref[...].reshape(1, D)).astype(BF).astype(F32)
    tail = tail_ref[...].astype(F32)
    taps = taps_ref[...]
    conved = taps[0:1, :] * tail[:, 0, :] + taps[1:2, :] * tail[:, 1, :]
    conved = (conved + taps[2:3, :] * normed).astype(BF)
    owners = owner_ref[...]
    target = owners * capacity + placing_rank(owners, 0)
    placing = lax.broadcasted_iota(jnp.int32, (out.shape[0], DEC), 0) == target
    cache_slot = jnp.sum(jnp.where(placing, slot_ref[...] + 1, 0), axis=1, keepdims=True) - 1
    qkv = dot(conved, projection(w_ref, heads), ((1,), (1,))).astype(BF)
    sent = dot(ones_where(placing), qkv)
    lane = lax.broadcasted_iota(jnp.int32, sent.shape, 1)
    mark = 2 * heads * F + DH
    out[...] = jnp.where(lane == mark, cache_slot.astype(F32), sent).astype(BF)


def cache_spreaders(heads):
    lane, entry = lanes_of(PHI * heads)
    feature = lane >> (heads.bit_length() - 1)
    quad = feature - (1 + F)
    a = jnp.where(quad < 0, feature - 1, quad >> 4)
    return ones_where(a == entry), ones_where((quad >= 0) & ((quad & (F - 1)) == entry))


def serve_kernel(heads, items_ref, gain_ref, cache_ref, wait_ref, out_ref, state, sem):
    count = items_ref.shape[0]
    mark = 2 * heads * F + DH
    flying = 4
    copies = [pltpu.make_async_copy(cache_ref.at[0, n], state.at[n], sem.at[n]) for n in range(state.shape[0])]
    for copy in copies[:flying]:
        copy.start()
    first, second = cache_spreaders(heads)
    phis = []
    for head in range(heads):
        q = items_ref[:, head * F : head * F + F]
        a = dot(q, first)
        b = dot(q, second)
        lane = lax.broadcasted_iota(jnp.int32, a.shape, 1)
        scale = jnp.where(lane < heads * (F + 1), 1.0 / math.sqrt(math.sqrt(F)), b * (1.0 / math.sqrt(2.0 * F)))
        value = jnp.where(lane < heads, 1.0, a * scale)
        phis.append(jnp.where((lane & (heads - 1)) == head, value, 0.0).astype(BF))
    phis = jnp.concatenate(phis, axis=0)
    slots = jnp.concatenate([items_ref[:, mark : mark + 1].astype(F32)] * heads, axis=0)
    total = jnp.zeros((heads * count, DH), F32)
    for n, copy in enumerate(copies):
        copy.wait()
        for later in copies[n + flying : n + flying + 1]:
            later.start()
        table = dot(phis, state[n].reshape(PHI * heads, DH).astype(BF))
        total = total + jnp.where(slots == float(n), table, 0.0)
    gains = gain_ref[...].reshape(1, heads * DH)
    for head in range(heads):
        q = items_ref[:, head * F : head * F + F].astype(F32)
        k = items_ref[:, (heads + head) * F : (heads + head) * F + F].astype(F32)
        at = 2 * heads * F + head * WIDE
        v = items_ref[:, at : at + DH].astype(F32)
        inner = jnp.sum(q * k, axis=-1, keepdims=True) * (1.0 / math.sqrt(F))
        value = total[head * count : (head + 1) * count, :] + (1.0 + inner + 0.5 * inner * inner) * v
        square = jnp.sum(value * value, axis=-1, keepdims=True)
        value = value * lax.rsqrt(square * (1.0 / DH) + 1e-05) * gains[:, head * DH : (head + 1) * DH]
        out_ref[:, head * WIDE : head * WIDE + DH] = value.astype(BF)
        out_ref[:, head * WIDE + DH : (head + 1) * WIDE] = jnp.zeros((count, WIDE - DH), BF)


def return_part(heads, capacity, items_ref, owner_ref, w_ref, out):
    owners = owner_ref[...]
    target = column(owners) * capacity + placing_rank(owners, 1)
    placing = lax.broadcasted_iota(jnp.int32, (DEC, items_ref.shape[0]), 1) == target
    attended = dot(ones_where(placing), items_ref[...]).astype(BF)
    out[...] = dot(attended, out_projection(w_ref, heads)).astype(BF)


class Fetched:
    def __init__(self, copy, place):
        self.copy, self.place, self.here = copy, place, False
        self.shape, self.dtype = place.shape, place.dtype

    def __getitem__(self, index):
        if not self.here:
            self.copy.wait()
            self.here = True
        return self.place[index]

    def part(self, number):
        self[0, 0]
        return self.place.at[number]


class Pushed:
    def __init__(self, copy, place):
        self.copy, self.place, self.gone = copy, place, False
        self.shape, self.dtype = place.shape, place.dtype

    def __getitem__(self, index):
        return self.place[index]

    def __setitem__(self, index, value):
        self.place[index] = value

    def push(self):
        if not self.gone:
            self.copy.start()
            self.gone = True


def hbm_call(kernel, outs, flops, size, scalars=(), picked=None, inner=(), waits=()):
    def run(*args):
        count, many = len(args), len(outs)

        def shape_in(n):
            return args[n].shape[2:] if n == picked else args[n].shape

        def body(*refs):
            numbers, sources = refs[: len(scalars)], refs[len(scalars) : len(scalars) + count]
            rest = refs[len(scalars) + count + len(waits) :]
            targets, places, results, own, sem = (
                rest[:many],
                rest[many : many + count],
                rest[many + count : 2 * many + count],
                rest[2 * many + count : -1],
                rest[-1],
            )
            ins = []
            for n, (source, place) in enumerate(zip(sources, places)):
                if n == picked:
                    source = source.at[0, numbers[-1][0]]
                copy = pltpu.make_async_copy(source, place, sem.at[n])
                copy.start()
                ins.append(Fetched(copy, place))
            done = [
                Pushed(pltpu.make_async_copy(result, target, sem.at[count + n]), result)
                for n, (result, target) in enumerate(zip(results, targets))
            ]
            kernel(*numbers[: len(scalars) - (picked is not None)], *ins, *done, *own)
            for out in done:
                out.push()
            for one in ins:
                if not one.here:
                    one.copy.wait()
            for out in done:
                out.copy.wait()

        hbm = pl.BlockSpec(memory_space=pltpu.HBM)
        return pl.pallas_call(
            body,
            out_shape=[pltpu.HBM(o.shape, o.dtype) for o in outs],
            in_specs=[pl.BlockSpec(memory_space=pltpu.SMEM)] * len(scalars)
            + [hbm] * count
            + [pl.BlockSpec(memory_space=pl.ANY)] * len(waits),
            out_specs=[hbm] * many,
            scratch_shapes=[pltpu.VMEM(shape_in(n), args[n].dtype) for n in range(count)]
            + [pltpu.VMEM(o.shape, o.dtype) for o in outs]
            + [pltpu.VMEM(o.shape, o.dtype) for o in inner]
            + [pltpu.SemaphoreType.DMA((count + many,))],
            compiler_params=pltpu.CompilerParams(vmem_limit_bytes=32 * MIB),
            cost_estimate=pl.CostEstimate(flops=flops, bytes_accessed=size, transcendentals=0),
        )(*scalars, *[pltpu.with_memory_space_constraint(a, pltpu.HBM) for a in args], *waits)

    return run


def call(kernel, outs, flops, size):
    def run(*args):
        many = isinstance(outs, (list, tuple))
        spec = pl.BlockSpec(memory_space=pltpu.VMEM)
        return pl.pallas_call(
            kernel,
            out_shape=outs,
            in_specs=[spec] * len(args),
            out_specs=[spec] * len(outs) if many else spec,
            compiler_params=pltpu.CompilerParams(vmem_limit_bytes=16 * MIB),
            cost_estimate=pl.CostEstimate(flops=flops, bytes_accessed=size, transcendentals=0),
        )(*args)

    return run


def shape(*dims, dtype=BF):
    return jax.ShapeDtypeStruct(dims, dtype)


def across(array, by):
    return lax.ppermute(array, "head", [(i, i ^ by) for i in range(4)])


def local_square(
    stretch_tokens,
    stretch_tail,
    decode_tokens,
    decode_tail,
    norm_gain,
    conv_taps,
    qkv_weight,
    out_gain,
    out_weight,
    state_cache,
    stretch_len,
    stretch_slot,
    decode_slot,
    decode_owner,
):
    heads = qkv_weight.shape[1]
    rows = stretch_tokens.shape[1]
    half = rows // 2
    wide = heads * (2 * F + WIDE)
    me = lax.axis_index("head").reshape(1)
    w_in = jnp.transpose(qkv_weight, (1, 2, 0))
    cache = jnp.transpose(state_cache, (0, 1, 4, 2, 3))
    hbm = pl.BlockSpec(memory_space=pltpu.HBM)
    in_vmem = pl.BlockSpec(memory_space=pltpu.VMEM)
    anywhere = pl.BlockSpec(memory_space=pl.ANY)
    piece, ends = shape(half, D), shape(16, D)

    low, top, begin, end = hbm_call(conv_kernel, [piece, piece, ends, ends], 20 * rows * D, 4 * rows * D)(
        stretch_tokens[0], stretch_tail[0], norm_gain, conv_taps
    )
    low_x = across(low, 1)
    low_y = across(low, 2)
    end = from_behind(end, "head", 1)

    groups = lax.axis_size("tok")
    capacity = max(2, 2 * DEC // groups)
    count = groups * capacity
    owner_row = decode_owner.reshape(1, DEC)
    (sent,) = hbm_call(functools.partial(send_kernel, heads, capacity), [shape(count, wide)], 2 * DEC * D * wide, 2 * D * wide)(
        decode_tokens[0], decode_tail[0], norm_gain, conv_taps, owner_row, decode_slot, w_in
    )
    top = pl.pallas_call(
        lambda first_ref, top_ref, begin_ref, end_ref, taps_ref, wait_ref, *refs: rim_kernel(
            first_ref, top_ref, begin_ref, end_ref, taps_ref, *refs
        ),
        out_shape=pltpu.HBM((half, D), BF),
        in_specs=[pl.BlockSpec(memory_space=pltpu.SMEM)] + [hbm] * 4 + [anywhere],
        out_specs=hbm,
        scratch_shapes=[pltpu.VMEM((16, D), BF), pltpu.VMEM((16, D), BF), pltpu.VMEM((3, D), F32), pltpu.VMEM((16, D), BF)]
        + [pltpu.SemaphoreType.DMA((4,))],
        input_output_aliases={1: 0},
        compiler_params=pltpu.CompilerParams(vmem_limit_bytes=16 * MIB),
        cost_estimate=pl.CostEstimate(flops=16 * D, bytes_accessed=128 * D, transcendentals=0),
    )(me, *[pltpu.with_memory_space_constraint(a, pltpu.HBM) for a in (top, begin, end, conv_taps)], sent)
    top_x = across(top, 1)
    top_y = across(top, 2)
    items = lax.all_to_all(sent.reshape(groups, capacity, wide), "tok", split_axis=0, concat_axis=0, tiled=True)

    length = stretch_len.astype(jnp.int32)
    slot = stretch_slot.astype(jnp.int32)
    sums, own = shape(heads, PHI_WIDE, WIDE, dtype=F32), shape(heads, rows, WIDE, dtype=F32)
    queries, states = shape(rows, heads * F), shape(heads, PHI_WIDE, WIDE)
    block_flops = 2 * rows * D * wide + 6 * heads * rows * rows * WIDE
    finish_flops = 2 * rows * heads * WIDE * (D + PHI_WIDE)
    sums0, own0, queries0 = hbm_call(
        functools.partial(first_kernel, heads), [sums, own, queries], block_flops, 4 * rows * D, scalars=[length], waits=[sent]
    )(low, top, w_in)
    served = pl.pallas_call(
        functools.partial(serve_kernel, heads),
        in_specs=[in_vmem, in_vmem, hbm, anywhere],
        out_specs=in_vmem,
        out_shape=shape(count, heads * WIDE),
        scratch_shapes=[pltpu.VMEM(cache.shape[1:], F32), pltpu.SemaphoreType.DMA((cache.shape[1],))],
        compiler_params=pltpu.CompilerParams(vmem_limit_bytes=32 * MIB),
        cost_estimate=pl.CostEstimate(
            flops=2 * cache.shape[1] * heads * heads * DH * PHI * count,
            bytes_accessed=4 * cache.shape[1] * heads * WIDE * PHI,
            transcendentals=0,
        ),
    )(items.reshape(count, wide), out_gain, pltpu.with_memory_space_constraint(cache, pltpu.HBM), queries0)
    returned = lax.all_to_all(
        served.reshape(groups, capacity, heads * WIDE), "tok", split_axis=0, concat_axis=0, tiled=True
    ).reshape(count, heads * WIDE)
    low_y, top_x = lax.optimization_barrier((low_y, top_x, served))[:2]
    low_xy = across(low_y, 1)
    top_xy = across(top_x, 2)
    sums1, own1, queries1, sums2, own2, queries2 = hbm_call(
        functools.partial(second_kernel, heads), [sums, own, queries] * 2, 2 * block_flops, 4 * rows * D, scalars=[length], waits=[served]
    )(low_x, top_x, w_in, low_y, top_y)

    returned, low_xy = lax.optimization_barrier((returned, low_xy, queries2))[:2]
    top3, low3, part, all_states, state_next = hbm_call(
        functools.partial(third_kernel, heads, capacity),
        [piece, piece, shape(DEC, D), shape(3, *states.shape), shape(1, PHI, heads, DH, dtype=F32)],
        block_flops + finish_flops,
        8 * rows * D,
        scalars=[length, slot],
        picked=3,
        inner=[sums, own, queries, states],
    )(low_xy, top_xy, w_in, cache, sums0, sums1, sums2, out_gain, out_weight, returned, owner_row)
    via_x = across(top3, 1)
    via_y = across(low3, 2)
    top1, low1, top2, low2 = hbm_call(
        functools.partial(fourth_kernel, heads), [piece] * 4, 2 * finish_flops, 4 * rows * D, scalars=[length]
    )(all_states, queries1, own1, out_gain, out_weight, queries2, own2)
    one_x = across(top1, 1)
    one_y = across(low2, 2)
    part = lax.optimization_barrier((part, top1))[0]
    shares = lax.all_to_all(part.reshape(4, DEC // 4, D), "head", split_axis=0, concat_axis=0, tiled=True)
    two_y, two_x = call(add_kernel, [piece, piece], 0, 6 * rows * D)(top2, via_x, low1, via_y)
    two_y = across(two_y, 2)
    two_x = across(two_x, 1)
    top0, low0 = hbm_call(
        functools.partial(fifth_kernel, heads), [piece] * 2, finish_flops, 4 * rows * D, scalars=[length], waits=[two_x, two_y][:0]
    )(all_states, queries0, own0, out_gain, out_weight)
    state_next = jnp.transpose(state_next, (0, 2, 3, 1))
    decode_out = jnp.sum(shares.astype(F32), axis=0).astype(BF)
    stretch_out = call(total_kernel, shape(1, rows, D), 0, 8 * rows * D)(top0, low0, one_x, one_y, two_y, two_x)
    return (stretch_out, decode_out[None], state_next)


def from_behind(array, axis, by):
    peers = lax.axis_size(axis)
    pairs = [(i, i + by) for i in range(peers) if 0 <= i + by < peers]
    return lax.ppermute(array, axis, pairs)


def rms_rows(values, gain):
    values = values.astype(jnp.float32)
    factor = lax.rsqrt(jnp.mean(values * values, axis=-1, keepdims=True) + 1e-05)
    return values * factor * gain


def features(vectors):
    breadth = vectors.shape[-1]
    linear = vectors / math.sqrt(math.sqrt(breadth))
    outer = vectors[..., :, None] * vectors[..., None, :] / math.sqrt(2.0 * breadth)
    outer = outer.reshape(vectors.shape[:-1] + (breadth * breadth,))
    ones = jnp.ones(vectors.shape[:-1] + (1,), vectors.dtype)
    return jnp.concatenate([ones, linear, outer], axis=-1)


def convolve(tail, normed, conv_taps):
    joined = jnp.concatenate([tail, normed], axis=-2).astype(jnp.float32)
    span_rows = normed.shape[-2]
    total = conv_taps[0] * joined[..., 0:span_rows, :]
    total = total + conv_taps[1] * joined[..., 1 : span_rows + 1, :]
    total = total + conv_taps[2] * joined[..., 2 : span_rows + 2, :]
    return total.astype(jnp.bfloat16)


def decode_items(items, slot_items, cache_own, out_gain, head_count):
    item_count = items.shape[0]
    shaped = items.reshape(item_count, head_count, 2 * F + DH).astype(jnp.float32)
    queries = shaped[:, :, :F]
    key_feats = shaped[:, :, F : 2 * F]
    values = shaped[:, :, 2 * F :]
    slot_total = cache_own.shape[0]
    table = jnp.einsum(
        "nhp,shdp->nshd", features(queries), cache_own, precision=lax.Precision.HIGHEST
    )
    picker = (slot_items[:, None] == jnp.arange(slot_total)[None, :]).astype(jnp.float32)
    carried = jnp.einsum("ns,nshd->nhd", picker, table, precision=lax.Precision.HIGHEST)
    inner = jnp.sum(queries * key_feats, axis=-1) / math.sqrt(F)
    own_term = (1.0 + inner + 0.5 * inner * inner)[..., None] * values
    attended = rms_rows(carried + own_term, out_gain.reshape(head_count, DH))
    return attended.astype(jnp.bfloat16).reshape(item_count, head_count * DH)


def local(
    stretch_tokens,
    stretch_tail,
    decode_tokens,
    decode_tail,
    norm_gain,
    conv_taps,
    qkv_weight,
    out_gain,
    out_weight,
    state_cache,
    stretch_len,
    stretch_slot,
    decode_slot,
    decode_owner,
):
    head_count = qkv_weight.shape[1]
    block_width = qkv_weight.shape[2]
    rows_own = stretch_tokens.shape[1]
    w_flat = qkv_weight.reshape(D, head_count * block_width)
    gains = out_gain.reshape(head_count, DH)
    normed = rms_rows(stretch_tokens[0], norm_gain).astype(jnp.bfloat16)
    rim_rows = from_behind(normed[rows_own - 2 :], "head", 1)
    first_dev = lax.axis_index("head") == 0
    rim_rows = jnp.where(first_dev, stretch_tail[0], rim_rows)
    conved = convolve(rim_rows, normed, conv_taps)
    grouped = jnp.dot(
        lax.all_gather(conved, "head", axis=0, tiled=True),
        w_flat,
        preferred_element_type=jnp.float32,
    ).astype(jnp.bfloat16)
    grouped = grouped.reshape(STRETCH, head_count, block_width)
    queries = grouped[:, :, :F]
    key_feats = grouped[:, :, F : 2 * F]
    values = grouped[:, :, 2 * F :]
    length = stretch_len[0]
    positions = jnp.arange(STRETCH)
    valid_rows = positions < length
    state_old = lax.dynamic_index_in_dim(state_cache[0], stretch_slot[0], 0, keepdims=False)
    carried = jnp.einsum(
        "ihp,hdp->ihd",
        features(queries.astype(jnp.float32)),
        state_old,
        precision=lax.Precision.HIGHEST,
    )
    block_rows = min(512, STRETCH)
    pieces = []
    for anchor in range(0, STRETCH, block_rows):
        finish = anchor + block_rows
        inner = jnp.einsum(
            "ihf,jhf->hij",
            queries[anchor:finish],
            key_feats[:finish],
            preferred_element_type=jnp.float32,
        ) / math.sqrt(F)
        weights = 1.0 + inner + 0.5 * inner * inner
        allowed = (positions[None, :finish] <= positions[anchor:finish, None]) & valid_rows[
            None, :finish
        ]
        weights = jnp.where(allowed[None], weights, 0.0).astype(jnp.bfloat16)
        pieces.append(
            jnp.einsum("hij,jhd->ihd", weights, values[:finish], preferred_element_type=jnp.float32)
        )
    local_sum = jnp.concatenate(pieces, axis=0)
    attended = rms_rows(carried + local_sum, gains)
    attended = (
        jnp.where(valid_rows[:, None, None], attended, 0.0)
        .astype(jnp.bfloat16)
        .reshape(STRETCH, head_count * DH)
    )
    key_phi = jnp.where(
        valid_rows[:, None, None], features(key_feats.astype(jnp.float32)), 0.0
    ).astype(jnp.bfloat16)
    state_next = state_old + jnp.einsum(
        "jhd,jhp->hdp", values, key_phi, preferred_element_type=jnp.float32
    )
    part_rows = attended
    stretch_out = lax.psum_scatter(
        jnp.dot(part_rows, out_weight, preferred_element_type=jnp.float32).astype(jnp.bfloat16),
        "head",
        scatter_dimension=0,
        tiled=True,
    )
    dec_normed = rms_rows(decode_tokens[0], norm_gain).astype(jnp.bfloat16)
    dec_conved = convolve(decode_tail[0], dec_normed[:, None, :], conv_taps)[:, 0, :]
    dec_qkv = jnp.dot(dec_conved, w_flat, preferred_element_type=jnp.float32).astype(jnp.bfloat16)
    owners = decode_owner[0, :, 0]
    slots_here = decode_slot[0]
    groups = lax.axis_size("tok")
    capacity = max(2, 2 * DEC // groups)
    earlier = jnp.arange(DEC)[None, :] < jnp.arange(DEC)[:, None]
    same_owner = owners[None, :] == owners[:, None]
    rank_in = jnp.sum(earlier & same_owner, axis=1)
    target = owners * capacity + rank_in
    placing = jnp.arange(groups * capacity)[:, None] == target[None, :]
    sent_rows = jnp.dot(
        placing.astype(jnp.bfloat16), dec_qkv, preferred_element_type=jnp.float32
    ).astype(jnp.bfloat16)
    sent_rows = sent_rows.reshape(groups, capacity, head_count * block_width)
    sent_slots = jnp.sum(jnp.where(placing, slots_here[None, :] + 1, 0), axis=1) - 1
    sent_slots = sent_slots.reshape(groups, capacity)
    item_rows = lax.all_to_all(sent_rows, "tok", split_axis=0, concat_axis=0, tiled=True)
    item_slots = lax.all_to_all(sent_slots, "tok", split_axis=0, concat_axis=0, tiled=True)
    item_count = item_rows.shape[1]
    flat_out = decode_items(
        item_rows.reshape(groups * item_count, head_count * block_width),
        item_slots.reshape(groups * item_count),
        state_cache[0],
        out_gain,
        head_count,
    )
    served = flat_out.reshape(groups, item_count, head_count * DH)
    returned = lax.all_to_all(served, "tok", split_axis=0, concat_axis=0, tiled=True)
    dec_attended = jnp.dot(
        jnp.transpose(placing).astype(jnp.bfloat16),
        returned.reshape(groups * capacity, head_count * DH),
        preferred_element_type=jnp.float32,
    ).astype(jnp.bfloat16)
    part_rows = dec_attended
    decode_out = lax.psum_scatter(
        jnp.dot(part_rows, out_weight, preferred_element_type=jnp.float32).astype(jnp.bfloat16),
        "head",
        scatter_dimension=0,
        tiled=True,
    )
    return (stretch_out[None], decode_out[None], state_next[None])


def solution(mesh):
    in_specs = (
        P("tok", "head", None),
        P("tok", None, None),
        P("tok", None, None),
        P("tok", None, None, None),
        P(),
        P(),
        P(None, "head", None),
        P("head"),
        P("head", None),
        P("tok", None, "head", None, None),
        P("tok"),
        P("tok"),
        P("tok", None),
        P("tok", None, None),
    )
    out_specs = (P("tok", "head", None), P("tok", "head", None), P("tok", "head", None, None))
    chosen = local_square if mesh.shape["head"] == 4 else local
    return jax.shard_map(chosen, mesh=mesh, in_specs=in_specs, out_specs=out_specs, check_vma=False)
```

```python
import functools
import math

import jax
import jax.numpy as jnp
import numpy as np
from jax import lax
from jax.experimental import pallas as pl
from jax.experimental.pallas import tpu as pltpu
from jax.sharding import PartitionSpec as P

D = 1792
DH = 112
F = 16
STRETCH = 1024
DEC = 32
QUAD = F * F
PHI = 1 + F + QUAD
WIDE = 128
PHI_WIDE = QUAD + 128
TILE = 16
MIB = 1 << 20
BF = jnp.bfloat16
F32 = jnp.float32


def lanes_of(size):
    return lax.broadcasted_iota(jnp.int32, (F, size), 1), lax.broadcasted_iota(jnp.int32, (F, size), 0)


def ones_where(mask):
    return jnp.where(mask, 1.0, 0.0).astype(BF)


def spreader():
    lane, entry = lanes_of(PHI_WIDE)
    return ones_where(jnp.where(lane < QUAD, lane >> 4, lane & (F - 1)) == entry)


def dot(left, right, contract=((1,), (0,))):
    return lax.dot_general(left, right, (contract, ((), ())), preferred_element_type=F32)


def phi_of(vectors, pick):
    spread = dot(vectors, pick)
    a, b = spread[:, :QUAD], spread[:, QUAD:]
    quad = a * jnp.concatenate([b] * (QUAD // 128), axis=1) * (1.0 / math.sqrt(2.0 * F))
    lane = lax.broadcasted_iota(jnp.int32, b.shape, 1)
    rest = jnp.where(lane < F, b * (1.0 / math.sqrt(math.sqrt(F))), jnp.where(lane == F, 1.0, 0.0))
    return jnp.concatenate([quad, rest], axis=1)


def unit_rows(values):
    values = values.astype(F32)
    total = jnp.sum(values * values, axis=-1, keepdims=True)
    return values, lax.rsqrt(total * (1.0 / D) + 1e-05)


def column(row):
    size = row.shape[1]
    same = lax.broadcasted_iota(jnp.int32, (size, size), 0) == lax.broadcasted_iota(jnp.int32, (size, size), 1)
    return jnp.sum(jnp.where(same, row, 0), axis=1, keepdims=True)


def projection(w_ref, heads):
    pieces = [w_ref[h, :F, :] for h in range(heads)] + [w_ref[h, F : 2 * F, :] for h in range(heads)]
    for h in range(heads):
        pieces += [w_ref[h, 2 * F :, :], jnp.zeros((WIDE - DH, D), w_ref.dtype)]
    return jnp.concatenate(pieces, axis=0)


def out_projection(w_ref, heads):
    pieces = []
    for h in range(heads):
        pieces += [w_ref[h * DH : (h + 1) * DH, :], jnp.zeros((WIDE - DH, D), w_ref.dtype)]
    return jnp.concatenate(pieces, axis=0)


def conv_kernel(tokens_ref, tail_ref, gain_ref, taps_ref, low, top, begin, end):
    rows = tokens_ref.shape[0]
    half = rows // 2
    gain = gain_ref[...].reshape(1, D)
    taps = taps_ref[...]
    _, factor = unit_rows(tokens_ref[...])
    step = 256
    row = lax.broadcasted_iota(jnp.int32, (rows, step), 0)
    for at in range(0, D, step):
        cols = slice(at, at + step)
        normed = tokens_ref[:, cols].astype(F32) * factor * gain[:, cols]
        normed = normed.astype(BF)
        begin[:, cols] = normed[:16]
        end[:, cols] = normed[rows - 16 :]
        normed = normed.astype(F32)
        tail = tail_ref[:, cols].astype(F32)
        one = jnp.where(row == 0, tail[1:2], pltpu.roll(normed, 1, 0))
        two = pltpu.roll(normed, 2, 0)
        two = jnp.where(row == 0, tail[0:1], jnp.where(row == 1, tail[1:2], two))
        total = taps[0:1, cols] * two + taps[1:2, cols] * one + taps[2:3, cols] * normed
        total = total.astype(BF)
        top[:, cols] = total[:half]
        low[:, cols] = total[half:]


def rim_kernel(first_ref, top_ref, begin_ref, end_ref, taps_ref, out_ref, begin, end, taps, rows, sem):
    copies = [
        pltpu.make_async_copy(src, place, sem.at[n])
        for n, (src, place) in enumerate([(begin_ref, begin), (end_ref, end), (taps_ref, taps)])
    ]
    for copy in copies:
        copy.start()
    for copy in copies:
        copy.wait()
    now = begin[...].astype(F32)
    last = end[...].astype(F32)
    row = lax.broadcasted_iota(jnp.int32, now.shape, 0)
    one = jnp.where(row == 0, last[15:16], pltpu.roll(now, 1, 0))
    two = jnp.where(row == 0, last[14:15], jnp.where(row == 1, last[15:16], pltpu.roll(now, 2, 0)))
    rows[...] = (taps[0:1, :] * two + taps[1:2, :] * one + taps[2:3, :] * now).astype(BF)

    @pl.when(first_ref[0] != 0)
    def _():
        back = pltpu.make_async_copy(rows, out_ref.at[:16], sem.at[3])
        back.start()
        back.wait()


def block_part(slot, heads, length, conved, w_ref, sums, own):
    rows = conved.shape[0]
    qkv = dot(conved, projection(w_ref, heads), ((1,), (1,))).astype(BF)
    live = length - rows * (lax.axis_index("head") ^ slot)
    row = lax.broadcasted_iota(jnp.int32, (rows, rows), 0)
    col = lax.broadcasted_iota(jnp.int32, (rows, rows), 1)
    allowed = (col <= row) & (col < live)
    live_row = lax.broadcasted_iota(jnp.int32, (rows, WIDE), 0) < live
    pick = spreader()
    keys = [qkv[:, (heads + head) * F : (heads + head) * F + F] for head in range(heads)]
    values = [qkv[:, 2 * heads * F + head * WIDE : 2 * heads * F + (head + 1) * WIDE] for head in range(heads)]
    for head in range(heads):
        live_values = jnp.where(live_row, values[head].astype(F32), 0.0).astype(BF)
        sums[head] = dot(phi_of(keys[head], pick).astype(BF), live_values, ((0,), (0,)))
        sums.push(head)
    for head in range(heads):
        inner = dot(qkv[:, head * F : head * F + F], keys[head], ((1,), (1,))) * (1.0 / math.sqrt(F))
        weights = jnp.where(allowed, 1.0 + inner + 0.5 * inner * inner, 0.0).astype(BF)
        own[head] = dot(weights, values[head])
        own.push(head)
    return qkv[:, : heads * F]


def old_state(cache_ref, head):
    pad = jnp.zeros((PHI_WIDE - PHI, DH), F32)
    old = [cache_ref[F + 1 :, head, :], cache_ref[1 : F + 1, head, :], cache_ref[0:1, head, :], pad]
    return jnp.concatenate([jnp.concatenate(old, axis=0), jnp.zeros((PHI_WIDE, WIDE - DH), F32)], axis=1)


def attend_part(slot, head, heads, length, q, own, state, gain_ref, pick):
    rows = q.shape[0]
    total = own + dot(phi_of(q, pick).astype(BF), state)
    square = jnp.sum(total * total, axis=-1, keepdims=True)
    gain = gain_ref[...].reshape(1, heads * DH)[:, head * DH : (head + 1) * DH]
    gain = jnp.concatenate([gain, jnp.zeros((1, WIDE - DH), F32)], axis=1)
    total = total * lax.rsqrt(square * (1.0 / DH) + 1e-05) * gain
    live = length - rows * (lax.axis_index("head") ^ slot)
    live_row = lax.broadcasted_iota(jnp.int32, (rows, WIDE), 0) < live
    return jnp.where(live_row, total, 0.0).astype(BF)


def project_part(parts, heads, w_ref, top, low, others=()):
    attended = jnp.concatenate(parts, axis=1)
    half = low.shape[0]
    w_out = out_projection(w_ref, heads)
    for order, (out, rows) in enumerate(((top, attended[:half]), (low, attended[half:]))):
        total = dot(rows, w_out)
        if others:
            total = total + others[order][...].astype(F32)
        out[...] = total.astype(BF)
        out.push()


def first_kernel(heads, len_ref, low, top, w_ref, sums, own, queries):
    conved = jnp.concatenate([top[...], low[...]], axis=0)
    queries[...] = block_part(0, heads, len_ref[0], conved, w_ref, sums, own)


def second_kernel(
    heads, len_ref, low1, top1, w_ref, low2, top2, cache, sums0, own1, queries1, own2, queries2, state3, bases, sums1, sums2
):
    conved = jnp.concatenate([top1[...], low1[...]], axis=0)
    sums1, sums2 = Near(sums1), Near(sums2)
    queries1[...] = block_part(1, heads, len_ref[0], conved, w_ref, sums1, own1)
    queries1.push()
    conved = jnp.concatenate([top2[...], low2[...]], axis=0)
    queries2[...] = block_part(2, heads, len_ref[0], conved, w_ref, sums2, own2)
    queries2.push()
    mine = lax.axis_index("head")
    for head in range(heads):
        old, sums = old_state(cache, head), (sums0[head], sums1[head], sums2[head])
        for slot in range(4):
            total = old
            for other in range(3):
                if other != slot:
                    total = total + ((mine ^ other) < (mine ^ slot)).astype(F32) * sums[other]
            if slot == 3:
                state3[head] = total.astype(BF)
            else:
                bases[slot, head] = total
        bases[3, head] = old + (sums[0] + (sums[1] + sums[2]))


def third_kernel(heads, len_ref, low, top, w_ref, state3, gain_ref, out_w_ref, top3, low3, sums3, own):
    length = len_ref[0]
    conved = jnp.concatenate([top[...], low[...]], axis=0)
    own = Near(own)
    queries = block_part(3, heads, length, conved, w_ref, sums3, own)
    pick = spreader()
    parts = []
    for head in range(heads):
        q = queries[:, head * F : head * F + F]
        parts.append(attend_part(3, head, heads, length, q, own[head], state3[head], gain_ref, pick))
    project_part(parts, heads, out_w_ref, top3, low3)


def attend_kernel(heads, slots, adds, len_ref, bases, sums3, gain_ref, out_w_ref, *refs):
    queries, own, refs = refs[: len(slots)], refs[len(slots) : 2 * len(slots)], refs[2 * len(slots) :]
    others, outs = refs[:adds], refs[adds:]
    mine = lax.axis_index("head")
    pick = spreader()
    for order, slot in enumerate(slots):
        parts = []
        for head in range(heads):
            q = queries[order][:, head * F : (head + 1) * F]
            state = bases[slot, head] + ((mine ^ 3) < (mine ^ slot)).astype(F32) * sums3[head]
            parts.append(attend_part(slot, head, heads, len_ref[0], q, own[order][head], state.astype(BF), gain_ref, pick))
        project_part(parts, heads, out_w_ref, outs[2 * order], outs[2 * order + 1], others)
    if len(outs) > 2 * len(slots):
        state_next = outs[-1]
        for head in range(heads):
            new = (bases[3, head] + sums3[head])[:, :DH]
            state_next[0, F + 1 :, head, :] = new[:QUAD]
            state_next[0, 1 : F + 1, head, :] = new[QUAD : QUAD + F]
            state_next[0, 0:1, head, :] = new[QUAD + F : QUAD + F + 1]


def add_kernel(top2, via_x, low1, via_y, two_y, two_x):
    two_y[...] = (top2[...].astype(F32) + via_x[...].astype(F32)).astype(BF)
    two_x[...] = (low1[...].astype(F32) + via_y[...].astype(F32)).astype(BF)


def total_kernel(dec0, dec1, dec2, dec3, top0, low0, two_y, two_x, out, decode_out):
    half = low0.shape[0]
    out[0, :half, :] = (top0[...].astype(F32) + two_y[...].astype(F32)).astype(BF)
    out[0, half:, :] = (low0[...].astype(F32) + two_x[...].astype(F32)).astype(BF)
    total = (dec0[...].astype(F32) + dec1[...].astype(F32)) + (dec2[...].astype(F32) + dec3[...].astype(F32))
    decode_out[0] = total[: DEC // 4].astype(BF)


def placing_rank(owners_row, axis):
    down = lax.broadcasted_iota(jnp.int32, (DEC, DEC), 0)
    along = lax.broadcasted_iota(jnp.int32, (DEC, DEC), 1)
    earlier = down < along if axis == 0 else along < down
    return jnp.sum(jnp.where(earlier & (column(owners_row) == owners_row), 1, 0), axis=axis, keepdims=True)


def send_kernel(heads, capacity, tokens_ref, tail_ref, gain_ref, taps_ref, owner_ref, slot_ref, w_ref, out):
    tokens, factor = unit_rows(tokens_ref[...])
    normed = (tokens * factor * gain_ref[...].reshape(1, D)).astype(BF).astype(F32)
    tail = tail_ref[...].astype(F32)
    taps = taps_ref[...]
    conved = taps[0:1, :] * tail[:, 0, :] + taps[1:2, :] * tail[:, 1, :]
    conved = (conved + taps[2:3, :] * normed).astype(BF)
    owners = owner_ref[...]
    target = owners * capacity + placing_rank(owners, 0)
    placing = lax.broadcasted_iota(jnp.int32, (out.shape[0], DEC), 0) == target
    cache_slot = jnp.sum(jnp.where(placing, slot_ref[...] + 1, 0), axis=1, keepdims=True) - 1
    qkv = dot(conved, projection(w_ref, heads), ((1,), (1,))).astype(BF)
    sent = dot(ones_where(placing), qkv)
    lane = lax.broadcasted_iota(jnp.int32, sent.shape, 1)
    mark = 2 * heads * F + DH
    out[...] = jnp.where(lane == mark, cache_slot.astype(F32), sent).astype(BF)


def cache_spreaders(heads):
    lane, entry = lanes_of(PHI * heads)
    feature = lane >> (heads.bit_length() - 1)
    quad = feature - (1 + F)
    a = jnp.where(quad < 0, feature - 1, quad >> 4)
    return ones_where(a == entry), ones_where((quad >= 0) & ((quad & (F - 1)) == entry))


def serve_kernel(heads, items, gain_ref, cache_ref, out, state, sem):
    flying = 6
    copies = [pltpu.make_async_copy(cache_ref.at[0, n], state.at[n], sem.at[n]) for n in range(state.shape[0])]
    for copy in copies[:flying]:
        copy.start()
    count = items.shape[0]
    mark = 2 * heads * F + DH
    first, second = cache_spreaders(heads)
    phis = []
    for head in range(heads):
        q = items[:, head * F : head * F + F]
        a = dot(q, first)
        b = dot(q, second)
        lane = lax.broadcasted_iota(jnp.int32, a.shape, 1)
        scale = jnp.where(lane < heads * (F + 1), 1.0 / math.sqrt(math.sqrt(F)), b * (1.0 / math.sqrt(2.0 * F)))
        value = jnp.where(lane < heads, 1.0, a * scale)
        phis.append(jnp.where((lane & (heads - 1)) == head, value, 0.0).astype(BF))
    phis = jnp.concatenate(phis, axis=0)
    slots = jnp.concatenate([items[:, mark : mark + 1].astype(F32)] * heads, axis=0)
    zeros = jnp.zeros((PHI * heads, WIDE - DH), BF)
    total = jnp.zeros((heads * count, WIDE), F32)
    for n in range(0, len(copies), 2):
        pair = []
        for place in (n, n + 1):
            copies[place].wait()
            for later in copies[place + flying : place + flying + 1]:
                later.start()
            pair += [state[place].reshape(PHI * heads, DH).astype(BF), zeros]
        table = dot(phis, jnp.concatenate(pair, axis=1))
        total = total + jnp.where(slots == float(n), table[:, :WIDE], 0.0)
        total = total + jnp.where(slots == float(n + 1), table[:, WIDE:], 0.0)
    gains = gain_ref[...].reshape(1, heads * DH)
    for head in range(heads):
        q = items[:, head * F : head * F + F].astype(F32)
        k = items[:, (heads + head) * F : (heads + head) * F + F].astype(F32)
        at = 2 * heads * F + head * WIDE
        v = items[:, at : at + DH].astype(F32)
        inner = jnp.sum(q * k, axis=-1, keepdims=True) * (1.0 / math.sqrt(F))
        value = total[head * count : (head + 1) * count, :DH] + (1.0 + inner + 0.5 * inner * inner) * v
        square = jnp.sum(value * value, axis=-1, keepdims=True)
        value = value * lax.rsqrt(square * (1.0 / DH) + 1e-05) * gains[:, head * DH : (head + 1) * DH]
        out[:, head * WIDE : head * WIDE + DH] = value.astype(BF)
        out[:, head * WIDE + DH : (head + 1) * WIDE] = jnp.zeros((count, WIDE - DH), BF)


def return_kernel(heads, capacity, items_ref, owner_ref, w_ref, *outs):
    owners = owner_ref[...]
    target = column(owners) * capacity + placing_rank(owners, 1)
    placing = lax.broadcasted_iota(jnp.int32, (DEC, items_ref.shape[0]), 1) == target
    attended = dot(ones_where(placing), items_ref[...]).astype(BF)
    row = lax.broadcasted_iota(jnp.int32, (4 * TILE, DEC), 0)
    entry = lax.broadcasted_iota(jnp.int32, (4 * TILE, DEC), 1)
    device = lax.axis_index("head") ^ (row // TILE)
    wanted = ((row % TILE) < DEC // 4) & (entry == device * (DEC // 4) + row % TILE)
    attended = dot(ones_where(wanted), attended).astype(BF)
    shares = dot(attended, out_projection(w_ref, heads)).astype(BF)
    for slot, out in enumerate(outs):
        out[...] = shares[slot * TILE : (slot + 1) * TILE]


def far_off(array):
    return pltpu.with_memory_space_constraint(array, pltpu.HBM)


def entries(ref):
    return [ref.at[n] for n in range(ref.shape[0])]


class Fetched:
    def __init__(self, copies, place):
        self.copies, self.place, self.here = copies, place, set()
        self.shape, self.dtype = place.shape, place.dtype

    def __getitem__(self, index):
        entry = index[0] if isinstance(index, tuple) else index
        wanted = [entry] if len(self.copies) > 1 and isinstance(entry, int) else range(len(self.copies))
        for n in wanted:
            self.wait(n)
        return self.place[index]

    def wait(self, n):
        if n not in self.here:
            self.copies[n].wait()
            self.here.add(n)


class Pushed:
    def __init__(self, copies, place):
        self.copies, self.place, self.gone = copies, place, set()
        self.shape, self.dtype = place.shape, place.dtype

    def __getitem__(self, index):
        return self.place[index]

    def __setitem__(self, index, value):
        self.place[index] = value

    def push(self, entry=0):
        if entry not in self.gone:
            self.copies[entry].start()
            self.gone.add(entry)


class Near:
    def __init__(self, ref):
        self.ref, self.shape, self.dtype, self.copies = ref, ref.shape, ref.dtype, []

    def __getitem__(self, index):
        return self.ref[index]

    def __setitem__(self, index, value):
        self.ref[index] = value

    def push(self, entry=0):
        pass


def hbm_call(kernel, outs, flops, size, scalars=(), picked=None, waits=(), loose=(), here=(), near=(), split=(), split_out=(), raw=(), scratch=()):
    def run(*args):
        count, many = len(args), len(outs)
        moved = [n for n in range(count) if n not in here and n not in raw]
        far = [n for n in range(many) if n not in near]

        def shape_in(n):
            return args[n].shape[2:] if n == picked else args[n].shape

        pieces = sum(shape_in(n)[0] if n in split else 1 for n in moved)
        pieces += sum(outs[n].shape[0] if n in split_out else 1 for n in far)

        def body(*refs):
            refs = list(refs)

            def take(number):
                taken = refs[:number]
                del refs[:number]
                return taken

            numbers, sources, _, targets = take(len(scalars)), take(count), take(len(waits)), take(many)
            places, results, own, (sem,) = dict(zip(moved, take(len(moved)))), dict(zip(far, take(len(far)))), take(len(scratch)), refs
            used = iter(range(pieces))

            def copies(source, target, apart):
                pairs = zip(entries(source), entries(target)) if apart else [(source, target)]
                return [pltpu.make_async_copy(a, b, sem.at[next(used)]) for a, b in pairs]

            ins = []
            for n, source in enumerate(sources):
                if n in here or n in raw:
                    ins.append(source)
                    continue
                if n == picked:
                    source = source.at[0, numbers[-1][0]]
                fetched = Fetched(copies(source, places[n], n in split), places[n])
                for copy in fetched.copies:
                    copy.start()
                ins.append(fetched)
            done = [
                Pushed(copies(results[n], target, n in split_out), results[n]) if n in far else Near(target)
                for n, target in enumerate(targets)
            ]
            kernel(*numbers[: len(scalars) - (picked is not None)], *ins, *done, *own)
            for n in far:
                for entry in range(len(done[n].copies)):
                    done[n].push(entry)
            for n in moved:
                for entry in range(len(ins[n].copies)):
                    ins[n].wait(entry)
            for n in far:
                for copy in done[n].copies:
                    copy.wait()

        hbm = pl.BlockSpec(memory_space=pltpu.HBM)
        in_vmem = pl.BlockSpec(memory_space=pltpu.VMEM)
        anywhere = pl.BlockSpec(memory_space=pl.ANY)
        free = set(loose) | set(here)
        return pl.pallas_call(
            body,
            out_shape=[o if n in near else pltpu.HBM(o.shape, o.dtype) for n, o in enumerate(outs)],
            in_specs=[pl.BlockSpec(memory_space=pltpu.SMEM)] * len(scalars)
            + [in_vmem if n in here else anywhere if n in loose else hbm for n in range(count)]
            + [hbm] * len(waits),
            out_specs=[in_vmem if n in near else hbm for n in range(many)],
            scratch_shapes=[pltpu.VMEM(shape_in(n), args[n].dtype) for n in moved]
            + [pltpu.VMEM(outs[n].shape, outs[n].dtype) for n in far]
            + list(scratch)
            + [pltpu.SemaphoreType.DMA((pieces,))],
            compiler_params=pltpu.CompilerParams(vmem_limit_bytes=40 * MIB),
            cost_estimate=pl.CostEstimate(flops=flops, bytes_accessed=size, transcendentals=0),
        )(*scalars, *[a if n in free else far_off(a) for n, a in enumerate(args)], *map(far_off, waits))

    return run


def shape(*dims, dtype=BF):
    return jax.ShapeDtypeStruct(dims, dtype)


def across(array, by):
    return lax.ppermute(array, "head", [(i, i ^ by) for i in range(4)])


def local_square(
    stretch_tokens,
    stretch_tail,
    decode_tokens,
    decode_tail,
    norm_gain,
    conv_taps,
    qkv_weight,
    out_gain,
    out_weight,
    state_cache,
    stretch_len,
    stretch_slot,
    decode_slot,
    decode_owner,
):
    heads = qkv_weight.shape[1]
    rows = stretch_tokens.shape[1]
    half = rows // 2
    wide = heads * (2 * F + WIDE)
    w_in = jnp.transpose(qkv_weight, (1, 2, 0))
    cache = jnp.transpose(state_cache, (0, 1, 4, 2, 3))
    length = stretch_len.astype(jnp.int32)
    slot = stretch_slot.astype(jnp.int32)
    hbm = pl.BlockSpec(memory_space=pltpu.HBM)
    piece = shape(half, D)
    block_flops = 2 * rows * D * wide + 6 * heads * rows * rows * WIDE
    attend_flops = 2 * rows * heads * WIDE * (D + PHI_WIDE)
    size = 4 * rows * D

    low, top, begin, end = hbm_call(conv_kernel, [piece, piece, shape(TILE, D), shape(TILE, D)], 20 * rows * D, size)(
        stretch_tokens[0], stretch_tail[0], norm_gain, conv_taps
    )
    low_x = across(low, 1)
    low_y = across(low, 2)
    end = from_behind(end, "head", 1)

    groups = lax.axis_size("tok")
    capacity = max(2, 2 * DEC // groups)
    count = groups * capacity
    owner_row = decode_owner.reshape(1, DEC)
    (sent,) = hbm_call(functools.partial(send_kernel, heads, capacity), [shape(count, wide)], 2 * DEC * D * wide, 2 * D * wide)(
        decode_tokens[0], decode_tail[0], norm_gain, conv_taps, owner_row, decode_slot, w_in
    )
    top = pl.pallas_call(
        lambda first_ref, top_ref, begin_ref, end_ref, taps_ref, wait_ref, *refs: rim_kernel(
            first_ref, top_ref, begin_ref, end_ref, taps_ref, *refs
        ),
        out_shape=pltpu.HBM((half, D), BF),
        in_specs=[pl.BlockSpec(memory_space=pltpu.SMEM), hbm, hbm, pl.BlockSpec(memory_space=pl.ANY), hbm, hbm],
        out_specs=hbm,
        scratch_shapes=[pltpu.VMEM((TILE, D), BF), pltpu.VMEM((TILE, D), BF), pltpu.VMEM((3, D), F32), pltpu.VMEM((TILE, D), BF)]
        + [pltpu.SemaphoreType.DMA((4,))],
        input_output_aliases={1: 0},
        compiler_params=pltpu.CompilerParams(vmem_limit_bytes=40 * MIB),
        cost_estimate=pl.CostEstimate(flops=16 * D, bytes_accessed=128 * D, transcendentals=0),
    )(lax.axis_index("head").reshape(1), far_off(top), far_off(begin), end, far_off(conv_taps), far_off(sent))
    top_x = across(top, 1)
    top_y = across(top, 2)
    items = lax.all_to_all(sent.reshape(groups, capacity, wide), "tok", split_axis=0, concat_axis=0, tiled=True)

    sums, own, queries = shape(heads, PHI_WIDE, WIDE, dtype=F32), shape(heads, rows, WIDE, dtype=F32), shape(rows, heads * F)
    sums0, own0, queries0 = hbm_call(
        functools.partial(first_kernel, heads),
        [sums, own, queries],
        block_flops,
        size,
        scalars=[length],
        split_out=(0, 1),
    )(low, top, w_in)
    (served,) = hbm_call(
        functools.partial(serve_kernel, heads),
        [shape(count, heads * WIDE)],
        2 * cache.shape[1] * heads * heads * DH * PHI * count,
        4 * cache.shape[1] * heads * WIDE * PHI,
        loose=(0,),
        raw=(2,),
        scratch=[pltpu.VMEM(cache.shape[1:], F32), pltpu.SemaphoreType.DMA((cache.shape[1],))],
        waits=[queries0],
    )(items.reshape(count, wide), out_gain, cache)
    low_y, top_x = lax.optimization_barrier((low_y, top_x, served))[:2]
    low_xy = across(low_y, 1)
    top_xy = across(top_x, 2)
    own1, queries1, own2, queries2, state3, bases = hbm_call(
        functools.partial(second_kernel, heads),
        [own, queries, own, queries, shape(heads, PHI_WIDE, WIDE), shape(4, heads, PHI_WIDE, WIDE, dtype=F32)],
        2 * block_flops,
        2 * size,
        scalars=[length, slot],
        picked=5,
        waits=[served],
        loose=(0, 1, 3, 4),
        split=(6,),
        split_out=(0, 2),
        scratch=[pltpu.VMEM(sums.shape, F32)] * 2,
    )(low_x, top_x, w_in, low_y, top_y, cache, sums0)
    top3, low3, sums3 = hbm_call(
        functools.partial(third_kernel, heads),
        [piece, piece, sums],
        block_flops + attend_flops,
        size,
        scalars=[length],
        loose=(0, 1),
        near=(0, 1),
        split=(3,),
        split_out=(2,),
        scratch=[pltpu.VMEM(own.shape, F32)],
        waits=[queries2],
    )(low_xy, top_xy, w_in, state3, out_gain, out_weight)

    def attend(slots, *blocks, others=(), keep=False, waits=()):
        ins = 4 + 2 * len(slots)
        return hbm_call(
            functools.partial(attend_kernel, heads, slots, len(others)),
            [piece] * (2 * len(slots)) + [shape(1, PHI, heads, DH, dtype=F32)] * keep,
            len(slots) * attend_flops,
            size,
            scalars=[length],
            split=(0, 1),
            loose=range(ins, ins + len(others)),
            waits=waits,
        )(bases, sums3, out_gain, out_weight, *[b[0] for b in blocks], *[b[1] for b in blocks], *others)

    via_x = across(top3, 1)
    via_y = across(low3, 2)
    served = lax.optimization_barrier((served, top3))[0]
    returned = lax.all_to_all(
        served.reshape(groups, capacity, heads * WIDE), "tok", split_axis=0, concat_axis=0, tiled=True
    ).reshape(count, heads * WIDE)
    top1, low1, top2, low2 = attend((1, 2), (queries1, own1), (queries2, own2))
    one_x = across(top1, 1)
    one_y = across(low2, 2)
    two_y, two_x = hbm_call(add_kernel, [piece, piece], 0, size, here=(1, 3), near=(0, 1), waits=[top1])(top2, via_x, low1, via_y)
    top0, low0, state_next = attend((0,), (queries0, own0), others=(one_x, one_y), keep=True, waits=[top1])
    decoded = hbm_call(
        functools.partial(return_kernel, heads, capacity),
        [shape(TILE, D)] * 4,
        2 * DEC * heads * WIDE * D,
        2 * heads * WIDE * D,
        loose=(0,),
        waits=[top0],
    )(returned, owner_row, out_weight)
    shares = [decoded[0]] + [across(decoded[by], by) for by in (1, 2, 3)]
    two_y = across(two_y, 2)
    two_x = across(two_x, 1)
    state_next = jnp.transpose(state_next, (0, 2, 3, 1))
    stretch_out, decode_out = hbm_call(
        total_kernel, [shape(1, rows, D), shape(1, DEC // 4, D)], 0, 8 * rows * D, loose=(1, 2, 3, 6, 7)
    )(*shares, top0, low0, two_y, two_x)
    return (stretch_out, decode_out, state_next)


def from_behind(array, axis, by):
    peers = lax.axis_size(axis)
    pairs = [(i, i + by) for i in range(peers) if 0 <= i + by < peers]
    return lax.ppermute(array, axis, pairs)


def rms_rows(values, gain):
    values = values.astype(jnp.float32)
    factor = lax.rsqrt(jnp.mean(values * values, axis=-1, keepdims=True) + 1e-05)
    return values * factor * gain


def features(vectors):
    breadth = vectors.shape[-1]
    linear = vectors / math.sqrt(math.sqrt(breadth))
    outer = vectors[..., :, None] * vectors[..., None, :] / math.sqrt(2.0 * breadth)
    outer = outer.reshape(vectors.shape[:-1] + (breadth * breadth,))
    ones = jnp.ones(vectors.shape[:-1] + (1,), vectors.dtype)
    return jnp.concatenate([ones, linear, outer], axis=-1)


def convolve(tail, normed, conv_taps):
    joined = jnp.concatenate([tail, normed], axis=-2).astype(jnp.float32)
    span_rows = normed.shape[-2]
    total = conv_taps[0] * joined[..., 0:span_rows, :]
    total = total + conv_taps[1] * joined[..., 1 : span_rows + 1, :]
    total = total + conv_taps[2] * joined[..., 2 : span_rows + 2, :]
    return total.astype(jnp.bfloat16)


def decode_items(items, slot_items, cache_own, out_gain, head_count):
    item_count = items.shape[0]
    shaped = items.reshape(item_count, head_count, 2 * F + DH).astype(jnp.float32)
    queries = shaped[:, :, :F]
    key_feats = shaped[:, :, F : 2 * F]
    values = shaped[:, :, 2 * F :]
    slot_total = cache_own.shape[0]
    table = jnp.einsum(
        "nhp,shdp->nshd", features(queries), cache_own, precision=lax.Precision.HIGHEST
    )
    picker = (slot_items[:, None] == jnp.arange(slot_total)[None, :]).astype(jnp.float32)
    carried = jnp.einsum("ns,nshd->nhd", picker, table, precision=lax.Precision.HIGHEST)
    inner = jnp.sum(queries * key_feats, axis=-1) / math.sqrt(F)
    own_term = (1.0 + inner + 0.5 * inner * inner)[..., None] * values
    attended = rms_rows(carried + own_term, out_gain.reshape(head_count, DH))
    return attended.astype(jnp.bfloat16).reshape(item_count, head_count * DH)


def local(
    stretch_tokens,
    stretch_tail,
    decode_tokens,
    decode_tail,
    norm_gain,
    conv_taps,
    qkv_weight,
    out_gain,
    out_weight,
    state_cache,
    stretch_len,
    stretch_slot,
    decode_slot,
    decode_owner,
):
    head_count = qkv_weight.shape[1]
    block_width = qkv_weight.shape[2]
    rows_own = stretch_tokens.shape[1]
    w_flat = qkv_weight.reshape(D, head_count * block_width)
    gains = out_gain.reshape(head_count, DH)
    normed = rms_rows(stretch_tokens[0], norm_gain).astype(jnp.bfloat16)
    rim_rows = from_behind(normed[rows_own - 2 :], "head", 1)
    first_dev = lax.axis_index("head") == 0
    rim_rows = jnp.where(first_dev, stretch_tail[0], rim_rows)
    conved = convolve(rim_rows, normed, conv_taps)
    grouped = jnp.dot(
        lax.all_gather(conved, "head", axis=0, tiled=True),
        w_flat,
        preferred_element_type=jnp.float32,
    ).astype(jnp.bfloat16)
    grouped = grouped.reshape(STRETCH, head_count, block_width)
    queries = grouped[:, :, :F]
    key_feats = grouped[:, :, F : 2 * F]
    values = grouped[:, :, 2 * F :]
    length = stretch_len[0]
    positions = jnp.arange(STRETCH)
    valid_rows = positions < length
    state_old = lax.dynamic_index_in_dim(state_cache[0], stretch_slot[0], 0, keepdims=False)
    carried = jnp.einsum(
        "ihp,hdp->ihd",
        features(queries.astype(jnp.float32)),
        state_old,
        precision=lax.Precision.HIGHEST,
    )
    block_rows = min(512, STRETCH)
    pieces = []
    for anchor in range(0, STRETCH, block_rows):
        finish = anchor + block_rows
        inner = jnp.einsum(
            "ihf,jhf->hij",
            queries[anchor:finish],
            key_feats[:finish],
            preferred_element_type=jnp.float32,
        ) / math.sqrt(F)
        weights = 1.0 + inner + 0.5 * inner * inner
        allowed = (positions[None, :finish] <= positions[anchor:finish, None]) & valid_rows[
            None, :finish
        ]
        weights = jnp.where(allowed[None], weights, 0.0).astype(jnp.bfloat16)
        pieces.append(
            jnp.einsum("hij,jhd->ihd", weights, values[:finish], preferred_element_type=jnp.float32)
        )
    local_sum = jnp.concatenate(pieces, axis=0)
    attended = rms_rows(carried + local_sum, gains)
    attended = (
        jnp.where(valid_rows[:, None, None], attended, 0.0)
        .astype(jnp.bfloat16)
        .reshape(STRETCH, head_count * DH)
    )
    key_phi = jnp.where(
        valid_rows[:, None, None], features(key_feats.astype(jnp.float32)), 0.0
    ).astype(jnp.bfloat16)
    state_next = state_old + jnp.einsum(
        "jhd,jhp->hdp", values, key_phi, preferred_element_type=jnp.float32
    )
    part_rows = attended
    stretch_out = lax.psum_scatter(
        jnp.dot(part_rows, out_weight, preferred_element_type=jnp.float32).astype(jnp.bfloat16),
        "head",
        scatter_dimension=0,
        tiled=True,
    )
    dec_normed = rms_rows(decode_tokens[0], norm_gain).astype(jnp.bfloat16)
    dec_conved = convolve(decode_tail[0], dec_normed[:, None, :], conv_taps)[:, 0, :]
    dec_qkv = jnp.dot(dec_conved, w_flat, preferred_element_type=jnp.float32).astype(jnp.bfloat16)
    owners = decode_owner[0, :, 0]
    slots_here = decode_slot[0]
    groups = lax.axis_size("tok")
    capacity = max(2, 2 * DEC // groups)
    earlier = jnp.arange(DEC)[None, :] < jnp.arange(DEC)[:, None]
    same_owner = owners[None, :] == owners[:, None]
    rank_in = jnp.sum(earlier & same_owner, axis=1)
    target = owners * capacity + rank_in
    placing = jnp.arange(groups * capacity)[:, None] == target[None, :]
    sent_rows = jnp.dot(
        placing.astype(jnp.bfloat16), dec_qkv, preferred_element_type=jnp.float32
    ).astype(jnp.bfloat16)
    sent_rows = sent_rows.reshape(groups, capacity, head_count * block_width)
    sent_slots = jnp.sum(jnp.where(placing, slots_here[None, :] + 1, 0), axis=1) - 1
    sent_slots = sent_slots.reshape(groups, capacity)
    item_rows = lax.all_to_all(sent_rows, "tok", split_axis=0, concat_axis=0, tiled=True)
    item_slots = lax.all_to_all(sent_slots, "tok", split_axis=0, concat_axis=0, tiled=True)
    item_count = item_rows.shape[1]
    flat_out = decode_items(
        item_rows.reshape(groups * item_count, head_count * block_width),
        item_slots.reshape(groups * item_count),
        state_cache[0],
        out_gain,
        head_count,
    )
    served = flat_out.reshape(groups, item_count, head_count * DH)
    returned = lax.all_to_all(served, "tok", split_axis=0, concat_axis=0, tiled=True)
    dec_attended = jnp.dot(
        jnp.transpose(placing).astype(jnp.bfloat16),
        returned.reshape(groups * capacity, head_count * DH),
        preferred_element_type=jnp.float32,
    ).astype(jnp.bfloat16)
    part_rows = dec_attended
    decode_out = lax.psum_scatter(
        jnp.dot(part_rows, out_weight, preferred_element_type=jnp.float32).astype(jnp.bfloat16),
        "head",
        scatter_dimension=0,
        tiled=True,
    )
    return (stretch_out[None], decode_out[None], state_next[None])


def solution(mesh):
    in_specs = (
        P("tok", "head", None),
        P("tok", None, None),
        P("tok", None, None),
        P("tok", None, None, None),
        P(),
        P(),
        P(None, "head", None),
        P("head"),
        P("head", None),
        P("tok", None, "head", None, None),
        P("tok"),
        P("tok"),
        P("tok", None),
        P("tok", None, None),
    )
    out_specs = (P("tok", "head", None), P("tok", "head", None), P("tok", "head", None, None))
    chosen = local_square if mesh.shape["head"] == 4 else local
    return jax.shard_map(chosen, mesh=mesh, in_specs=in_specs, out_specs=out_specs, check_vma=False)
```

```python
import functools
import math

import jax
import jax.numpy as jnp
import numpy as np
from jax import lax
from jax.experimental import pallas as pl
from jax.experimental.pallas import tpu as pltpu
from jax.sharding import PartitionSpec as P

D = 1792
DH = 112
F = 16
STRETCH = 1024
DEC = 32
QUAD = F * F
PHI = 1 + F + QUAD
WIDE = 128
PHI_WIDE = QUAD + 128
TILE = 16
MIB = 1 << 20
BF = jnp.bfloat16
F32 = jnp.float32


def lanes_of(size):
    return lax.broadcasted_iota(jnp.int32, (F, size), 1), lax.broadcasted_iota(jnp.int32, (F, size), 0)


def ones_where(mask):
    return jnp.where(mask, 1.0, 0.0).astype(BF)


def spreader():
    lane, entry = lanes_of(PHI_WIDE)
    return ones_where(jnp.where(lane < QUAD, lane >> 4, lane & (F - 1)) == entry)


def dot(left, right, contract=((1,), (0,))):
    return lax.dot_general(left, right, (contract, ((), ())), preferred_element_type=F32)


def phi_of(vectors, pick):
    spread = dot(vectors, pick)
    a, b = spread[:, :QUAD], spread[:, QUAD:]
    quad = a * jnp.concatenate([b] * (QUAD // 128), axis=1) * (1.0 / math.sqrt(2.0 * F))
    lane = lax.broadcasted_iota(jnp.int32, b.shape, 1)
    rest = jnp.where(lane < F, b * (1.0 / math.sqrt(math.sqrt(F))), jnp.where(lane == F, 1.0, 0.0))
    return jnp.concatenate([quad, rest], axis=1)


def unit_rows(values):
    values = values.astype(F32)
    total = jnp.sum(values * values, axis=-1, keepdims=True)
    return values, lax.rsqrt(total * (1.0 / D) + 1e-05)


def column(row):
    size = row.shape[1]
    same = lax.broadcasted_iota(jnp.int32, (size, size), 0) == lax.broadcasted_iota(jnp.int32, (size, size), 1)
    return jnp.sum(jnp.where(same, row, 0), axis=1, keepdims=True)


def projection(w_ref, heads):
    pieces = [w_ref[h, :F, :] for h in range(heads)] + [w_ref[h, F : 2 * F, :] for h in range(heads)]
    for h in range(heads):
        pieces += [w_ref[h, 2 * F :, :], jnp.zeros((WIDE - DH, D), w_ref.dtype)]
    return jnp.concatenate(pieces, axis=0)


def out_projection(w_ref, heads):
    pieces = []
    for h in range(heads):
        pieces += [w_ref[h * DH : (h + 1) * DH, :], jnp.zeros((WIDE - DH, D), w_ref.dtype)]
    return jnp.concatenate(pieces, axis=0)


def conv_kernel(tokens_ref, tail_ref, gain_ref, taps_ref, low, top, begin, end):
    rows = tokens_ref.shape[0]
    half = rows // 2
    gain = gain_ref[...].reshape(1, D)
    taps = taps_ref[...]
    _, factor = unit_rows(tokens_ref[...])
    step = 256
    row = lax.broadcasted_iota(jnp.int32, (rows, step), 0)
    for at in range(0, D, step):
        cols = slice(at, at + step)
        normed = tokens_ref[:, cols].astype(F32) * factor * gain[:, cols]
        normed = normed.astype(BF)
        begin[:, cols] = normed[:16]
        end[:, cols] = normed[rows - 16 :]
        normed = normed.astype(F32)
        tail = tail_ref[:, cols].astype(F32)
        one = jnp.where(row == 0, tail[1:2], pltpu.roll(normed, 1, 0))
        two = pltpu.roll(normed, 2, 0)
        two = jnp.where(row == 0, tail[0:1], jnp.where(row == 1, tail[1:2], two))
        total = taps[0:1, cols] * two + taps[1:2, cols] * one + taps[2:3, cols] * normed
        total = total.astype(BF)
        top[:, cols] = total[:half]
        low[:, cols] = total[half:]


def rim_kernel(first_ref, top_ref, begin_ref, end_ref, taps_ref, out_ref, begin, end, taps, rows, sem):
    copies = [
        pltpu.make_async_copy(src, place, sem.at[n])
        for n, (src, place) in enumerate([(begin_ref, begin), (end_ref, end), (taps_ref, taps)])
    ]
    for copy in copies:
        copy.start()
    for copy in copies:
        copy.wait()
    now = begin[...].astype(F32)
    last = end[...].astype(F32)
    row = lax.broadcasted_iota(jnp.int32, now.shape, 0)
    one = jnp.where(row == 0, last[15:16], pltpu.roll(now, 1, 0))
    two = jnp.where(row == 0, last[14:15], jnp.where(row == 1, last[15:16], pltpu.roll(now, 2, 0)))
    rows[...] = (taps[0:1, :] * two + taps[1:2, :] * one + taps[2:3, :] * now).astype(BF)

    @pl.when(first_ref[0] != 0)
    def _():
        back = pltpu.make_async_copy(rows, out_ref.at[:16], sem.at[3])
        back.start()
        back.wait()


def qkv_of(heads, top, low, w_ref):
    conved = jnp.concatenate([top[...], low[...]], axis=0)
    return dot(conved, projection(w_ref, heads), ((1,), (1,))).astype(BF)


def parts_of(qkv, heads, head):
    at = 2 * heads * F + head * WIDE
    return qkv[:, head * F : (head + 1) * F], qkv[:, (heads + head) * F : (heads + head + 1) * F], qkv[:, at : at + WIDE]


def sums_of(slot, heads, head, length, qkv, pick):
    _, k, v = parts_of(qkv, heads, head)
    live = length - v.shape[0] * (lax.axis_index("head") ^ slot)
    live_row = lax.broadcasted_iota(jnp.int32, v.shape, 0) < live
    v = jnp.where(live_row, v.astype(F32), 0.0).astype(BF)
    return dot(phi_of(k, pick).astype(BF), v, ((0,), (0,)))


def own_of(slot, heads, head, length, qkv):
    q, k, v = parts_of(qkv, heads, head)
    rows = v.shape[0]
    live = length - rows * (lax.axis_index("head") ^ slot)
    row = lax.broadcasted_iota(jnp.int32, (rows, rows), 0)
    col = lax.broadcasted_iota(jnp.int32, (rows, rows), 1)
    shifted = dot(q, k, ((1,), (1,))) * (1.0 / math.sqrt(F)) + 1.0
    weights = jnp.where((col <= row) & (col < live), 0.5 * shifted * shifted + 0.5, 0.0).astype(BF)
    return dot(weights, v)


def old_state(cache_ref, head):
    pad = jnp.zeros((PHI_WIDE - PHI, DH), F32)
    old = [cache_ref[F + 1 :, head, :], cache_ref[1 : F + 1, head, :], cache_ref[0:1, head, :], pad]
    return jnp.concatenate([jnp.concatenate(old, axis=0), jnp.zeros((PHI_WIDE, WIDE - DH), F32)], axis=1)


def attend_part(slot, head, heads, length, q, own, state, gain_ref, pick):
    rows = q.shape[0]
    total = own + dot(phi_of(q, pick).astype(BF), state)
    square = jnp.sum(total * total, axis=-1, keepdims=True)
    gain = gain_ref[...].reshape(1, heads * DH)[:, head * DH : (head + 1) * DH]
    gain = jnp.concatenate([gain, jnp.zeros((1, WIDE - DH), F32)], axis=1)
    total = total * lax.rsqrt(square * (1.0 / DH) + 1e-05) * gain
    live = length - rows * (lax.axis_index("head") ^ slot)
    live_row = lax.broadcasted_iota(jnp.int32, (rows, WIDE), 0) < live
    return jnp.where(live_row, total, 0.0).astype(BF)


def project_part(parts, heads, w_ref, top, low):
    attended = jnp.concatenate(parts, axis=1)
    half = low.shape[0]
    w_out = out_projection(w_ref, heads)
    for out, rows in ((top, attended[:half]), (low, attended[half:])):
        out[...] = dot(rows, w_out).astype(BF)
        out.push()


def first_kernel(heads, len_ref, low, top, w_ref, sums, own, queries):
    qkv = qkv_of(heads, top, low, w_ref)
    pick = spreader()
    for head in range(heads):
        sums[head] = sums_of(0, heads, head, len_ref[0], qkv, pick)
    sums.push()
    for head in range(heads):
        own[head] = own_of(0, heads, head, len_ref[0], qkv)
    queries[...] = qkv[:, : heads * F]


def second_kernel(heads, len_ref, low1, top1, w_ref, low2, top2, cache, sums0, sums1, qkv1, sums2, qkv2, state3):
    pick = spreader()
    for slot, low, top, sums, qkv in ((1, low1, top1, sums1, qkv1), (2, low2, top2, sums2, qkv2)):
        found = qkv_of(heads, top, low, w_ref)
        qkv[...] = found
        qkv.push()
        for head in range(heads):
            sums[head] = sums_of(slot, heads, head, len_ref[0], found, pick)
        sums.push()
    for head in range(heads):
        state3[head] = state_before(3, old_state(cache, head), (sums0[head], sums1[head], sums2[head]))


def state_before(slot, old, sums):
    mine = lax.axis_index("head")
    for other, part in enumerate(sums):
        if other != slot:
            old = old + ((mine ^ other) < (mine ^ slot)).astype(F32) * part
    return old.astype(BF)


def third_kernel(heads, len_ref, low, top, w_ref, state3, gain_ref, out_w_ref, top3, low3, qkv3):
    length = len_ref[0]
    qkv = qkv_of(heads, top, low, w_ref)
    qkv3[...] = qkv
    qkv3.push()
    pick = spreader()
    parts = []
    for head in range(heads):
        q = parts_of(qkv, heads, head)[0]
        own = own_of(3, heads, head, length, qkv)
        parts.append(attend_part(3, head, heads, length, q, own, state3[head], gain_ref, pick))
    project_part(parts, heads, out_w_ref, top3, low3)


def fourth_kernel(
    heads, len_ref, qkv3, qkv1, cache, sums0, sums1, sums2, qkv2, gain_ref, out_w_ref, top1, low1, top2, low2, sums3
):
    pick = spreader()
    length = len_ref[0]
    for head in range(heads):
        sums3[head] = sums_of(3, heads, head, length, qkv3, pick)
    sums3.push()
    for slot, qkv, top, low in ((1, qkv1, top1, low1), (2, qkv2, top2, low2)):
        parts = []
        for head in range(heads):
            q = parts_of(qkv, heads, head)[0]
            own = own_of(slot, heads, head, length, qkv)
            state = state_before(slot, old_state(cache, head), (sums0[head], sums1[head], sums2[head], sums3[head]))
            parts.append(attend_part(slot, head, heads, length, q, own, state, gain_ref, pick))
        project_part(parts, heads, out_w_ref, top, low)


def fifth_kernel(
    heads, len_ref, cache, sums0, sums1, sums2, sums3, queries, own, gain_ref, out_w_ref, top0, low0, state_next
):
    pick = spreader()
    parts = []
    for head in range(heads):
        old = old_state(cache, head)
        sums = [part[head] for part in (sums0, sums1, sums2, sums3)]
        q = queries[:, head * F : (head + 1) * F]
        state = state_before(0, old, sums)
        parts.append(attend_part(0, head, heads, len_ref[0], q, own[head], state, gain_ref, pick))
        new = (old + (sums[0] + sums[1]) + (sums[2] + sums[3]))[:, :DH]
        state_next[0, F + 1 :, head, :] = new[:QUAD]
        state_next[0, 1 : F + 1, head, :] = new[QUAD : QUAD + F]
        state_next[0, 0:1, head, :] = new[QUAD + F : QUAD + F + 1]
    project_part(parts, heads, out_w_ref, top0, low0)


def add_kernel(top2, via_x, low1, via_y, two_y, two_x):
    two_y[...] = (top2[...].astype(F32) + via_x[...].astype(F32)).astype(BF)
    two_x[...] = (low1[...].astype(F32) + via_y[...].astype(F32)).astype(BF)


def total_kernel(top0, one_x, two_y, low0, one_y, two_x, dec0, dec1, dec2, dec3, out, decode_out):
    out[0] = (top0[...].astype(F32) + one_x[...].astype(F32) + two_y[...].astype(F32)).astype(BF)
    out.push(0)
    out[1] = (low0[...].astype(F32) + one_y[...].astype(F32) + two_x[...].astype(F32)).astype(BF)
    out.push(1)
    total = (dec0[...].astype(F32) + dec1[...].astype(F32)) + (dec2[...].astype(F32) + dec3[...].astype(F32))
    decode_out[0] = total[: DEC // 4].astype(BF)


def placing_rank(owners_row, axis):
    down = lax.broadcasted_iota(jnp.int32, (DEC, DEC), 0)
    along = lax.broadcasted_iota(jnp.int32, (DEC, DEC), 1)
    earlier = down < along if axis == 0 else along < down
    return jnp.sum(jnp.where(earlier & (column(owners_row) == owners_row), 1, 0), axis=axis, keepdims=True)


def send_kernel(heads, capacity, tokens_ref, tail_ref, gain_ref, taps_ref, owner_ref, slot_ref, w_ref, out):
    tokens, factor = unit_rows(tokens_ref[...])
    normed = (tokens * factor * gain_ref[...].reshape(1, D)).astype(BF).astype(F32)
    tail = tail_ref[...].astype(F32)
    taps = taps_ref[...]
    conved = taps[0:1, :] * tail[:, 0, :] + taps[1:2, :] * tail[:, 1, :]
    conved = (conved + taps[2:3, :] * normed).astype(BF)
    owners = owner_ref[...]
    target = owners * capacity + placing_rank(owners, 0)
    placing = lax.broadcasted_iota(jnp.int32, (out.shape[0], DEC), 0) == target
    cache_slot = jnp.sum(jnp.where(placing, slot_ref[...] + 1, 0), axis=1, keepdims=True) - 1
    qkv = dot(conved, projection(w_ref, heads), ((1,), (1,))).astype(BF)
    sent = dot(ones_where(placing), qkv)
    lane = lax.broadcasted_iota(jnp.int32, sent.shape, 1)
    mark = 2 * heads * F + DH
    out[...] = jnp.where(lane == mark, cache_slot.astype(F32), sent).astype(BF)


def cache_spreaders(heads):
    lane, entry = lanes_of(PHI * heads)
    feature = lane >> (heads.bit_length() - 1)
    quad = feature - (1 + F)
    a = jnp.where(quad < 0, feature - 1, quad >> 4)
    return ones_where(a == entry), ones_where((quad >= 0) & ((quad & (F - 1)) == entry))


def serve_kernel(heads, items, gain_ref, cache_ref, out, state, sem):
    flying = 6
    copies = [pltpu.make_async_copy(cache_ref.at[0, n], state.at[n], sem.at[n]) for n in range(state.shape[0])]
    for copy in copies[:flying]:
        copy.start()
    count = items.shape[0]
    mark = 2 * heads * F + DH
    first, second = cache_spreaders(heads)
    phis = []
    for head in range(heads):
        q = items[:, head * F : head * F + F]
        a = dot(q, first)
        b = dot(q, second)
        lane = lax.broadcasted_iota(jnp.int32, a.shape, 1)
        scale = jnp.where(lane < heads * (F + 1), 1.0 / math.sqrt(math.sqrt(F)), b * (1.0 / math.sqrt(2.0 * F)))
        value = jnp.where(lane < heads, 1.0, a * scale)
        phis.append(jnp.where((lane & (heads - 1)) == head, value, 0.0).astype(BF))
    phis = jnp.concatenate(phis, axis=0)
    slots = jnp.concatenate([items[:, mark : mark + 1].astype(F32)] * heads, axis=0)
    zeros = jnp.zeros((PHI * heads, WIDE - DH), BF)
    total = jnp.zeros((heads * count, WIDE), F32)
    for n in range(0, len(copies), 2):
        pair = []
        for place in (n, n + 1):
            copies[place].wait()
            for later in copies[place + flying : place + flying + 1]:
                later.start()
            pair += [state[place].reshape(PHI * heads, DH).astype(BF), zeros]
        table = dot(phis, jnp.concatenate(pair, axis=1))
        total = total + jnp.where(slots == float(n), table[:, :WIDE], 0.0)
        total = total + jnp.where(slots == float(n + 1), table[:, WIDE:], 0.0)
    gains = gain_ref[...].reshape(1, heads * DH)
    for head in range(heads):
        q = items[:, head * F : head * F + F].astype(F32)
        k = items[:, (heads + head) * F : (heads + head) * F + F].astype(F32)
        at = 2 * heads * F + head * WIDE
        v = items[:, at : at + DH].astype(F32)
        inner = jnp.sum(q * k, axis=-1, keepdims=True) * (1.0 / math.sqrt(F))
        value = total[head * count : (head + 1) * count, :DH] + (1.0 + inner + 0.5 * inner * inner) * v
        square = jnp.sum(value * value, axis=-1, keepdims=True)
        value = value * lax.rsqrt(square * (1.0 / DH) + 1e-05) * gains[:, head * DH : (head + 1) * DH]
        out[:, head * WIDE : head * WIDE + DH] = value.astype(BF)
        out[:, head * WIDE + DH : (head + 1) * WIDE] = jnp.zeros((count, WIDE - DH), BF)


def return_kernel(heads, capacity, items_ref, owner_ref, w_ref, seen_x, seen_y, *outs):
    owners = owner_ref[...]
    target = column(owners) * capacity + placing_rank(owners, 1)
    placing = lax.broadcasted_iota(jnp.int32, (DEC, items_ref.shape[0]), 1) == target
    attended = dot(ones_where(placing), items_ref[...]).astype(BF)
    row = lax.broadcasted_iota(jnp.int32, (4 * TILE, DEC), 0)
    entry = lax.broadcasted_iota(jnp.int32, (4 * TILE, DEC), 1)
    device = lax.axis_index("head") ^ (row // TILE)
    wanted = ((row % TILE) < DEC // 4) & (entry == device * (DEC // 4) + row % TILE)
    attended = dot(ones_where(wanted), attended).astype(BF)
    shares = dot(attended, out_projection(w_ref, heads)).astype(BF)
    for slot, out in enumerate(outs):
        out[...] = shares[slot * TILE : (slot + 1) * TILE]


def far_off(array):
    return pltpu.with_memory_space_constraint(array, pltpu.HBM)


def entries(ref):
    return [ref.at[n] for n in range(ref.shape[0])]


class Fetched:
    def __init__(self, copies, place):
        self.copies, self.place, self.here = copies, place, set()
        self.shape, self.dtype = place.shape, place.dtype

    def __getitem__(self, index):
        entry = index[0] if isinstance(index, tuple) else index
        wanted = [entry] if len(self.copies) > 1 and isinstance(entry, int) else range(len(self.copies))
        for n in wanted:
            self.wait(n)
        return self.place[index]

    def wait(self, n):
        if n not in self.here:
            self.copies[n].wait()
            self.here.add(n)


class Pushed:
    def __init__(self, copies, place):
        self.copies, self.place, self.gone = copies, place, set()
        self.shape, self.dtype = place.shape, place.dtype

    def __getitem__(self, index):
        return self.place[index]

    def __setitem__(self, index, value):
        self.place[index] = value

    def push(self, entry=None):
        if (entry is None) == (len(self.copies) == 1):
            self.send(entry or 0)

    def send(self, n):
        if n not in self.gone:
            self.copies[n].start()
            self.gone.add(n)


class Near:
    def __init__(self, ref):
        self.ref, self.shape, self.dtype, self.copies = ref, ref.shape, ref.dtype, []

    def __getitem__(self, index):
        return self.ref[index]

    def __setitem__(self, index, value):
        self.ref[index] = value

    def push(self, entry=None):
        pass


def hbm_call(kernel, outs, flops, size, scalars=(), picked=None, waits=(), loose=(), here=(), near=(), split=(), split_out=(), raw=(), scratch=()):
    def run(*args):
        count, many = len(args), len(outs)
        moved = [n for n in range(count) if n not in here and n not in raw]
        far = [n for n in range(many) if n not in near]

        def shape_in(n):
            return args[n].shape[2:] if n == picked else args[n].shape

        pieces = sum(shape_in(n)[0] if n in split else 1 for n in moved)
        pieces += sum(outs[n].shape[0] if n in split_out else 1 for n in far)

        def body(*refs):
            refs = list(refs)

            def take(number):
                taken = refs[:number]
                del refs[:number]
                return taken

            numbers, sources, _, targets = take(len(scalars)), take(count), take(len(waits)), take(many)
            places, results, own, (sem,) = dict(zip(moved, take(len(moved)))), dict(zip(far, take(len(far)))), take(len(scratch)), refs
            used = iter(range(pieces))

            def copies(source, target, apart):
                pairs = zip(entries(source), entries(target)) if apart else [(source, target)]
                return [pltpu.make_async_copy(a, b, sem.at[next(used)]) for a, b in pairs]

            ins = []
            for n, source in enumerate(sources):
                if n in here or n in raw:
                    ins.append(source)
                    continue
                if n == picked:
                    source = source.at[0, numbers[-1][0]]
                fetched = Fetched(copies(source, places[n], n in split), places[n])
                for copy in fetched.copies:
                    copy.start()
                ins.append(fetched)
            done = [
                Pushed(copies(results[n], target, n in split_out), results[n]) if n in far else Near(target)
                for n, target in enumerate(targets)
            ]
            kernel(*numbers[: len(scalars) - (picked is not None)], *ins, *done, *own)
            for n in far:
                for entry in range(len(done[n].copies)):
                    done[n].send(entry)
            for n in moved:
                for entry in range(len(ins[n].copies)):
                    ins[n].wait(entry)
            for n in far:
                for copy in done[n].copies:
                    copy.wait()

        hbm = pl.BlockSpec(memory_space=pltpu.HBM)
        in_vmem = pl.BlockSpec(memory_space=pltpu.VMEM)
        anywhere = pl.BlockSpec(memory_space=pl.ANY)
        free = set(loose) | set(here)
        return pl.pallas_call(
            body,
            out_shape=[o if n in near else pltpu.HBM(o.shape, o.dtype) for n, o in enumerate(outs)],
            in_specs=[pl.BlockSpec(memory_space=pltpu.SMEM)] * len(scalars)
            + [in_vmem if n in here else anywhere if n in loose else hbm for n in range(count)]
            + [hbm] * len(waits),
            out_specs=[in_vmem if n in near else hbm for n in range(many)],
            scratch_shapes=[pltpu.VMEM(shape_in(n), args[n].dtype) for n in moved]
            + [pltpu.VMEM(outs[n].shape, outs[n].dtype) for n in far]
            + list(scratch)
            + [pltpu.SemaphoreType.DMA((pieces,))],
            compiler_params=pltpu.CompilerParams(vmem_limit_bytes=40 * MIB),
            cost_estimate=pl.CostEstimate(flops=flops, bytes_accessed=size, transcendentals=0),
        )(*scalars, *[a if n in free else far_off(a) for n, a in enumerate(args)], *map(far_off, waits))

    return run


def shape(*dims, dtype=BF):
    return jax.ShapeDtypeStruct(dims, dtype)


def across(array, by):
    return lax.ppermute(array, "head", [(i, i ^ by) for i in range(4)])


def local_square(
    stretch_tokens,
    stretch_tail,
    decode_tokens,
    decode_tail,
    norm_gain,
    conv_taps,
    qkv_weight,
    out_gain,
    out_weight,
    state_cache,
    stretch_len,
    stretch_slot,
    decode_slot,
    decode_owner,
):
    heads = qkv_weight.shape[1]
    rows = stretch_tokens.shape[1]
    half = rows // 2
    wide = heads * (2 * F + WIDE)
    w_in = jnp.transpose(qkv_weight, (1, 2, 0))
    cache = jnp.transpose(state_cache, (0, 1, 4, 2, 3))
    length = stretch_len.astype(jnp.int32)
    slot = stretch_slot.astype(jnp.int32)
    hbm = pl.BlockSpec(memory_space=pltpu.HBM)
    piece = shape(half, D)
    block_flops = 2 * rows * D * wide + 6 * heads * rows * rows * WIDE
    attend_flops = 2 * rows * heads * WIDE * (D + PHI_WIDE)
    size = 4 * rows * D

    low, top, begin, end = hbm_call(conv_kernel, [piece, piece, shape(TILE, D), shape(TILE, D)], 20 * rows * D, size)(
        stretch_tokens[0], stretch_tail[0], norm_gain, conv_taps
    )
    low_x = across(low, 1)
    low_y = across(low, 2)
    end = from_behind(end, "head", 1)

    groups = lax.axis_size("tok")
    capacity = max(2, 2 * DEC // groups)
    count = groups * capacity
    owner_row = decode_owner.reshape(1, DEC)
    (sent,) = hbm_call(functools.partial(send_kernel, heads, capacity), [shape(count, wide)], 2 * DEC * D * wide, 2 * D * wide)(
        decode_tokens[0], decode_tail[0], norm_gain, conv_taps, owner_row, decode_slot, w_in
    )
    top = pl.pallas_call(
        lambda first_ref, top_ref, begin_ref, end_ref, taps_ref, wait_ref, *refs: rim_kernel(
            first_ref, top_ref, begin_ref, end_ref, taps_ref, *refs
        ),
        out_shape=pltpu.HBM((half, D), BF),
        in_specs=[pl.BlockSpec(memory_space=pltpu.SMEM), hbm, hbm, pl.BlockSpec(memory_space=pl.ANY), hbm, hbm],
        out_specs=hbm,
        scratch_shapes=[pltpu.VMEM((TILE, D), BF), pltpu.VMEM((TILE, D), BF), pltpu.VMEM((3, D), F32), pltpu.VMEM((TILE, D), BF)]
        + [pltpu.SemaphoreType.DMA((4,))],
        input_output_aliases={1: 0},
        compiler_params=pltpu.CompilerParams(vmem_limit_bytes=40 * MIB),
        cost_estimate=pl.CostEstimate(flops=16 * D, bytes_accessed=128 * D, transcendentals=0),
    )(lax.axis_index("head").reshape(1), far_off(top), far_off(begin), end, far_off(conv_taps), far_off(sent))
    top_x = across(top, 1)
    top_y = across(top, 2)
    items = lax.all_to_all(sent.reshape(groups, capacity, wide), "tok", split_axis=0, concat_axis=0, tiled=True)

    sums, own, queries = shape(heads, PHI_WIDE, WIDE, dtype=F32), shape(heads, rows, WIDE, dtype=F32), shape(rows, heads * F)
    sums0, own0, queries0 = hbm_call(
        functools.partial(first_kernel, heads),
        [sums, own, queries],
        block_flops,
        size,
        scalars=[length],
    )(low, top, w_in)
    low_y, top_x = lax.optimization_barrier((low_y, top_x, queries0, items))[:2]
    low_xy = across(low_y, 1)
    top_xy = across(top_x, 2)
    (served,) = hbm_call(
        functools.partial(serve_kernel, heads),
        [shape(count, heads * WIDE)],
        2 * cache.shape[1] * heads * heads * DH * PHI * count,
        4 * cache.shape[1] * heads * WIDE * PHI,
        loose=(0,),
        raw=(2,),
        scratch=[pltpu.VMEM(cache.shape[1:], F32), pltpu.SemaphoreType.DMA((cache.shape[1],))],
        waits=[queries0],
    )(items.reshape(count, wide), out_gain, cache)
    blocks = shape(rows, wide)
    sums1, qkv1, sums2, qkv2, state3 = hbm_call(
        functools.partial(second_kernel, heads),
        [sums, blocks, sums, blocks, shape(heads, PHI_WIDE, WIDE)],
        2 * block_flops,
        2 * size,
        scalars=[length, slot],
        picked=5,
        waits=[served],
        loose=(0, 1, 3, 4),
    )(low_x, top_x, w_in, low_y, top_y, cache, sums0)
    top3, low3, qkv3 = hbm_call(
        functools.partial(third_kernel, heads),
        [piece, piece, blocks],
        block_flops + attend_flops,
        size,
        scalars=[length],
        loose=(0, 1),
        near=(0, 1),
        waits=[qkv2],
    )(low_xy, top_xy, w_in, state3, out_gain, out_weight)

    via_x = across(top3, 1)
    via_y = across(low3, 2)
    served = lax.optimization_barrier((served, top3))[0]
    returned = lax.all_to_all(
        served.reshape(groups, capacity, heads * WIDE), "tok", split_axis=0, concat_axis=0, tiled=True
    ).reshape(count, heads * WIDE)
    top1, low1, top2, low2, sums3 = hbm_call(
        functools.partial(fourth_kernel, heads),
        [piece] * 4 + [sums],
        2 * attend_flops,
        size,
        scalars=[length, slot],
        picked=2,
    )(qkv3, qkv1, cache, sums0, sums1, sums2, qkv2, out_gain, out_weight)
    one_x = across(top1, 1)
    one_y = across(low2, 2)
    two_y, two_x = hbm_call(add_kernel, [piece, piece], 0, size, here=(1, 3), near=(0, 1), waits=[top1])(top2, via_x, low1, via_y)
    top0, low0, state_next = hbm_call(
        functools.partial(fifth_kernel, heads),
        [piece] * 2 + [shape(1, PHI, heads, DH, dtype=F32)],
        attend_flops,
        size,
        scalars=[length, slot],
        picked=0,
        waits=[two_x],
    )(cache, sums0, sums1, sums2, sums3, queries0, own0, out_gain, out_weight)
    decoded = hbm_call(
        functools.partial(return_kernel, heads, capacity),
        [shape(TILE, D)] * 4,
        2 * DEC * heads * WIDE * D,
        2 * heads * WIDE * D,
        loose=(0, 3, 4),
        waits=[top0],
        raw=(3, 4),
    )(returned, owner_row, out_weight, one_x, one_y)
    shares = [decoded[0]] + [across(decoded[by], by) for by in (1, 2, 3)]
    two_y = across(two_y, 2)
    two_x = across(two_x, 1)
    state_next = jnp.transpose(state_next, (0, 2, 3, 1))
    stretch_out, decode_out = hbm_call(
        total_kernel,
        [shape(2, half, D), shape(1, DEC // 4, D)],
        0,
        8 * rows * D,
        loose=(1, 2, 4, 5, 7, 8, 9),
        split_out=(0,),
    )(top0, one_x, two_y, low0, one_y, two_x, *shares)
    return (stretch_out.reshape(1, rows, D), decode_out, state_next)


def from_behind(array, axis, by):
    peers = lax.axis_size(axis)
    pairs = [(i, i + by) for i in range(peers) if 0 <= i + by < peers]
    return lax.ppermute(array, axis, pairs)


def rms_rows(values, gain):
    values = values.astype(jnp.float32)
    factor = lax.rsqrt(jnp.mean(values * values, axis=-1, keepdims=True) + 1e-05)
    return values * factor * gain


def features(vectors):
    breadth = vectors.shape[-1]
    linear = vectors / math.sqrt(math.sqrt(breadth))
    outer = vectors[..., :, None] * vectors[..., None, :] / math.sqrt(2.0 * breadth)
    outer = outer.reshape(vectors.shape[:-1] + (breadth * breadth,))
    ones = jnp.ones(vectors.shape[:-1] + (1,), vectors.dtype)
    return jnp.concatenate([ones, linear, outer], axis=-1)


def convolve(tail, normed, conv_taps):
    joined = jnp.concatenate([tail, normed], axis=-2).astype(jnp.float32)
    span_rows = normed.shape[-2]
    total = conv_taps[0] * joined[..., 0:span_rows, :]
    total = total + conv_taps[1] * joined[..., 1 : span_rows + 1, :]
    total = total + conv_taps[2] * joined[..., 2 : span_rows + 2, :]
    return total.astype(jnp.bfloat16)


def decode_items(items, slot_items, cache_own, out_gain, head_count):
    item_count = items.shape[0]
    shaped = items.reshape(item_count, head_count, 2 * F + DH).astype(jnp.float32)
    queries = shaped[:, :, :F]
    key_feats = shaped[:, :, F : 2 * F]
    values = shaped[:, :, 2 * F :]
    slot_total = cache_own.shape[0]
    table = jnp.einsum(
        "nhp,shdp->nshd", features(queries), cache_own, precision=lax.Precision.HIGHEST
    )
    picker = (slot_items[:, None] == jnp.arange(slot_total)[None, :]).astype(jnp.float32)
    carried = jnp.einsum("ns,nshd->nhd", picker, table, precision=lax.Precision.HIGHEST)
    inner = jnp.sum(queries * key_feats, axis=-1) / math.sqrt(F)
    own_term = (1.0 + inner + 0.5 * inner * inner)[..., None] * values
    attended = rms_rows(carried + own_term, out_gain.reshape(head_count, DH))
    return attended.astype(jnp.bfloat16).reshape(item_count, head_count * DH)


def local(
    stretch_tokens,
    stretch_tail,
    decode_tokens,
    decode_tail,
    norm_gain,
    conv_taps,
    qkv_weight,
    out_gain,
    out_weight,
    state_cache,
    stretch_len,
    stretch_slot,
    decode_slot,
    decode_owner,
):
    head_count = qkv_weight.shape[1]
    block_width = qkv_weight.shape[2]
    rows_own = stretch_tokens.shape[1]
    w_flat = qkv_weight.reshape(D, head_count * block_width)
    gains = out_gain.reshape(head_count, DH)
    normed = rms_rows(stretch_tokens[0], norm_gain).astype(jnp.bfloat16)
    rim_rows = from_behind(normed[rows_own - 2 :], "head", 1)
    first_dev = lax.axis_index("head") == 0
    rim_rows = jnp.where(first_dev, stretch_tail[0], rim_rows)
    conved = convolve(rim_rows, normed, conv_taps)
    grouped = jnp.dot(
        lax.all_gather(conved, "head", axis=0, tiled=True),
        w_flat,
        preferred_element_type=jnp.float32,
    ).astype(jnp.bfloat16)
    grouped = grouped.reshape(STRETCH, head_count, block_width)
    queries = grouped[:, :, :F]
    key_feats = grouped[:, :, F : 2 * F]
    values = grouped[:, :, 2 * F :]
    length = stretch_len[0]
    positions = jnp.arange(STRETCH)
    valid_rows = positions < length
    state_old = lax.dynamic_index_in_dim(state_cache[0], stretch_slot[0], 0, keepdims=False)
    carried = jnp.einsum(
        "ihp,hdp->ihd",
        features(queries.astype(jnp.float32)),
        state_old,
        precision=lax.Precision.HIGHEST,
    )
    block_rows = min(512, STRETCH)
    pieces = []
    for anchor in range(0, STRETCH, block_rows):
        finish = anchor + block_rows
        inner = jnp.einsum(
            "ihf,jhf->hij",
            queries[anchor:finish],
            key_feats[:finish],
            preferred_element_type=jnp.float32,
        ) / math.sqrt(F)
        weights = 1.0 + inner + 0.5 * inner * inner
        allowed = (positions[None, :finish] <= positions[anchor:finish, None]) & valid_rows[
            None, :finish
        ]
        weights = jnp.where(allowed[None], weights, 0.0).astype(jnp.bfloat16)
        pieces.append(
            jnp.einsum("hij,jhd->ihd", weights, values[:finish], preferred_element_type=jnp.float32)
        )
    local_sum = jnp.concatenate(pieces, axis=0)
    attended = rms_rows(carried + local_sum, gains)
    attended = (
        jnp.where(valid_rows[:, None, None], attended, 0.0)
        .astype(jnp.bfloat16)
        .reshape(STRETCH, head_count * DH)
    )
    key_phi = jnp.where(
        valid_rows[:, None, None], features(key_feats.astype(jnp.float32)), 0.0
    ).astype(jnp.bfloat16)
    state_next = state_old + jnp.einsum(
        "jhd,jhp->hdp", values, key_phi, preferred_element_type=jnp.float32
    )
    part_rows = attended
    stretch_out = lax.psum_scatter(
        jnp.dot(part_rows, out_weight, preferred_element_type=jnp.float32).astype(jnp.bfloat16),
        "head",
        scatter_dimension=0,
        tiled=True,
    )
    dec_normed = rms_rows(decode_tokens[0], norm_gain).astype(jnp.bfloat16)
    dec_conved = convolve(decode_tail[0], dec_normed[:, None, :], conv_taps)[:, 0, :]
    dec_qkv = jnp.dot(dec_conved, w_flat, preferred_element_type=jnp.float32).astype(jnp.bfloat16)
    owners = decode_owner[0, :, 0]
    slots_here = decode_slot[0]
    groups = lax.axis_size("tok")
    capacity = max(2, 2 * DEC // groups)
    earlier = jnp.arange(DEC)[None, :] < jnp.arange(DEC)[:, None]
    same_owner = owners[None, :] == owners[:, None]
    rank_in = jnp.sum(earlier & same_owner, axis=1)
    target = owners * capacity + rank_in
    placing = jnp.arange(groups * capacity)[:, None] == target[None, :]
    sent_rows = jnp.dot(
        placing.astype(jnp.bfloat16), dec_qkv, preferred_element_type=jnp.float32
    ).astype(jnp.bfloat16)
    sent_rows = sent_rows.reshape(groups, capacity, head_count * block_width)
    sent_slots = jnp.sum(jnp.where(placing, slots_here[None, :] + 1, 0), axis=1) - 1
    sent_slots = sent_slots.reshape(groups, capacity)
    item_rows = lax.all_to_all(sent_rows, "tok", split_axis=0, concat_axis=0, tiled=True)
    item_slots = lax.all_to_all(sent_slots, "tok", split_axis=0, concat_axis=0, tiled=True)
    item_count = item_rows.shape[1]
    flat_out = decode_items(
        item_rows.reshape(groups * item_count, head_count * block_width),
        item_slots.reshape(groups * item_count),
        state_cache[0],
        out_gain,
        head_count,
    )
    served = flat_out.reshape(groups, item_count, head_count * DH)
    returned = lax.all_to_all(served, "tok", split_axis=0, concat_axis=0, tiled=True)
    dec_attended = jnp.dot(
        jnp.transpose(placing).astype(jnp.bfloat16),
        returned.reshape(groups * capacity, head_count * DH),
        preferred_element_type=jnp.float32,
    ).astype(jnp.bfloat16)
    part_rows = dec_attended
    decode_out = lax.psum_scatter(
        jnp.dot(part_rows, out_weight, preferred_element_type=jnp.float32).astype(jnp.bfloat16),
        "head",
        scatter_dimension=0,
        tiled=True,
    )
    return (stretch_out[None], decode_out[None], state_next[None])


def solution(mesh):
    in_specs = (
        P("tok", "head", None),
        P("tok", None, None),
        P("tok", None, None),
        P("tok", None, None, None),
        P(),
        P(),
        P(None, "head", None),
        P("head"),
        P("head", None),
        P("tok", None, "head", None, None),
        P("tok"),
        P("tok"),
        P("tok", None),
        P("tok", None, None),
    )
    out_specs = (P("tok", "head", None), P("tok", "head", None), P("tok", "head", None, None))
    chosen = local_square if mesh.shape["head"] == 4 else local
    return jax.shard_map(chosen, mesh=mesh, in_specs=in_specs, out_specs=out_specs, check_vma=False)
```

```python
import functools
import math

import jax
import jax.numpy as jnp
import numpy as np
from jax import lax
from jax.experimental import pallas as pl
from jax.experimental.pallas import tpu as pltpu
from jax.sharding import PartitionSpec as P

D = 1792
DH = 112
F = 16
STRETCH = 1024
DEC = 32
QUAD = F * F
PHI = 1 + F + QUAD
WIDE = 128
PHI_WIDE = QUAD + 128
TILE = 16
MIB = 1 << 20
BF = jnp.bfloat16
F32 = jnp.float32


def lanes_of(size):
    return lax.broadcasted_iota(jnp.int32, (F, size), 1), lax.broadcasted_iota(jnp.int32, (F, size), 0)


def ones_where(mask):
    return jnp.where(mask, 1.0, 0.0).astype(BF)


def spreader():
    lane, entry = lanes_of(PHI_WIDE)
    return ones_where(jnp.where(lane < QUAD, lane >> 4, lane & (F - 1)) == entry)


def dot(left, right, contract=((1,), (0,))):
    return lax.dot_general(left, right, (contract, ((), ())), preferred_element_type=F32)


def phi_of(vectors, pick):
    spread = dot(vectors, pick)
    a, b = spread[:, :QUAD], spread[:, QUAD:]
    quad = a * jnp.concatenate([b] * (QUAD // 128), axis=1) * (1.0 / math.sqrt(2.0 * F))
    lane = lax.broadcasted_iota(jnp.int32, b.shape, 1)
    rest = jnp.where(lane < F, b * (1.0 / math.sqrt(math.sqrt(F))), jnp.where(lane == F, 1.0, 0.0))
    return jnp.concatenate([quad, rest], axis=1)


def unit_rows(values):
    values = values.astype(F32)
    total = jnp.sum(values * values, axis=-1, keepdims=True)
    return values, lax.rsqrt(total * (1.0 / D) + 1e-05)


def column(row):
    size = row.shape[1]
    same = lax.broadcasted_iota(jnp.int32, (size, size), 0) == lax.broadcasted_iota(jnp.int32, (size, size), 1)
    return jnp.sum(jnp.where(same, row, 0), axis=1, keepdims=True)


def projection(w_ref, heads):
    pieces = [w_ref[h, :F, :] for h in range(heads)] + [w_ref[h, F : 2 * F, :] for h in range(heads)]
    for h in range(heads):
        pieces += [w_ref[h, 2 * F :, :], jnp.zeros((WIDE - DH, D), w_ref.dtype)]
    return jnp.concatenate(pieces, axis=0)


def out_projection(w_ref, heads):
    pieces = []
    for h in range(heads):
        pieces += [w_ref[h * DH : (h + 1) * DH, :], jnp.zeros((WIDE - DH, D), w_ref.dtype)]
    return jnp.concatenate(pieces, axis=0)


def conv_kernel(tokens_ref, tail_ref, gain_ref, taps_ref, low, top, begin, end):
    rows = tokens_ref.shape[0]
    half = rows // 2
    gain = gain_ref[...].reshape(1, D)
    taps = taps_ref[...]
    _, factor = unit_rows(tokens_ref[...])
    step = 256
    row = lax.broadcasted_iota(jnp.int32, (rows, step), 0)
    for at in range(0, D, step):
        cols = slice(at, at + step)
        normed = tokens_ref[:, cols].astype(F32) * factor * gain[:, cols]
        normed = normed.astype(BF)
        begin[:, cols] = normed[:16]
        end[:, cols] = normed[rows - 16 :]
        normed = normed.astype(F32)
        tail = tail_ref[:, cols].astype(F32)
        one = jnp.where(row == 0, tail[1:2], pltpu.roll(normed, 1, 0))
        two = pltpu.roll(normed, 2, 0)
        two = jnp.where(row == 0, tail[0:1], jnp.where(row == 1, tail[1:2], two))
        total = taps[0:1, cols] * two + taps[1:2, cols] * one + taps[2:3, cols] * normed
        total = total.astype(BF)
        top[:, cols] = total[:half]
        low[:, cols] = total[half:]


def rim_kernel(first_ref, top_ref, begin_ref, end_ref, taps_ref, out_ref, begin, end, taps, rows, sem):
    copies = [
        pltpu.make_async_copy(src, place, sem.at[n])
        for n, (src, place) in enumerate([(begin_ref, begin), (end_ref, end), (taps_ref, taps)])
    ]
    for copy in copies:
        copy.start()
    for copy in copies:
        copy.wait()
    now = begin[...].astype(F32)
    last = end[...].astype(F32)
    row = lax.broadcasted_iota(jnp.int32, now.shape, 0)
    one = jnp.where(row == 0, last[15:16], pltpu.roll(now, 1, 0))
    two = jnp.where(row == 0, last[14:15], jnp.where(row == 1, last[15:16], pltpu.roll(now, 2, 0)))
    rows[...] = (taps[0:1, :] * two + taps[1:2, :] * one + taps[2:3, :] * now).astype(BF)

    @pl.when(first_ref[0] != 0)
    def _():
        back = pltpu.make_async_copy(rows, out_ref.at[:16], sem.at[3])
        back.start()
        back.wait()


def qkv_of(heads, top, low, w_ref):
    conved = jnp.concatenate([top[...], low[...]], axis=0)
    return dot(conved, projection(w_ref, heads), ((1,), (1,))).astype(BF)


def parts_of(qkv, heads, head):
    at = 2 * heads * F + head * WIDE
    return qkv[:, head * F : (head + 1) * F], qkv[:, (heads + head) * F : (heads + head + 1) * F], qkv[:, at : at + WIDE]


def sums_of(slot, heads, head, length, qkv, pick):
    _, k, v = parts_of(qkv, heads, head)
    live = length - v.shape[0] * (lax.axis_index("head") ^ slot)
    live_row = lax.broadcasted_iota(jnp.int32, v.shape, 0) < live
    v = jnp.where(live_row, v.astype(F32), 0.0).astype(BF)
    return dot(phi_of(k, pick).astype(BF), v, ((0,), (0,)))


def own_of(slot, heads, head, length, qkv):
    q, k, v = parts_of(qkv, heads, head)
    rows = v.shape[0]
    live = length - rows * (lax.axis_index("head") ^ slot)
    row = lax.broadcasted_iota(jnp.int32, (rows, rows), 0)
    col = lax.broadcasted_iota(jnp.int32, (rows, rows), 1)
    shifted = dot(q, k, ((1,), (1,))) * (1.0 / math.sqrt(F)) + 1.0
    weights = jnp.where((col <= row) & (col < live), 0.5 * shifted * shifted + 0.5, 0.0).astype(BF)
    return dot(weights, v)


def old_state(cache_ref, head):
    pad = jnp.zeros((PHI_WIDE - PHI, DH), F32)
    old = [cache_ref[F + 1 :, head, :], cache_ref[1 : F + 1, head, :], cache_ref[0:1, head, :], pad]
    return jnp.concatenate([jnp.concatenate(old, axis=0), jnp.zeros((PHI_WIDE, WIDE - DH), F32)], axis=1)


def attend_part(slot, head, heads, length, q, own, state, gain_ref, pick):
    rows = q.shape[0]
    total = own + dot(phi_of(q, pick).astype(BF), state)
    square = jnp.sum(total * total, axis=-1, keepdims=True)
    gain = gain_ref[...].reshape(1, heads * DH)[:, head * DH : (head + 1) * DH]
    gain = jnp.concatenate([gain, jnp.zeros((1, WIDE - DH), F32)], axis=1)
    total = total * lax.rsqrt(square * (1.0 / DH) + 1e-05) * gain
    live = length - rows * (lax.axis_index("head") ^ slot)
    live_row = lax.broadcasted_iota(jnp.int32, (rows, WIDE), 0) < live
    return jnp.where(live_row, total, 0.0).astype(BF)


def project_part(parts, heads, w_ref, top, low):
    attended = jnp.concatenate(parts, axis=1)
    half = low.shape[0]
    w_out = out_projection(w_ref, heads)
    for out, rows in ((top, attended[:half]), (low, attended[half:])):
        out[...] = dot(rows, w_out).astype(BF)
        out.push()


def first_kernel(heads, len_ref, low, top, w_ref, sums, own, queries):
    qkv = qkv_of(heads, top, low, w_ref)
    pick = spreader()
    for head in range(heads):
        sums[head] = sums_of(0, heads, head, len_ref[0], qkv, pick)
    sums.push()
    for head in range(heads):
        own[head] = own_of(0, heads, head, len_ref[0], qkv)
    queries[...] = qkv[:, : heads * F]


def second_kernel(
    heads, len_ref, low1, top1, w_ref, low2, top2, cache, sums0, items, half_total, gain_ref, cache_ref,
    sums1, qkv1, sums2, qkv2, state3, served, state, sem
):
    start = 2 * sem.shape[0]
    copies = slot_copies(heads, start, start, cache_ref, state, sem)
    pick = spreader()
    for slot, low, top, sums, qkv in ((1, low1, top1, sums1, qkv1), (2, low2, top2, sums2, qkv2)):
        found = qkv_of(heads, top, low, w_ref)
        if slot == 1:
            for copy in copies:
                copy.start()
        qkv[...] = found
        qkv.push()
        for head in range(heads):
            sums[head] = sums_of(slot, heads, head, len_ref[0], found, pick)
        sums.push()
    for head in range(heads):
        state3[head] = state_before(3, old_state(cache, head), (sums0[head], sums1[head], sums2[head]))
    state3.push()
    serve_part(heads, start, items, half_total, gain_ref, copies, state, served)


def state_before(slot, old, sums):
    mine = lax.axis_index("head")
    for other, part in enumerate(sums):
        if other != slot:
            old = old + ((mine ^ other) < (mine ^ slot)).astype(F32) * part
    return old.astype(BF)


def third_kernel(heads, len_ref, low, top, w_ref, state3, gain_ref, out_w_ref, top3, low3, qkv3):
    length = len_ref[0]
    qkv = qkv_of(heads, top, low, w_ref)
    qkv3[...] = qkv
    qkv3.push()
    pick = spreader()
    parts = []
    for head in range(heads):
        q = parts_of(qkv, heads, head)[0]
        own = own_of(3, heads, head, length, qkv)
        parts.append(attend_part(3, head, heads, length, q, own, state3[head], gain_ref, pick))
    project_part(parts, heads, out_w_ref, top3, low3)


def fourth_kernel(
    heads, len_ref, qkv3, qkv1, cache, sums0, sums1, sums2, qkv2, gain_ref, out_w_ref, top1, low1, top2, low2, sums3
):
    pick = spreader()
    length = len_ref[0]
    for head in range(heads):
        sums3[head] = sums_of(3, heads, head, length, qkv3, pick)
    sums3.push()
    for slot, qkv, top, low in ((1, qkv1, top1, low1), (2, qkv2, top2, low2)):
        parts = []
        for head in range(heads):
            q = parts_of(qkv, heads, head)[0]
            own = own_of(slot, heads, head, length, qkv)
            state = state_before(slot, old_state(cache, head), (sums0[head], sums1[head], sums2[head], sums3[head]))
            parts.append(attend_part(slot, head, heads, length, q, own, state, gain_ref, pick))
        project_part(parts, heads, out_w_ref, top, low)


def fifth_kernel(
    heads, len_ref, cache, sums0, sums1, sums2, sums3, queries, own, gain_ref, out_w_ref, top0, low0, state_next
):
    pick = spreader()
    parts = []
    for head in range(heads):
        old = old_state(cache, head)
        sums = [part[head] for part in (sums0, sums1, sums2, sums3)]
        q = queries[:, head * F : (head + 1) * F]
        state = state_before(0, old, sums)
        parts.append(attend_part(0, head, heads, len_ref[0], q, own[head], state, gain_ref, pick))
        new = (old + (sums[0] + sums[1]) + (sums[2] + sums[3]))[:, :DH]
        state_next[0, F + 1 :, head, :] = new[:QUAD]
        state_next[0, 1 : F + 1, head, :] = new[QUAD : QUAD + F]
        state_next[0, 0:1, head, :] = new[QUAD + F : QUAD + F + 1]
    project_part(parts, heads, out_w_ref, top0, low0)


def add_kernel(top2, via_x, low1, via_y, two_y, two_x):
    two_y[...] = (top2[...].astype(F32) + via_x[...].astype(F32)).astype(BF)
    two_x[...] = (low1[...].astype(F32) + via_y[...].astype(F32)).astype(BF)


def total_kernel(top0, one_x, two_y, low0, one_y, two_x, dec0, dec1, dec2, dec3, out, decode_out):
    out[0] = (top0[...].astype(F32) + one_x[...].astype(F32) + two_y[...].astype(F32)).astype(BF)
    out.push(0)
    out[1] = (low0[...].astype(F32) + one_y[...].astype(F32) + two_x[...].astype(F32)).astype(BF)
    out.push(1)
    total = (dec0[...].astype(F32) + dec1[...].astype(F32)) + (dec2[...].astype(F32) + dec3[...].astype(F32))
    decode_out[0] = total[: DEC // 4].astype(BF)


def placing_rank(owners_row, axis):
    down = lax.broadcasted_iota(jnp.int32, (DEC, DEC), 0)
    along = lax.broadcasted_iota(jnp.int32, (DEC, DEC), 1)
    earlier = down < along if axis == 0 else along < down
    return jnp.sum(jnp.where(earlier & (column(owners_row) == owners_row), 1, 0), axis=axis, keepdims=True)


def send_kernel(heads, capacity, tokens_ref, tail_ref, gain_ref, taps_ref, owner_ref, slot_ref, w_ref, out):
    tokens, factor = unit_rows(tokens_ref[...])
    normed = (tokens * factor * gain_ref[...].reshape(1, D)).astype(BF).astype(F32)
    tail = tail_ref[...].astype(F32)
    taps = taps_ref[...]
    conved = taps[0:1, :] * tail[:, 0, :] + taps[1:2, :] * tail[:, 1, :]
    conved = (conved + taps[2:3, :] * normed).astype(BF)
    owners = owner_ref[...]
    target = owners * capacity + placing_rank(owners, 0)
    placing = lax.broadcasted_iota(jnp.int32, (out.shape[0], DEC), 0) == target
    cache_slot = jnp.sum(jnp.where(placing, slot_ref[...] + 1, 0), axis=1, keepdims=True) - 1
    qkv = dot(conved, projection(w_ref, heads), ((1,), (1,))).astype(BF)
    sent = dot(ones_where(placing), qkv)
    lane = lax.broadcasted_iota(jnp.int32, sent.shape, 1)
    mark = 2 * heads * F + DH
    out[...] = jnp.where(lane == mark, cache_slot.astype(F32), sent).astype(BF)


def cache_spreaders(heads):
    lane, entry = lanes_of(PHI * heads)
    feature = lane >> (heads.bit_length() - 1)
    quad = feature - (1 + F)
    a = jnp.where(quad < 0, feature - 1, quad >> 4)
    return ones_where(a == entry), ones_where((quad >= 0) & ((quad & (F - 1)) == entry))


def slot_features(heads, items):
    mark = 2 * heads * F + DH
    first, second = cache_spreaders(heads)
    phis = []
    for head in range(heads):
        q = items[:, head * F : head * F + F]
        a = dot(q, first)
        b = dot(q, second)
        lane = lax.broadcasted_iota(jnp.int32, a.shape, 1)
        scale = jnp.where(lane < heads * (F + 1), 1.0 / math.sqrt(math.sqrt(F)), b * (1.0 / math.sqrt(2.0 * F)))
        value = jnp.where(lane < heads, 1.0, a * scale)
        phis.append(jnp.where((lane & (heads - 1)) == head, value, 0.0).astype(BF))
    slots = jnp.concatenate([items[:, mark : mark + 1].astype(F32)] * heads, axis=0)
    return jnp.concatenate(phis, axis=0), slots


def slot_copies(heads, start, count, cache_ref, state, sem):
    size = 2 * PHI * heads
    return [
        pltpu.make_async_copy(cache_ref.at[pl.ds(start * size // 2 + n * size, size)], state.at[pl.ds(n * size, size)], sem.at[n])
        for n in range(count // 2)
    ]


def slot_totals(heads, start, phis, slots, copies, state, total):
    span = PHI * heads
    waiting = list(copies)
    done = {}
    for n in range(2 * len(copies)):
        if n % 2 == 0:
            waiting.pop(0).wait()
        shift = n * span % 8
        rows = -(-(span + shift) // 8) * 8
        block = state[n * span - shift : n * span - shift + rows, :].astype(BF)
        done.setdefault(shift, []).append((n, block))
        if len(done[shift]) == 2:
            zeros = jnp.zeros((rows, WIDE - DH), BF)
            pair = [part for _, block in done[shift] for part in (block, zeros)]
            sides = [jnp.zeros((phis.shape[0], size), BF) for size in (shift, rows - span - shift)]
            wide = [side for side in (sides[0], phis, sides[1]) if side.shape[1] > 0]
            table = dot(jnp.concatenate(wide, axis=1), jnp.concatenate(pair, axis=1))
            for side, (place, _) in enumerate(done.pop(shift)):
                here = slots == float(start + place)
                total = total + jnp.where(here, table[:, side * WIDE : (side + 1) * WIDE], 0.0)
    return total


def serve_kernel(heads, items, cache_ref, total, state, sem):
    copies = slot_copies(heads, 0, 2 * sem.shape[0], cache_ref, state, sem)
    for copy in copies:
        copy.start()
    phis, slots = slot_features(heads, items)
    total[...] = slot_totals(heads, 0, phis, slots, copies, state, jnp.zeros(total.shape, F32))


def serve_part(heads, start, items, half_total, gain_ref, copies, state, out):
    count = items.shape[0]
    phis, slots = slot_features(heads, items)
    total = slot_totals(heads, start, phis, slots, copies, state, half_total[...])
    gains = gain_ref[...].reshape(1, heads * DH)
    for head in range(heads):
        q = items[:, head * F : head * F + F].astype(F32)
        k = items[:, (heads + head) * F : (heads + head) * F + F].astype(F32)
        at = 2 * heads * F + head * WIDE
        v = items[:, at : at + DH].astype(F32)
        inner = jnp.sum(q * k, axis=-1, keepdims=True) * (1.0 / math.sqrt(F))
        value = total[head * count : (head + 1) * count, :DH] + (1.0 + inner + 0.5 * inner * inner) * v
        square = jnp.sum(value * value, axis=-1, keepdims=True)
        value = value * lax.rsqrt(square * (1.0 / DH) + 1e-05) * gains[:, head * DH : (head + 1) * DH]
        out[:, head * WIDE : head * WIDE + DH] = value.astype(BF)
        out[:, head * WIDE + DH : (head + 1) * WIDE] = jnp.zeros((count, WIDE - DH), BF)


def return_kernel(heads, capacity, items_ref, owner_ref, w_ref, seen_x, seen_y, *outs):
    owners = owner_ref[...]
    target = column(owners) * capacity + placing_rank(owners, 1)
    placing = lax.broadcasted_iota(jnp.int32, (DEC, items_ref.shape[0]), 1) == target
    attended = dot(ones_where(placing), items_ref[...]).astype(BF)
    row = lax.broadcasted_iota(jnp.int32, (4 * TILE, DEC), 0)
    entry = lax.broadcasted_iota(jnp.int32, (4 * TILE, DEC), 1)
    device = lax.axis_index("head") ^ (row // TILE)
    wanted = ((row % TILE) < DEC // 4) & (entry == device * (DEC // 4) + row % TILE)
    attended = dot(ones_where(wanted), attended).astype(BF)
    shares = dot(attended, out_projection(w_ref, heads)).astype(BF)
    for slot, out in enumerate(outs):
        out[...] = shares[slot * TILE : (slot + 1) * TILE]


def far_off(array):
    return pltpu.with_memory_space_constraint(array, pltpu.HBM)


def entries(ref):
    return [ref.at[n] for n in range(ref.shape[0])]


class Fetched:
    def __init__(self, copies, place):
        self.copies, self.place, self.here = copies, place, set()
        self.shape, self.dtype = place.shape, place.dtype

    def __getitem__(self, index):
        entry = index[0] if isinstance(index, tuple) else index
        wanted = [entry] if len(self.copies) > 1 and isinstance(entry, int) else range(len(self.copies))
        for n in wanted:
            self.wait(n)
        return self.place[index]

    def wait(self, n):
        if n not in self.here:
            self.copies[n].wait()
            self.here.add(n)


class Pushed:
    def __init__(self, copies, place):
        self.copies, self.place, self.gone = copies, place, set()
        self.shape, self.dtype = place.shape, place.dtype

    def __getitem__(self, index):
        return self.place[index]

    def __setitem__(self, index, value):
        self.place[index] = value

    def push(self, entry=None):
        if (entry is None) == (len(self.copies) == 1):
            self.send(entry or 0)

    def send(self, n):
        if n not in self.gone:
            self.copies[n].start()
            self.gone.add(n)


class Near:
    def __init__(self, ref):
        self.ref, self.shape, self.dtype, self.copies = ref, ref.shape, ref.dtype, []

    def __getitem__(self, index):
        return self.ref[index]

    def __setitem__(self, index, value):
        self.ref[index] = value

    def push(self, entry=None):
        pass


def hbm_call(kernel, outs, flops, size, scalars=(), picked=None, waits=(), loose=(), here=(), near=(), split=(), split_out=(), raw=(), scratch=()):
    def run(*args):
        count, many = len(args), len(outs)
        moved = [n for n in range(count) if n not in here and n not in raw]
        far = [n for n in range(many) if n not in near]

        def shape_in(n):
            return args[n].shape[2:] if n == picked else args[n].shape

        pieces = sum(shape_in(n)[0] if n in split else 1 for n in moved)
        pieces += sum(outs[n].shape[0] if n in split_out else 1 for n in far)

        def body(*refs):
            refs = list(refs)

            def take(number):
                taken = refs[:number]
                del refs[:number]
                return taken

            numbers, sources, _, targets = take(len(scalars)), take(count), take(len(waits)), take(many)
            places, results, own, (sem,) = dict(zip(moved, take(len(moved)))), dict(zip(far, take(len(far)))), take(len(scratch)), refs
            used = iter(range(pieces))

            def copies(source, target, apart):
                pairs = zip(entries(source), entries(target)) if apart else [(source, target)]
                return [pltpu.make_async_copy(a, b, sem.at[next(used)]) for a, b in pairs]

            ins = []
            for n, source in enumerate(sources):
                if n in here or n in raw:
                    ins.append(source)
                    continue
                if n == picked:
                    source = source.at[0, numbers[-1][0]]
                fetched = Fetched(copies(source, places[n], n in split), places[n])
                for copy in fetched.copies:
                    copy.start()
                ins.append(fetched)
            done = [
                Pushed(copies(results[n], target, n in split_out), results[n]) if n in far else Near(target)
                for n, target in enumerate(targets)
            ]
            kernel(*numbers[: len(scalars) - (picked is not None)], *ins, *done, *own)
            for n in far:
                for entry in range(len(done[n].copies)):
                    done[n].send(entry)
            for n in moved:
                for entry in range(len(ins[n].copies)):
                    ins[n].wait(entry)
            for n in far:
                for copy in done[n].copies:
                    copy.wait()

        hbm = pl.BlockSpec(memory_space=pltpu.HBM)
        in_vmem = pl.BlockSpec(memory_space=pltpu.VMEM)
        anywhere = pl.BlockSpec(memory_space=pl.ANY)
        free = set(loose) | set(here)
        return pl.pallas_call(
            body,
            out_shape=[o if n in near else pltpu.HBM(o.shape, o.dtype) for n, o in enumerate(outs)],
            in_specs=[pl.BlockSpec(memory_space=pltpu.SMEM)] * len(scalars)
            + [in_vmem if n in here else anywhere if n in loose else hbm for n in range(count)]
            + [hbm] * len(waits),
            out_specs=[in_vmem if n in near else hbm for n in range(many)],
            scratch_shapes=[pltpu.VMEM(shape_in(n), args[n].dtype) for n in moved]
            + [pltpu.VMEM(outs[n].shape, outs[n].dtype) for n in far]
            + list(scratch)
            + [pltpu.SemaphoreType.DMA((pieces,))],
            compiler_params=pltpu.CompilerParams(vmem_limit_bytes=40 * MIB),
            cost_estimate=pl.CostEstimate(flops=flops, bytes_accessed=size, transcendentals=0),
        )(*scalars, *[a if n in free else far_off(a) for n, a in enumerate(args)], *map(far_off, waits))

    return run


def shape(*dims, dtype=BF):
    return jax.ShapeDtypeStruct(dims, dtype)


def across(array, by):
    return lax.ppermute(array, "head", [(i, i ^ by) for i in range(4)])


def local_square(
    stretch_tokens,
    stretch_tail,
    decode_tokens,
    decode_tail,
    norm_gain,
    conv_taps,
    qkv_weight,
    out_gain,
    out_weight,
    state_cache,
    stretch_len,
    stretch_slot,
    decode_slot,
    decode_owner,
):
    heads = qkv_weight.shape[1]
    rows = stretch_tokens.shape[1]
    half = rows // 2
    wide = heads * (2 * F + WIDE)
    w_in = jnp.transpose(qkv_weight, (1, 2, 0))
    cache = jnp.transpose(state_cache, (0, 1, 4, 2, 3))
    length = stretch_len.astype(jnp.int32)
    slot = stretch_slot.astype(jnp.int32)
    hbm = pl.BlockSpec(memory_space=pltpu.HBM)
    piece = shape(half, D)
    block_flops = 2 * rows * D * wide + 6 * heads * rows * rows * WIDE
    attend_flops = 2 * rows * heads * WIDE * (D + PHI_WIDE)
    size = 4 * rows * D

    low, top, begin, end = hbm_call(conv_kernel, [piece, piece, shape(TILE, D), shape(TILE, D)], 20 * rows * D, size)(
        stretch_tokens[0], stretch_tail[0], norm_gain, conv_taps
    )
    low_x = across(low, 1)
    low_y = across(low, 2)
    end = from_behind(end, "head", 1)

    groups = lax.axis_size("tok")
    capacity = max(2, 2 * DEC // groups)
    count = groups * capacity
    owner_row = decode_owner.reshape(1, DEC)
    (sent,) = hbm_call(functools.partial(send_kernel, heads, capacity), [shape(count, wide)], 2 * DEC * D * wide, 2 * D * wide)(
        decode_tokens[0], decode_tail[0], norm_gain, conv_taps, owner_row, decode_slot, w_in
    )
    top = pl.pallas_call(
        lambda first_ref, top_ref, begin_ref, end_ref, taps_ref, wait_ref, *refs: rim_kernel(
            first_ref, top_ref, begin_ref, end_ref, taps_ref, *refs
        ),
        out_shape=pltpu.HBM((half, D), BF),
        in_specs=[pl.BlockSpec(memory_space=pltpu.SMEM), hbm, hbm, pl.BlockSpec(memory_space=pl.ANY), hbm, hbm],
        out_specs=hbm,
        scratch_shapes=[pltpu.VMEM((TILE, D), BF), pltpu.VMEM((TILE, D), BF), pltpu.VMEM((3, D), F32), pltpu.VMEM((TILE, D), BF)]
        + [pltpu.SemaphoreType.DMA((4,))],
        input_output_aliases={1: 0},
        compiler_params=pltpu.CompilerParams(vmem_limit_bytes=40 * MIB),
        cost_estimate=pl.CostEstimate(flops=16 * D, bytes_accessed=128 * D, transcendentals=0),
    )(lax.axis_index("head").reshape(1), far_off(top), far_off(begin), end, far_off(conv_taps), far_off(sent))
    top_x = across(top, 1)
    top_y = across(top, 2)
    items = lax.all_to_all(sent.reshape(groups, capacity, wide), "tok", split_axis=0, concat_axis=0, tiled=True)

    sums, own, queries = shape(heads, PHI_WIDE, WIDE, dtype=F32), shape(heads, rows, WIDE, dtype=F32), shape(rows, heads * F)
    sums0, own0, queries0 = hbm_call(
        functools.partial(first_kernel, heads),
        [sums, own, queries],
        block_flops,
        size,
        scalars=[length],
    )(low, top, w_in)
    items = items.reshape(count, wide)
    slots = cache.shape[1]
    flat = cache.reshape(slots * PHI * heads, DH)
    states = [pltpu.VMEM((slots // 2 * PHI * heads, DH), F32), pltpu.SemaphoreType.DMA((slots // 4,))]
    serve_flops = slots * heads * heads * DH * PHI * count
    (half_total,) = hbm_call(
        functools.partial(serve_kernel, heads),
        [shape(heads * count, WIDE, dtype=F32)],
        serve_flops,
        2 * slots * heads * WIDE * PHI,
        loose=(0,),
        raw=(1,),
        scratch=states,
        waits=[queries0],
    )(items, flat)
    low_y, top_x, low_x = lax.optimization_barrier((low_y, top_x, low_x, half_total))[:3]
    low_xy = across(low_y, 1)
    top_xy = across(top_x, 2)
    blocks = shape(rows, wide)
    sums1, qkv1, sums2, qkv2, state3, served = hbm_call(
        functools.partial(second_kernel, heads),
        [sums, blocks, sums, blocks, shape(heads, PHI_WIDE, WIDE), shape(count, heads * WIDE)],
        2 * block_flops + serve_flops,
        2 * slots * heads * WIDE * PHI,
        scalars=[length, slot],
        picked=5,
        loose=(0, 1, 3, 4, 7),
        raw=(10,),
        scratch=states,
    )(low_x, top_x, w_in, low_y, top_y, cache, sums0, items, half_total, out_gain, flat)
    top3, low3, qkv3 = hbm_call(
        functools.partial(third_kernel, heads),
        [piece, piece, blocks],
        block_flops + attend_flops,
        size,
        scalars=[length],
        loose=(0, 1),
        near=(0, 1),
        waits=[qkv2],
    )(low_xy, top_xy, w_in, state3, out_gain, out_weight)

    via_x = across(top3, 1)
    via_y = across(low3, 2)
    served = lax.optimization_barrier((served, top3))[0]
    returned = lax.all_to_all(
        served.reshape(groups, capacity, heads * WIDE), "tok", split_axis=0, concat_axis=0, tiled=True
    ).reshape(count, heads * WIDE)
    top1, low1, top2, low2, sums3 = hbm_call(
        functools.partial(fourth_kernel, heads),
        [piece] * 4 + [sums],
        2 * attend_flops,
        size,
        scalars=[length, slot],
        picked=2,
    )(qkv3, qkv1, cache, sums0, sums1, sums2, qkv2, out_gain, out_weight)
    one_x = across(top1, 1)
    one_y = across(low2, 2)
    two_y, two_x = hbm_call(add_kernel, [piece, piece], 0, size, here=(1, 3), near=(0, 1), waits=[top1])(top2, via_x, low1, via_y)
    top0, low0, state_next = hbm_call(
        functools.partial(fifth_kernel, heads),
        [piece] * 2 + [shape(1, PHI, heads, DH, dtype=F32)],
        attend_flops,
        size,
        scalars=[length, slot],
        picked=0,
        waits=[two_x],
    )(cache, sums0, sums1, sums2, sums3, queries0, own0, out_gain, out_weight)
    decoded = hbm_call(
        functools.partial(return_kernel, heads, capacity),
        [shape(TILE, D)] * 4,
        2 * DEC * heads * WIDE * D,
        2 * heads * WIDE * D,
        loose=(0, 3, 4),
        waits=[top0],
        raw=(3, 4),
    )(returned, owner_row, out_weight, one_x, one_y)
    shares = [decoded[0]] + [across(decoded[by], by) for by in (1, 2, 3)]
    two_y = across(two_y, 2)
    two_x = across(two_x, 1)
    state_next = jnp.transpose(state_next, (0, 2, 3, 1))
    stretch_out, decode_out = hbm_call(
        total_kernel,
        [shape(2, half, D), shape(1, DEC // 4, D)],
        0,
        8 * rows * D,
        loose=(1, 2, 4, 5, 7, 8, 9),
        split_out=(0,),
    )(top0, one_x, two_y, low0, one_y, two_x, *shares)
    return (stretch_out.reshape(1, rows, D), decode_out, state_next)


def from_behind(array, axis, by):
    peers = lax.axis_size(axis)
    pairs = [(i, i + by) for i in range(peers) if 0 <= i + by < peers]
    return lax.ppermute(array, axis, pairs)


def rms_rows(values, gain):
    values = values.astype(jnp.float32)
    factor = lax.rsqrt(jnp.mean(values * values, axis=-1, keepdims=True) + 1e-05)
    return values * factor * gain


def features(vectors):
    breadth = vectors.shape[-1]
    linear = vectors / math.sqrt(math.sqrt(breadth))
    outer = vectors[..., :, None] * vectors[..., None, :] / math.sqrt(2.0 * breadth)
    outer = outer.reshape(vectors.shape[:-1] + (breadth * breadth,))
    ones = jnp.ones(vectors.shape[:-1] + (1,), vectors.dtype)
    return jnp.concatenate([ones, linear, outer], axis=-1)


def convolve(tail, normed, conv_taps):
    joined = jnp.concatenate([tail, normed], axis=-2).astype(jnp.float32)
    span_rows = normed.shape[-2]
    total = conv_taps[0] * joined[..., 0:span_rows, :]
    total = total + conv_taps[1] * joined[..., 1 : span_rows + 1, :]
    total = total + conv_taps[2] * joined[..., 2 : span_rows + 2, :]
    return total.astype(jnp.bfloat16)


def decode_items(items, slot_items, cache_own, out_gain, head_count):
    item_count = items.shape[0]
    shaped = items.reshape(item_count, head_count, 2 * F + DH).astype(jnp.float32)
    queries = shaped[:, :, :F]
    key_feats = shaped[:, :, F : 2 * F]
    values = shaped[:, :, 2 * F :]
    slot_total = cache_own.shape[0]
    table = jnp.einsum(
        "nhp,shdp->nshd", features(queries), cache_own, precision=lax.Precision.HIGHEST
    )
    picker = (slot_items[:, None] == jnp.arange(slot_total)[None, :]).astype(jnp.float32)
    carried = jnp.einsum("ns,nshd->nhd", picker, table, precision=lax.Precision.HIGHEST)
    inner = jnp.sum(queries * key_feats, axis=-1) / math.sqrt(F)
    own_term = (1.0 + inner + 0.5 * inner * inner)[..., None] * values
    attended = rms_rows(carried + own_term, out_gain.reshape(head_count, DH))
    return attended.astype(jnp.bfloat16).reshape(item_count, head_count * DH)


def local(
    stretch_tokens,
    stretch_tail,
    decode_tokens,
    decode_tail,
    norm_gain,
    conv_taps,
    qkv_weight,
    out_gain,
    out_weight,
    state_cache,
    stretch_len,
    stretch_slot,
    decode_slot,
    decode_owner,
):
    head_count = qkv_weight.shape[1]
    block_width = qkv_weight.shape[2]
    rows_own = stretch_tokens.shape[1]
    w_flat = qkv_weight.reshape(D, head_count * block_width)
    gains = out_gain.reshape(head_count, DH)
    normed = rms_rows(stretch_tokens[0], norm_gain).astype(jnp.bfloat16)
    rim_rows = from_behind(normed[rows_own - 2 :], "head", 1)
    first_dev = lax.axis_index("head") == 0
    rim_rows = jnp.where(first_dev, stretch_tail[0], rim_rows)
    conved = convolve(rim_rows, normed, conv_taps)
    grouped = jnp.dot(
        lax.all_gather(conved, "head", axis=0, tiled=True),
        w_flat,
        preferred_element_type=jnp.float32,
    ).astype(jnp.bfloat16)
    grouped = grouped.reshape(STRETCH, head_count, block_width)
    queries = grouped[:, :, :F]
    key_feats = grouped[:, :, F : 2 * F]
    values = grouped[:, :, 2 * F :]
    length = stretch_len[0]
    positions = jnp.arange(STRETCH)
    valid_rows = positions < length
    state_old = lax.dynamic_index_in_dim(state_cache[0], stretch_slot[0], 0, keepdims=False)
    carried = jnp.einsum(
        "ihp,hdp->ihd",
        features(queries.astype(jnp.float32)),
        state_old,
        precision=lax.Precision.HIGHEST,
    )
    block_rows = min(512, STRETCH)
    pieces = []
    for anchor in range(0, STRETCH, block_rows):
        finish = anchor + block_rows
        inner = jnp.einsum(
            "ihf,jhf->hij",
            queries[anchor:finish],
            key_feats[:finish],
            preferred_element_type=jnp.float32,
        ) / math.sqrt(F)
        weights = 1.0 + inner + 0.5 * inner * inner
        allowed = (positions[None, :finish] <= positions[anchor:finish, None]) & valid_rows[
            None, :finish
        ]
        weights = jnp.where(allowed[None], weights, 0.0).astype(jnp.bfloat16)
        pieces.append(
            jnp.einsum("hij,jhd->ihd", weights, values[:finish], preferred_element_type=jnp.float32)
        )
    local_sum = jnp.concatenate(pieces, axis=0)
    attended = rms_rows(carried + local_sum, gains)
    attended = (
        jnp.where(valid_rows[:, None, None], attended, 0.0)
        .astype(jnp.bfloat16)
        .reshape(STRETCH, head_count * DH)
    )
    key_phi = jnp.where(
        valid_rows[:, None, None], features(key_feats.astype(jnp.float32)), 0.0
    ).astype(jnp.bfloat16)
    state_next = state_old + jnp.einsum(
        "jhd,jhp->hdp", values, key_phi, preferred_element_type=jnp.float32
    )
    part_rows = attended
    stretch_out = lax.psum_scatter(
        jnp.dot(part_rows, out_weight, preferred_element_type=jnp.float32).astype(jnp.bfloat16),
        "head",
        scatter_dimension=0,
        tiled=True,
    )
    dec_normed = rms_rows(decode_tokens[0], norm_gain).astype(jnp.bfloat16)
    dec_conved = convolve(decode_tail[0], dec_normed[:, None, :], conv_taps)[:, 0, :]
    dec_qkv = jnp.dot(dec_conved, w_flat, preferred_element_type=jnp.float32).astype(jnp.bfloat16)
    owners = decode_owner[0, :, 0]
    slots_here = decode_slot[0]
    groups = lax.axis_size("tok")
    capacity = max(2, 2 * DEC // groups)
    earlier = jnp.arange(DEC)[None, :] < jnp.arange(DEC)[:, None]
    same_owner = owners[None, :] == owners[:, None]
    rank_in = jnp.sum(earlier & same_owner, axis=1)
    target = owners * capacity + rank_in
    placing = jnp.arange(groups * capacity)[:, None] == target[None, :]
    sent_rows = jnp.dot(
        placing.astype(jnp.bfloat16), dec_qkv, preferred_element_type=jnp.float32
    ).astype(jnp.bfloat16)
    sent_rows = sent_rows.reshape(groups, capacity, head_count * block_width)
    sent_slots = jnp.sum(jnp.where(placing, slots_here[None, :] + 1, 0), axis=1) - 1
    sent_slots = sent_slots.reshape(groups, capacity)
    item_rows = lax.all_to_all(sent_rows, "tok", split_axis=0, concat_axis=0, tiled=True)
    item_slots = lax.all_to_all(sent_slots, "tok", split_axis=0, concat_axis=0, tiled=True)
    item_count = item_rows.shape[1]
    flat_out = decode_items(
        item_rows.reshape(groups * item_count, head_count * block_width),
        item_slots.reshape(groups * item_count),
        state_cache[0],
        out_gain,
        head_count,
    )
    served = flat_out.reshape(groups, item_count, head_count * DH)
    returned = lax.all_to_all(served, "tok", split_axis=0, concat_axis=0, tiled=True)
    dec_attended = jnp.dot(
        jnp.transpose(placing).astype(jnp.bfloat16),
        returned.reshape(groups * capacity, head_count * DH),
        preferred_element_type=jnp.float32,
    ).astype(jnp.bfloat16)
    part_rows = dec_attended
    decode_out = lax.psum_scatter(
        jnp.dot(part_rows, out_weight, preferred_element_type=jnp.float32).astype(jnp.bfloat16),
        "head",
        scatter_dimension=0,
        tiled=True,
    )
    return (stretch_out[None], decode_out[None], state_next[None])


def solution(mesh):
    in_specs = (
        P("tok", "head", None),
        P("tok", None, None),
        P("tok", None, None),
        P("tok", None, None, None),
        P(),
        P(),
        P(None, "head", None),
        P("head"),
        P("head", None),
        P("tok", None, "head", None, None),
        P("tok"),
        P("tok"),
        P("tok", None),
        P("tok", None, None),
    )
    out_specs = (P("tok", "head", None), P("tok", "head", None), P("tok", "head", None, None))
    chosen = local_square if mesh.shape["head"] == 4 else local
    return jax.shard_map(chosen, mesh=mesh, in_specs=in_specs, out_specs=out_specs, check_vma=False)
```

```python
import functools
import math

import jax
import jax.numpy as jnp
import numpy as np
from jax import lax
from jax.experimental import pallas as pl
from jax.experimental.pallas import tpu as pltpu
from jax.sharding import PartitionSpec as P

D = 1792
DH = 112
F = 16
STRETCH = 1024
DEC = 32
QUAD = F * F
PHI = 1 + F + QUAD
WIDE = 128
PHI_WIDE = QUAD + 128
TILE = 16
MIB = 1 << 20
BF = jnp.bfloat16
F32 = jnp.float32


def lanes_of(size):
    return lax.broadcasted_iota(jnp.int32, (F, size), 1), lax.broadcasted_iota(jnp.int32, (F, size), 0)


def ones_where(mask):
    return jnp.where(mask, 1.0, 0.0).astype(BF)


def spreader():
    lane, entry = lanes_of(PHI_WIDE)
    return ones_where(jnp.where(lane < QUAD, lane >> 4, lane & (F - 1)) == entry)


def dot(left, right, contract=((1,), (0,))):
    return lax.dot_general(left, right, (contract, ((), ())), preferred_element_type=F32)


def phi_of(vectors, pick):
    spread = dot(vectors, pick)
    a, b = spread[:, :QUAD], spread[:, QUAD:]
    quad = a * jnp.concatenate([b] * (QUAD // 128), axis=1) * (1.0 / math.sqrt(2.0 * F))
    lane = lax.broadcasted_iota(jnp.int32, b.shape, 1)
    rest = jnp.where(lane < F, b * (1.0 / math.sqrt(math.sqrt(F))), jnp.where(lane == F, 1.0, 0.0))
    return jnp.concatenate([quad, rest], axis=1)


def unit_rows(values):
    values = values.astype(F32)
    total = jnp.sum(values * values, axis=-1, keepdims=True)
    return values, lax.rsqrt(total * (1.0 / D) + 1e-05)


def column(row):
    size = row.shape[1]
    same = lax.broadcasted_iota(jnp.int32, (size, size), 0) == lax.broadcasted_iota(jnp.int32, (size, size), 1)
    return jnp.sum(jnp.where(same, row, 0), axis=1, keepdims=True)


def projection(w_ref, heads):
    pieces = [w_ref[h, :F, :] for h in range(heads)] + [w_ref[h, F : 2 * F, :] for h in range(heads)]
    for h in range(heads):
        pieces += [w_ref[h, 2 * F :, :], jnp.zeros((WIDE - DH, D), w_ref.dtype)]
    return jnp.concatenate(pieces, axis=0)


def out_projection(w_ref, heads):
    pieces = []
    for h in range(heads):
        pieces += [w_ref[h * DH : (h + 1) * DH, :], jnp.zeros((WIDE - DH, D), w_ref.dtype)]
    return jnp.concatenate(pieces, axis=0)


def conv_kernel(tokens_ref, tail_ref, gain_ref, taps_ref, low, top, begin, end):
    rows = tokens_ref.shape[0]
    half = rows // 2
    gain = gain_ref[...].reshape(1, D)
    taps = taps_ref[...]
    _, factor = unit_rows(tokens_ref[...])
    step = 256
    row = lax.broadcasted_iota(jnp.int32, (rows, step), 0)
    for at in range(0, D, step):
        cols = slice(at, at + step)
        normed = tokens_ref[:, cols].astype(F32) * factor * gain[:, cols]
        normed = normed.astype(BF)
        begin[:, cols] = normed[:16]
        end[:, cols] = normed[rows - 16 :]
        normed = normed.astype(F32)
        tail = tail_ref[:, cols].astype(F32)
        one = jnp.where(row == 0, tail[1:2], pltpu.roll(normed, 1, 0))
        two = pltpu.roll(normed, 2, 0)
        two = jnp.where(row == 0, tail[0:1], jnp.where(row == 1, tail[1:2], two))
        total = taps[0:1, cols] * two + taps[1:2, cols] * one + taps[2:3, cols] * normed
        total = total.astype(BF)
        top[:, cols] = total[:half]
        low[:, cols] = total[half:]


def rim_kernel(first_ref, top_ref, begin_ref, end_ref, taps_ref, out_ref, begin, end, taps, rows, sem):
    copies = [
        pltpu.make_async_copy(src, place, sem.at[n])
        for n, (src, place) in enumerate([(begin_ref, begin), (end_ref, end), (taps_ref, taps)])
    ]
    for copy in copies:
        copy.start()
    for copy in copies:
        copy.wait()
    now = begin[...].astype(F32)
    last = end[...].astype(F32)
    row = lax.broadcasted_iota(jnp.int32, now.shape, 0)
    one = jnp.where(row == 0, last[15:16], pltpu.roll(now, 1, 0))
    two = jnp.where(row == 0, last[14:15], jnp.where(row == 1, last[15:16], pltpu.roll(now, 2, 0)))
    rows[...] = (taps[0:1, :] * two + taps[1:2, :] * one + taps[2:3, :] * now).astype(BF)

    @pl.when(first_ref[0] != 0)
    def _():
        back = pltpu.make_async_copy(rows, out_ref.at[:16], sem.at[3])
        back.start()
        back.wait()


def qkv_of(heads, top, low, w_ref):
    conved = jnp.concatenate([top[...], low[...]], axis=0)
    return dot(conved, projection(w_ref, heads), ((1,), (1,))).astype(BF)


def parts_of(qkv, heads, head):
    at = 2 * heads * F + head * WIDE
    return qkv[:, head * F : (head + 1) * F], qkv[:, (heads + head) * F : (heads + head + 1) * F], qkv[:, at : at + WIDE]


def sums_of(slot, heads, head, length, qkv, pick):
    _, k, v = parts_of(qkv, heads, head)
    live = length - v.shape[0] * (lax.axis_index("head") ^ slot)
    live_row = lax.broadcasted_iota(jnp.int32, v.shape, 0) < live
    v = jnp.where(live_row, v.astype(F32), 0.0).astype(BF)
    return dot(phi_of(k, pick).astype(BF), v, ((0,), (0,)))


def own_of(slot, heads, head, length, qkv):
    q, k, v = parts_of(qkv, heads, head)
    rows = v.shape[0]
    live = length - rows * (lax.axis_index("head") ^ slot)
    row = lax.broadcasted_iota(jnp.int32, (rows, rows), 0)
    col = lax.broadcasted_iota(jnp.int32, (rows, rows), 1)
    shifted = dot(q, k, ((1,), (1,))) * (1.0 / math.sqrt(F)) + 1.0
    weights = jnp.where((col <= row) & (col < live), 0.5 * shifted * shifted + 0.5, 0.0).astype(BF)
    return dot(weights, v)


def old_state(cache_ref, head):
    pad = jnp.zeros((PHI_WIDE - PHI, DH), F32)
    old = [cache_ref[F + 1 :, head, :], cache_ref[1 : F + 1, head, :], cache_ref[0:1, head, :], pad]
    return jnp.concatenate([jnp.concatenate(old, axis=0), jnp.zeros((PHI_WIDE, WIDE - DH), F32)], axis=1)


def attend_part(slot, head, heads, length, q, own, state, gain_ref, pick):
    rows = q.shape[0]
    total = own + dot(phi_of(q, pick).astype(BF), state)
    square = jnp.sum(total * total, axis=-1, keepdims=True)
    gain = gain_ref[...].reshape(1, heads * DH)[:, head * DH : (head + 1) * DH]
    gain = jnp.concatenate([gain, jnp.zeros((1, WIDE - DH), F32)], axis=1)
    total = total * lax.rsqrt(square * (1.0 / DH) + 1e-05) * gain
    live = length - rows * (lax.axis_index("head") ^ slot)
    live_row = lax.broadcasted_iota(jnp.int32, (rows, WIDE), 0) < live
    return jnp.where(live_row, total, 0.0).astype(BF)


def project_part(parts, heads, w_ref, top, low):
    attended = jnp.concatenate(parts, axis=1)
    half = low.shape[0]
    w_out = out_projection(w_ref, heads)
    for out, rows in ((top, attended[:half]), (low, attended[half:])):
        out[...] = dot(rows, w_out).astype(BF)
        out.push()


def first_kernel(heads, len_ref, low, top, w_ref, sums, own, queries):
    qkv = qkv_of(heads, top, low, w_ref)
    pick = spreader()
    for head in range(heads):
        sums[head] = sums_of(0, heads, head, len_ref[0], qkv, pick)
    sums.push()
    for head in range(heads):
        own[head] = own_of(0, heads, head, len_ref[0], qkv)
    queries[...] = qkv[:, : heads * F]


def second_kernel(
    heads, len_ref, low1, top1, w_ref, low2, top2, cache, sums0, items, half_total, gain_ref, cache_ref,
    sums1, qkv1, sums2, qkv2, state3, served, state, sem
):
    start = 2 * sem.shape[0]
    copies = slot_copies(heads, start, start, cache_ref, state, sem)
    pick = spreader()
    for slot, low, top, sums, qkv in ((1, low1, top1, sums1, qkv1), (2, low2, top2, sums2, qkv2)):
        found = qkv_of(heads, top, low, w_ref)
        if slot == 1:
            for copy in copies:
                copy.start()
        qkv[...] = found
        qkv.push()
        for head in range(heads):
            sums[head] = sums_of(slot, heads, head, len_ref[0], found, pick)
        sums.push()
    for head in range(heads):
        state3[head] = state_before(3, old_state(cache, head), (sums0[head], sums1[head], sums2[head]))
    state3.push()
    serve_part(heads, start, items, half_total, gain_ref, copies, state, served)


def state_before(slot, old, sums):
    mine = lax.axis_index("head")
    for other, part in enumerate(sums):
        if other != slot:
            old = old + ((mine ^ other) < (mine ^ slot)).astype(F32) * part
    return old.astype(BF)


def third_kernel(heads, len_ref, low, top, w_ref, state3, gain_ref, out_w_ref, top3, low3, qkv3):
    length = len_ref[0]
    qkv = qkv_of(heads, top, low, w_ref)
    qkv3[...] = qkv
    qkv3.push()
    pick = spreader()
    parts = []
    for head in range(heads):
        q = parts_of(qkv, heads, head)[0]
        own = own_of(3, heads, head, length, qkv)
        parts.append(attend_part(3, head, heads, length, q, own, state3[head], gain_ref, pick))
    project_part(parts, heads, out_w_ref, top3, low3)


def fourth_kernel(
    heads, len_ref, qkv3, qkv1, cache, sums0, sums1, sums2, qkv2, gain_ref, out_w_ref, top1, low1, top2, low2, sums3
):
    pick = spreader()
    length = len_ref[0]
    for head in range(heads):
        sums3[head] = sums_of(3, heads, head, length, qkv3, pick)
    sums3.push()
    for slot, qkv, top, low in ((1, qkv1, top1, low1), (2, qkv2, top2, low2)):
        parts = []
        for head in range(heads):
            q = parts_of(qkv, heads, head)[0]
            own = own_of(slot, heads, head, length, qkv)
            state = state_before(slot, old_state(cache, head), (sums0[head], sums1[head], sums2[head], sums3[head]))
            parts.append(attend_part(slot, head, heads, length, q, own, state, gain_ref, pick))
        project_part(parts, heads, out_w_ref, top, low)


def fifth_kernel(
    heads, len_ref, cache, sums0, sums1, sums2, sums3, queries, own, gain_ref, out_w_ref, top0, low0, state_next
):
    pick = spreader()
    parts = []
    for head in range(heads):
        old = old_state(cache, head)
        sums = [part[head] for part in (sums0, sums1, sums2, sums3)]
        q = queries[:, head * F : (head + 1) * F]
        state = state_before(0, old, sums)
        parts.append(attend_part(0, head, heads, len_ref[0], q, own[head], state, gain_ref, pick))
        new = (old + (sums[0] + sums[1]) + (sums[2] + sums[3]))[:, :DH]
        state_next[0, F + 1 :, head, :] = new[:QUAD]
        state_next[0, 1 : F + 1, head, :] = new[QUAD : QUAD + F]
        state_next[0, 0:1, head, :] = new[QUAD + F : QUAD + F + 1]
    project_part(parts, heads, out_w_ref, top0, low0)


def add_kernel(top2, via_x, low1, via_y, two_y, two_x):
    two_y[...] = (top2[...].astype(F32) + via_x[...].astype(F32)).astype(BF)
    two_x[...] = (low1[...].astype(F32) + via_y[...].astype(F32)).astype(BF)


def total_kernel(top0, one_x, two_y, low0, one_y, two_x, out):
    out[0] = (top0[...].astype(F32) + one_x[...].astype(F32) + two_y[...].astype(F32)).astype(BF)
    out.push(0)
    out[1] = (low0[...].astype(F32) + one_y[...].astype(F32) + two_x[...].astype(F32)).astype(BF)
    out.push(1)


def placing_rank(owners_row, axis):
    down = lax.broadcasted_iota(jnp.int32, (DEC, DEC), 0)
    along = lax.broadcasted_iota(jnp.int32, (DEC, DEC), 1)
    earlier = down < along if axis == 0 else along < down
    return jnp.sum(jnp.where(earlier & (column(owners_row) == owners_row), 1, 0), axis=axis, keepdims=True)


def send_kernel(heads, capacity, tokens_ref, tail_ref, gain_ref, taps_ref, owner_ref, slot_ref, w_ref, out):
    tokens, factor = unit_rows(tokens_ref[...])
    normed = (tokens * factor * gain_ref[...].reshape(1, D)).astype(BF).astype(F32)
    tail = tail_ref[...].astype(F32)
    taps = taps_ref[...]
    conved = taps[0:1, :] * tail[:, 0, :] + taps[1:2, :] * tail[:, 1, :]
    conved = (conved + taps[2:3, :] * normed).astype(BF)
    owners = owner_ref[...]
    target = owners * capacity + placing_rank(owners, 0)
    placing = lax.broadcasted_iota(jnp.int32, (out.shape[0], DEC), 0) == target
    cache_slot = jnp.sum(jnp.where(placing, slot_ref[...] + 1, 0), axis=1, keepdims=True) - 1
    qkv = dot(conved, projection(w_ref, heads), ((1,), (1,))).astype(BF)
    sent = dot(ones_where(placing), qkv)
    lane = lax.broadcasted_iota(jnp.int32, sent.shape, 1)
    mark = 2 * heads * F + DH
    out[...] = jnp.where(lane == mark, cache_slot.astype(F32), sent).astype(BF)


def cache_spreaders(heads):
    lane, entry = lanes_of(PHI * heads)
    feature = lane >> (heads.bit_length() - 1)
    quad = feature - (1 + F)
    a = jnp.where(quad < 0, feature - 1, quad >> 4)
    return ones_where(a == entry), ones_where((quad >= 0) & ((quad & (F - 1)) == entry))


def slot_features(heads, items):
    mark = 2 * heads * F + DH
    first, second = cache_spreaders(heads)
    phis = []
    for head in range(heads):
        q = items[:, head * F : head * F + F]
        a = dot(q, first)
        b = dot(q, second)
        lane = lax.broadcasted_iota(jnp.int32, a.shape, 1)
        scale = jnp.where(lane < heads * (F + 1), 1.0 / math.sqrt(math.sqrt(F)), b * (1.0 / math.sqrt(2.0 * F)))
        value = jnp.where(lane < heads, 1.0, a * scale)
        phis.append(jnp.where((lane & (heads - 1)) == head, value, 0.0).astype(BF))
    slots = jnp.concatenate([items[:, mark : mark + 1].astype(F32)] * heads, axis=0)
    return jnp.concatenate(phis, axis=0), slots


def slot_copies(heads, start, count, cache_ref, state, sem):
    size = 2 * PHI * heads
    return [
        pltpu.make_async_copy(cache_ref.at[pl.ds(start * size // 2 + n * size, size)], state.at[pl.ds(n * size, size)], sem.at[n])
        for n in range(count // 2)
    ]


def slot_totals(heads, start, phis, slots, copies, state, total):
    span = PHI * heads
    waiting = list(copies)
    done = {}
    for n in range(2 * len(copies)):
        if n % 2 == 0:
            waiting.pop(0).wait()
        shift = n * span % 8
        rows = -(-(span + shift) // 8) * 8
        block = state[n * span - shift : n * span - shift + rows, :].astype(BF)
        done.setdefault(shift, []).append((n, block))
        if len(done[shift]) == 2:
            zeros = jnp.zeros((rows, WIDE - DH), BF)
            pair = [part for _, block in done[shift] for part in (block, zeros)]
            sides = [jnp.zeros((phis.shape[0], size), BF) for size in (shift, rows - span - shift)]
            wide = [side for side in (sides[0], phis, sides[1]) if side.shape[1] > 0]
            table = dot(jnp.concatenate(wide, axis=1), jnp.concatenate(pair, axis=1))
            for side, (place, _) in enumerate(done.pop(shift)):
                here = slots == float(start + place)
                total = total + jnp.where(here, table[:, side * WIDE : (side + 1) * WIDE], 0.0)
    return total


def serve_kernel(heads, items, cache_ref, total, state, sem):
    copies = slot_copies(heads, 0, 2 * sem.shape[0], cache_ref, state, sem)
    for copy in copies:
        copy.start()
    phis, slots = slot_features(heads, items)
    total[...] = slot_totals(heads, 0, phis, slots, copies, state, jnp.zeros(total.shape, F32))


def serve_part(heads, start, items, half_total, gain_ref, copies, state, out):
    count = items.shape[0]
    phis, slots = slot_features(heads, items)
    total = slot_totals(heads, start, phis, slots, copies, state, half_total[...])
    gains = gain_ref[...].reshape(1, heads * DH)
    for head in range(heads):
        q = items[:, head * F : head * F + F].astype(F32)
        k = items[:, (heads + head) * F : (heads + head) * F + F].astype(F32)
        at = 2 * heads * F + head * WIDE
        v = items[:, at : at + DH].astype(F32)
        inner = jnp.sum(q * k, axis=-1, keepdims=True) * (1.0 / math.sqrt(F))
        value = total[head * count : (head + 1) * count, :DH] + (1.0 + inner + 0.5 * inner * inner) * v
        square = jnp.sum(value * value, axis=-1, keepdims=True)
        value = value * lax.rsqrt(square * (1.0 / DH) + 1e-05) * gains[:, head * DH : (head + 1) * DH]
        out[:, head * WIDE : head * WIDE + DH] = value.astype(BF)
        out[:, head * WIDE + DH : (head + 1) * WIDE] = jnp.zeros((count, WIDE - DH), BF)


def return_kernel(heads, capacity, items_ref, owner_ref, w_ref, seen_x, seen_y, *outs):
    owners = owner_ref[...]
    target = column(owners) * capacity + placing_rank(owners, 1)
    placing = lax.broadcasted_iota(jnp.int32, (DEC, items_ref.shape[0]), 1) == target
    attended = dot(ones_where(placing), items_ref[...]).astype(BF)
    row = lax.broadcasted_iota(jnp.int32, (4 * TILE, DEC), 0)
    entry = lax.broadcasted_iota(jnp.int32, (4 * TILE, DEC), 1)
    device = lax.axis_index("head") ^ (row // TILE)
    wanted = ((row % TILE) < DEC // 4) & (entry == device * (DEC // 4) + row % TILE)
    attended = dot(ones_where(wanted), attended).astype(BF)
    shares = dot(attended, out_projection(w_ref, heads)).astype(BF)
    for slot, out in enumerate(outs):
        out[...] = shares[slot * TILE : (slot + 1) * TILE]


def far_off(array):
    return pltpu.with_memory_space_constraint(array, pltpu.HBM)


def entries(ref):
    return [ref.at[n] for n in range(ref.shape[0])]


class Fetched:
    def __init__(self, copies, place):
        self.copies, self.place, self.here = copies, place, set()
        self.shape, self.dtype = place.shape, place.dtype

    def __getitem__(self, index):
        entry = index[0] if isinstance(index, tuple) else index
        wanted = [entry] if len(self.copies) > 1 and isinstance(entry, int) else range(len(self.copies))
        for n in wanted:
            self.wait(n)
        return self.place[index]

    def wait(self, n):
        if n not in self.here:
            self.copies[n].wait()
            self.here.add(n)


class Pushed:
    def __init__(self, copies, place):
        self.copies, self.place, self.gone = copies, place, set()
        self.shape, self.dtype = place.shape, place.dtype

    def __getitem__(self, index):
        return self.place[index]

    def __setitem__(self, index, value):
        self.place[index] = value

    def push(self, entry=None):
        if (entry is None) == (len(self.copies) == 1):
            self.send(entry or 0)

    def send(self, n):
        if n not in self.gone:
            self.copies[n].start()
            self.gone.add(n)


class Near:
    def __init__(self, ref):
        self.ref, self.shape, self.dtype, self.copies = ref, ref.shape, ref.dtype, []

    def __getitem__(self, index):
        return self.ref[index]

    def __setitem__(self, index, value):
        self.ref[index] = value

    def push(self, entry=None):
        pass


def hbm_call(kernel, outs, flops, size, scalars=(), picked=None, waits=(), loose=(), here=(), near=(), split=(), split_out=(), raw=(), scratch=()):
    def run(*args):
        count, many = len(args), len(outs)
        moved = [n for n in range(count) if n not in here and n not in raw]
        far = [n for n in range(many) if n not in near]

        def shape_in(n):
            return args[n].shape[2:] if n == picked else args[n].shape

        pieces = sum(shape_in(n)[0] if n in split else 1 for n in moved)
        pieces += sum(outs[n].shape[0] if n in split_out else 1 for n in far)

        def body(*refs):
            refs = list(refs)

            def take(number):
                taken = refs[:number]
                del refs[:number]
                return taken

            numbers, sources, _, targets = take(len(scalars)), take(count), take(len(waits)), take(many)
            places, results, own, (sem,) = dict(zip(moved, take(len(moved)))), dict(zip(far, take(len(far)))), take(len(scratch)), refs
            used = iter(range(pieces))

            def copies(source, target, apart):
                pairs = zip(entries(source), entries(target)) if apart else [(source, target)]
                return [pltpu.make_async_copy(a, b, sem.at[next(used)]) for a, b in pairs]

            ins = []
            for n, source in enumerate(sources):
                if n in here or n in raw:
                    ins.append(source)
                    continue
                if n == picked:
                    source = source.at[0, numbers[-1][0]]
                fetched = Fetched(copies(source, places[n], n in split), places[n])
                for copy in fetched.copies:
                    copy.start()
                ins.append(fetched)
            done = [
                Pushed(copies(results[n], target, n in split_out), results[n]) if n in far else Near(target)
                for n, target in enumerate(targets)
            ]
            kernel(*numbers[: len(scalars) - (picked is not None)], *ins, *done, *own)
            for n in far:
                for entry in range(len(done[n].copies)):
                    done[n].send(entry)
            for n in moved:
                for entry in range(len(ins[n].copies)):
                    ins[n].wait(entry)
            for n in far:
                for copy in done[n].copies:
                    copy.wait()

        hbm = pl.BlockSpec(memory_space=pltpu.HBM)
        in_vmem = pl.BlockSpec(memory_space=pltpu.VMEM)
        anywhere = pl.BlockSpec(memory_space=pl.ANY)
        free = set(loose) | set(here)
        return pl.pallas_call(
            body,
            out_shape=[o if n in near else pltpu.HBM(o.shape, o.dtype) for n, o in enumerate(outs)],
            in_specs=[pl.BlockSpec(memory_space=pltpu.SMEM)] * len(scalars)
            + [in_vmem if n in here else anywhere if n in loose else hbm for n in range(count)]
            + [hbm] * len(waits),
            out_specs=[in_vmem if n in near else hbm for n in range(many)],
            scratch_shapes=[pltpu.VMEM(shape_in(n), args[n].dtype) for n in moved]
            + [pltpu.VMEM(outs[n].shape, outs[n].dtype) for n in far]
            + list(scratch)
            + [pltpu.SemaphoreType.DMA((pieces,))],
            compiler_params=pltpu.CompilerParams(vmem_limit_bytes=40 * MIB),
            cost_estimate=pl.CostEstimate(flops=flops, bytes_accessed=size, transcendentals=0),
        )(*scalars, *[a if n in free else far_off(a) for n, a in enumerate(args)], *map(far_off, waits))

    return run


def shape(*dims, dtype=BF):
    return jax.ShapeDtypeStruct(dims, dtype)


def across(array, by):
    return lax.ppermute(array, "head", [(i, i ^ by) for i in range(4)])


def local_square(
    stretch_tokens,
    stretch_tail,
    decode_tokens,
    decode_tail,
    norm_gain,
    conv_taps,
    qkv_weight,
    out_gain,
    out_weight,
    state_cache,
    stretch_len,
    stretch_slot,
    decode_slot,
    decode_owner,
):
    heads = qkv_weight.shape[1]
    rows = stretch_tokens.shape[1]
    half = rows // 2
    wide = heads * (2 * F + WIDE)
    w_in = jnp.transpose(qkv_weight, (1, 2, 0))
    cache = jnp.transpose(state_cache, (0, 1, 4, 2, 3))
    length = stretch_len.astype(jnp.int32)
    slot = stretch_slot.astype(jnp.int32)
    hbm = pl.BlockSpec(memory_space=pltpu.HBM)
    piece = shape(half, D)
    block_flops = 2 * rows * D * wide + 6 * heads * rows * rows * WIDE
    attend_flops = 2 * rows * heads * WIDE * (D + PHI_WIDE)
    size = 4 * rows * D

    low, top, begin, end = hbm_call(conv_kernel, [piece, piece, shape(TILE, D), shape(TILE, D)], 20 * rows * D, size)(
        stretch_tokens[0], stretch_tail[0], norm_gain, conv_taps
    )
    low_x = across(low, 1)
    low_y = across(low, 2)
    end = from_behind(end, "head", 1)

    groups = lax.axis_size("tok")
    capacity = max(2, 2 * DEC // groups)
    count = groups * capacity
    owner_row = decode_owner.reshape(1, DEC)
    (sent,) = hbm_call(functools.partial(send_kernel, heads, capacity), [shape(count, wide)], 2 * DEC * D * wide, 2 * D * wide)(
        decode_tokens[0], decode_tail[0], norm_gain, conv_taps, owner_row, decode_slot, w_in
    )
    top = pl.pallas_call(
        lambda first_ref, top_ref, begin_ref, end_ref, taps_ref, wait_ref, *refs: rim_kernel(
            first_ref, top_ref, begin_ref, end_ref, taps_ref, *refs
        ),
        out_shape=pltpu.HBM((half, D), BF),
        in_specs=[pl.BlockSpec(memory_space=pltpu.SMEM), hbm, hbm, pl.BlockSpec(memory_space=pl.ANY), hbm, hbm],
        out_specs=hbm,
        scratch_shapes=[pltpu.VMEM((TILE, D), BF), pltpu.VMEM((TILE, D), BF), pltpu.VMEM((3, D), F32), pltpu.VMEM((TILE, D), BF)]
        + [pltpu.SemaphoreType.DMA((4,))],
        input_output_aliases={1: 0},
        compiler_params=pltpu.CompilerParams(vmem_limit_bytes=40 * MIB),
        cost_estimate=pl.CostEstimate(flops=16 * D, bytes_accessed=128 * D, transcendentals=0),
    )(lax.axis_index("head").reshape(1), far_off(top), far_off(begin), end, far_off(conv_taps), far_off(sent))
    top_x = across(top, 1)
    top_y = across(top, 2)
    items = lax.all_to_all(sent.reshape(groups, capacity, wide), "tok", split_axis=0, concat_axis=0, tiled=True)

    sums, own, queries = shape(heads, PHI_WIDE, WIDE, dtype=F32), shape(heads, rows, WIDE, dtype=F32), shape(rows, heads * F)
    sums0, own0, queries0 = hbm_call(
        functools.partial(first_kernel, heads),
        [sums, own, queries],
        block_flops,
        size,
        scalars=[length],
    )(low, top, w_in)
    items = items.reshape(count, wide)
    slots = cache.shape[1]
    flat = cache.reshape(slots * PHI * heads, DH)
    states = [pltpu.VMEM((slots // 2 * PHI * heads, DH), F32), pltpu.SemaphoreType.DMA((slots // 4,))]
    serve_flops = slots * heads * heads * DH * PHI * count
    (half_total,) = hbm_call(
        functools.partial(serve_kernel, heads),
        [shape(heads * count, WIDE, dtype=F32)],
        serve_flops,
        2 * slots * heads * WIDE * PHI,
        loose=(0,),
        raw=(1,),
        scratch=states,
        waits=[queries0],
    )(items, flat)
    low_y, top_x, low_x = lax.optimization_barrier((low_y, top_x, low_x, half_total))[:3]
    low_xy = across(low_y, 1)
    top_xy = across(top_x, 2)
    blocks = shape(rows, wide)
    sums1, qkv1, sums2, qkv2, state3, served = hbm_call(
        functools.partial(second_kernel, heads),
        [sums, blocks, sums, blocks, shape(heads, PHI_WIDE, WIDE), shape(count, heads * WIDE)],
        2 * block_flops + serve_flops,
        2 * slots * heads * WIDE * PHI,
        scalars=[length, slot],
        picked=5,
        loose=(0, 1, 3, 4, 7),
        raw=(10,),
        scratch=states,
    )(low_x, top_x, w_in, low_y, top_y, cache, sums0, items, half_total, out_gain, flat)
    top3, low3, qkv3 = hbm_call(
        functools.partial(third_kernel, heads),
        [piece, piece, blocks],
        block_flops + attend_flops,
        size,
        scalars=[length],
        loose=(0, 1),
        near=(0, 1),
        waits=[qkv2],
    )(low_xy, top_xy, w_in, state3, out_gain, out_weight)

    via_x = across(top3, 1)
    via_y = across(low3, 2)
    served = lax.optimization_barrier((served, top3))[0]
    returned = lax.all_to_all(
        served.reshape(groups, capacity, heads * WIDE), "tok", split_axis=0, concat_axis=0, tiled=True
    ).reshape(count, heads * WIDE)
    top1, low1, top2, low2, sums3 = hbm_call(
        functools.partial(fourth_kernel, heads),
        [piece] * 4 + [sums],
        2 * attend_flops,
        size,
        scalars=[length, slot],
        picked=2,
    )(qkv3, qkv1, cache, sums0, sums1, sums2, qkv2, out_gain, out_weight)
    one_x = across(top1, 1)
    one_y = across(low2, 2)
    two_y, two_x = hbm_call(add_kernel, [piece, piece], 0, size, here=(1, 3), near=(0, 1), waits=[top1])(top2, via_x, low1, via_y)
    top0, low0, state_next = hbm_call(
        functools.partial(fifth_kernel, heads),
        [piece] * 2 + [shape(1, PHI, heads, DH, dtype=F32)],
        attend_flops,
        size,
        scalars=[length, slot],
        picked=0,
        waits=[two_x],
    )(cache, sums0, sums1, sums2, sums3, queries0, own0, out_gain, out_weight)
    decoded = hbm_call(
        functools.partial(return_kernel, heads, capacity),
        [shape(TILE, D)] * 4,
        2 * DEC * heads * WIDE * D,
        2 * heads * WIDE * D,
        loose=(0, 3, 4),
        waits=[top0],
        raw=(3, 4),
    )(returned, owner_row, out_weight, one_x, one_y)
    shares = [decoded[0]] + [across(decoded[by], by) for by in (1, 2, 3)]
    two_y = across(two_y, 2)
    two_x = across(two_x, 1)
    state_next = jnp.transpose(state_next, (0, 2, 3, 1))
    (stretch_out,) = hbm_call(
        total_kernel,
        [shape(2, half, D)],
        0,
        8 * rows * D,
        loose=(1, 2, 4, 5),
        split_out=(0,),
        waits=[decoded[0]],
    )(top0, one_x, two_y, low0, one_y, two_x)
    shares = lax.optimization_barrier((*shares, stretch_out))[:4]
    decode_out = sum(share[: DEC // 4].astype(F32) for share in shares).astype(BF)
    return (stretch_out.reshape(1, rows, D), decode_out[None], state_next)


def from_behind(array, axis, by):
    peers = lax.axis_size(axis)
    pairs = [(i, i + by) for i in range(peers) if 0 <= i + by < peers]
    return lax.ppermute(array, axis, pairs)


def rms_rows(values, gain):
    values = values.astype(jnp.float32)
    factor = lax.rsqrt(jnp.mean(values * values, axis=-1, keepdims=True) + 1e-05)
    return values * factor * gain


def features(vectors):
    breadth = vectors.shape[-1]
    linear = vectors / math.sqrt(math.sqrt(breadth))
    outer = vectors[..., :, None] * vectors[..., None, :] / math.sqrt(2.0 * breadth)
    outer = outer.reshape(vectors.shape[:-1] + (breadth * breadth,))
    ones = jnp.ones(vectors.shape[:-1] + (1,), vectors.dtype)
    return jnp.concatenate([ones, linear, outer], axis=-1)


def convolve(tail, normed, conv_taps):
    joined = jnp.concatenate([tail, normed], axis=-2).astype(jnp.float32)
    span_rows = normed.shape[-2]
    total = conv_taps[0] * joined[..., 0:span_rows, :]
    total = total + conv_taps[1] * joined[..., 1 : span_rows + 1, :]
    total = total + conv_taps[2] * joined[..., 2 : span_rows + 2, :]
    return total.astype(jnp.bfloat16)


def decode_items(items, slot_items, cache_own, out_gain, head_count):
    item_count = items.shape[0]
    shaped = items.reshape(item_count, head_count, 2 * F + DH).astype(jnp.float32)
    queries = shaped[:, :, :F]
    key_feats = shaped[:, :, F : 2 * F]
    values = shaped[:, :, 2 * F :]
    slot_total = cache_own.shape[0]
    table = jnp.einsum(
        "nhp,shdp->nshd", features(queries), cache_own, precision=lax.Precision.HIGHEST
    )
    picker = (slot_items[:, None] == jnp.arange(slot_total)[None, :]).astype(jnp.float32)
    carried = jnp.einsum("ns,nshd->nhd", picker, table, precision=lax.Precision.HIGHEST)
    inner = jnp.sum(queries * key_feats, axis=-1) / math.sqrt(F)
    own_term = (1.0 + inner + 0.5 * inner * inner)[..., None] * values
    attended = rms_rows(carried + own_term, out_gain.reshape(head_count, DH))
    return attended.astype(jnp.bfloat16).reshape(item_count, head_count * DH)


def local(
    stretch_tokens,
    stretch_tail,
    decode_tokens,
    decode_tail,
    norm_gain,
    conv_taps,
    qkv_weight,
    out_gain,
    out_weight,
    state_cache,
    stretch_len,
    stretch_slot,
    decode_slot,
    decode_owner,
):
    head_count = qkv_weight.shape[1]
    block_width = qkv_weight.shape[2]
    rows_own = stretch_tokens.shape[1]
    w_flat = qkv_weight.reshape(D, head_count * block_width)
    gains = out_gain.reshape(head_count, DH)
    normed = rms_rows(stretch_tokens[0], norm_gain).astype(jnp.bfloat16)
    rim_rows = from_behind(normed[rows_own - 2 :], "head", 1)
    first_dev = lax.axis_index("head") == 0
    rim_rows = jnp.where(first_dev, stretch_tail[0], rim_rows)
    conved = convolve(rim_rows, normed, conv_taps)
    grouped = jnp.dot(
        lax.all_gather(conved, "head", axis=0, tiled=True),
        w_flat,
        preferred_element_type=jnp.float32,
    ).astype(jnp.bfloat16)
    grouped = grouped.reshape(STRETCH, head_count, block_width)
    queries = grouped[:, :, :F]
    key_feats = grouped[:, :, F : 2 * F]
    values = grouped[:, :, 2 * F :]
    length = stretch_len[0]
    positions = jnp.arange(STRETCH)
    valid_rows = positions < length
    state_old = lax.dynamic_index_in_dim(state_cache[0], stretch_slot[0], 0, keepdims=False)
    carried = jnp.einsum(
        "ihp,hdp->ihd",
        features(queries.astype(jnp.float32)),
        state_old,
        precision=lax.Precision.HIGHEST,
    )
    block_rows = min(512, STRETCH)
    pieces = []
    for anchor in range(0, STRETCH, block_rows):
        finish = anchor + block_rows
        inner = jnp.einsum(
            "ihf,jhf->hij",
            queries[anchor:finish],
            key_feats[:finish],
            preferred_element_type=jnp.float32,
        ) / math.sqrt(F)
        weights = 1.0 + inner + 0.5 * inner * inner
        allowed = (positions[None, :finish] <= positions[anchor:finish, None]) & valid_rows[
            None, :finish
        ]
        weights = jnp.where(allowed[None], weights, 0.0).astype(jnp.bfloat16)
        pieces.append(
            jnp.einsum("hij,jhd->ihd", weights, values[:finish], preferred_element_type=jnp.float32)
        )
    local_sum = jnp.concatenate(pieces, axis=0)
    attended = rms_rows(carried + local_sum, gains)
    attended = (
        jnp.where(valid_rows[:, None, None], attended, 0.0)
        .astype(jnp.bfloat16)
        .reshape(STRETCH, head_count * DH)
    )
    key_phi = jnp.where(
        valid_rows[:, None, None], features(key_feats.astype(jnp.float32)), 0.0
    ).astype(jnp.bfloat16)
    state_next = state_old + jnp.einsum(
        "jhd,jhp->hdp", values, key_phi, preferred_element_type=jnp.float32
    )
    part_rows = attended
    stretch_out = lax.psum_scatter(
        jnp.dot(part_rows, out_weight, preferred_element_type=jnp.float32).astype(jnp.bfloat16),
        "head",
        scatter_dimension=0,
        tiled=True,
    )
    dec_normed = rms_rows(decode_tokens[0], norm_gain).astype(jnp.bfloat16)
    dec_conved = convolve(decode_tail[0], dec_normed[:, None, :], conv_taps)[:, 0, :]
    dec_qkv = jnp.dot(dec_conved, w_flat, preferred_element_type=jnp.float32).astype(jnp.bfloat16)
    owners = decode_owner[0, :, 0]
    slots_here = decode_slot[0]
    groups = lax.axis_size("tok")
    capacity = max(2, 2 * DEC // groups)
    earlier = jnp.arange(DEC)[None, :] < jnp.arange(DEC)[:, None]
    same_owner = owners[None, :] == owners[:, None]
    rank_in = jnp.sum(earlier & same_owner, axis=1)
    target = owners * capacity + rank_in
    placing = jnp.arange(groups * capacity)[:, None] == target[None, :]
    sent_rows = jnp.dot(
        placing.astype(jnp.bfloat16), dec_qkv, preferred_element_type=jnp.float32
    ).astype(jnp.bfloat16)
    sent_rows = sent_rows.reshape(groups, capacity, head_count * block_width)
    sent_slots = jnp.sum(jnp.where(placing, slots_here[None, :] + 1, 0), axis=1) - 1
    sent_slots = sent_slots.reshape(groups, capacity)
    item_rows = lax.all_to_all(sent_rows, "tok", split_axis=0, concat_axis=0, tiled=True)
    item_slots = lax.all_to_all(sent_slots, "tok", split_axis=0, concat_axis=0, tiled=True)
    item_count = item_rows.shape[1]
    flat_out = decode_items(
        item_rows.reshape(groups * item_count, head_count * block_width),
        item_slots.reshape(groups * item_count),
        state_cache[0],
        out_gain,
        head_count,
    )
    served = flat_out.reshape(groups, item_count, head_count * DH)
    returned = lax.all_to_all(served, "tok", split_axis=0, concat_axis=0, tiled=True)
    dec_attended = jnp.dot(
        jnp.transpose(placing).astype(jnp.bfloat16),
        returned.reshape(groups * capacity, head_count * DH),
        preferred_element_type=jnp.float32,
    ).astype(jnp.bfloat16)
    part_rows = dec_attended
    decode_out = lax.psum_scatter(
        jnp.dot(part_rows, out_weight, preferred_element_type=jnp.float32).astype(jnp.bfloat16),
        "head",
        scatter_dimension=0,
        tiled=True,
    )
    return (stretch_out[None], decode_out[None], state_next[None])


def solution(mesh):
    in_specs = (
        P("tok", "head", None),
        P("tok", None, None),
        P("tok", None, None),
        P("tok", None, None, None),
        P(),
        P(),
        P(None, "head", None),
        P("head"),
        P("head", None),
        P("tok", None, "head", None, None),
        P("tok"),
        P("tok"),
        P("tok", None),
        P("tok", None, None),
    )
    out_specs = (P("tok", "head", None), P("tok", "head", None), P("tok", "head", None, None))
    chosen = local_square if mesh.shape["head"] == 4 else local
    return jax.shard_map(chosen, mesh=mesh, in_specs=in_specs, out_specs=out_specs, check_vma=False)
```

```python
import functools
import math

import jax
import jax.numpy as jnp
import numpy as np
from jax import lax
from jax.experimental import pallas as pl
from jax.experimental.pallas import tpu as pltpu
from jax.sharding import PartitionSpec as P

D = 1792
DH = 112
F = 16
STRETCH = 1024
DEC = 32
QUAD = F * F
PHI = 1 + F + QUAD
WIDE = 128
PHI_WIDE = QUAD + 128
TILE = 16
MIB = 1 << 20
BF = jnp.bfloat16
F32 = jnp.float32


def lanes_of(size):
    return lax.broadcasted_iota(jnp.int32, (F, size), 1), lax.broadcasted_iota(jnp.int32, (F, size), 0)


def ones_where(mask):
    return jnp.where(mask, 1.0, 0.0).astype(BF)


def spreader():
    lane, entry = lanes_of(PHI_WIDE)
    return ones_where(jnp.where(lane < QUAD, lane >> 4, lane & (F - 1)) == entry)


def dot(left, right, contract=((1,), (0,))):
    return lax.dot_general(left, right, (contract, ((), ())), preferred_element_type=F32)


def phi_of(vectors, pick):
    spread = dot(vectors, pick)
    a, b = spread[:, :QUAD], spread[:, QUAD:]
    quad = a * jnp.concatenate([b] * (QUAD // 128), axis=1) * (1.0 / math.sqrt(2.0 * F))
    lane = lax.broadcasted_iota(jnp.int32, b.shape, 1)
    rest = jnp.where(lane < F, b * (1.0 / math.sqrt(math.sqrt(F))), jnp.where(lane == F, 1.0, 0.0))
    return jnp.concatenate([quad, rest], axis=1)


def unit_rows(values):
    values = values.astype(F32)
    total = jnp.sum(values * values, axis=-1, keepdims=True)
    return values, lax.rsqrt(total * (1.0 / D) + 1e-05)


def column(row):
    size = row.shape[1]
    same = lax.broadcasted_iota(jnp.int32, (size, size), 0) == lax.broadcasted_iota(jnp.int32, (size, size), 1)
    return jnp.sum(jnp.where(same, row, 0), axis=1, keepdims=True)


def projection(w_ref, heads):
    pieces = [w_ref[h, :F, :] for h in range(heads)] + [w_ref[h, F : 2 * F, :] for h in range(heads)]
    for h in range(heads):
        pieces += [w_ref[h, 2 * F :, :], jnp.zeros((WIDE - DH, D), w_ref.dtype)]
    return jnp.concatenate(pieces, axis=0)


def out_projection(w_ref, heads):
    pieces = []
    for h in range(heads):
        pieces += [w_ref[h * DH : (h + 1) * DH, :], jnp.zeros((WIDE - DH, D), w_ref.dtype)]
    return jnp.concatenate(pieces, axis=0)


def conv_kernel(tokens_ref, tail_ref, gain_ref, taps_ref, low, top, begin, end):
    rows = tokens_ref.shape[0]
    half = rows // 2
    gain = gain_ref[...].reshape(1, D)
    taps = taps_ref[...]
    _, factor = unit_rows(tokens_ref[...])
    step = 256
    row = lax.broadcasted_iota(jnp.int32, (rows, step), 0)
    for at in range(0, D, step):
        cols = slice(at, at + step)
        normed = tokens_ref[:, cols].astype(F32) * factor * gain[:, cols]
        normed = normed.astype(BF)
        begin[:, cols] = normed[:16]
        end[:, cols] = normed[rows - 16 :]
        normed = normed.astype(F32)
        tail = tail_ref[:, cols].astype(F32)
        one = jnp.where(row == 0, tail[1:2], pltpu.roll(normed, 1, 0))
        two = pltpu.roll(normed, 2, 0)
        two = jnp.where(row == 0, tail[0:1], jnp.where(row == 1, tail[1:2], two))
        total = taps[0:1, cols] * two + taps[1:2, cols] * one + taps[2:3, cols] * normed
        total = total.astype(BF)
        top[:, cols] = total[:half]
        low[:, cols] = total[half:]


def rim_kernel(first_ref, top_ref, begin_ref, end_ref, taps_ref, out_ref, begin, end, taps, rows, sem):
    copies = [
        pltpu.make_async_copy(src, place, sem.at[n])
        for n, (src, place) in enumerate([(begin_ref, begin), (end_ref, end), (taps_ref, taps)])
    ]
    for copy in copies:
        copy.start()
    for copy in copies:
        copy.wait()
    now = begin[...].astype(F32)
    last = end[...].astype(F32)
    row = lax.broadcasted_iota(jnp.int32, now.shape, 0)
    one = jnp.where(row == 0, last[15:16], pltpu.roll(now, 1, 0))
    two = jnp.where(row == 0, last[14:15], jnp.where(row == 1, last[15:16], pltpu.roll(now, 2, 0)))
    rows[...] = (taps[0:1, :] * two + taps[1:2, :] * one + taps[2:3, :] * now).astype(BF)

    @pl.when(first_ref[0] != 0)
    def _():
        back = pltpu.make_async_copy(rows, out_ref.at[:16], sem.at[3])
        back.start()
        back.wait()


def qkv_of(heads, top, low, w_ref):
    conved = jnp.concatenate([top[...], low[...]], axis=0)
    return dot(conved, projection(w_ref, heads), ((1,), (1,))).astype(BF)


def parts_of(qkv, heads, head):
    at = 2 * heads * F + head * WIDE
    return qkv[:, head * F : (head + 1) * F], qkv[:, (heads + head) * F : (heads + head + 1) * F], qkv[:, at : at + WIDE]


def sums_of(slot, heads, head, length, qkv, pick):
    _, k, v = parts_of(qkv, heads, head)
    live = length - v.shape[0] * (lax.axis_index("head") ^ slot)
    live_row = lax.broadcasted_iota(jnp.int32, v.shape, 0) < live
    v = jnp.where(live_row, v.astype(F32), 0.0).astype(BF)
    return dot(phi_of(k, pick).astype(BF), v, ((0,), (0,)))


def own_of(slot, heads, head, length, qkv):
    q, k, v = parts_of(qkv, heads, head)
    rows = v.shape[0]
    live = length - rows * (lax.axis_index("head") ^ slot)
    row = lax.broadcasted_iota(jnp.int32, (rows, rows), 0)
    col = lax.broadcasted_iota(jnp.int32, (rows, rows), 1)
    shifted = dot(q, k, ((1,), (1,))) * (1.0 / math.sqrt(F)) + 1.0
    weights = jnp.where((col <= row) & (col < live), 0.5 * shifted * shifted + 0.5, 0.0).astype(BF)
    return dot(weights, v)


def old_state(cache_ref, head):
    pad = jnp.zeros((PHI_WIDE - PHI, DH), F32)
    old = [cache_ref[F + 1 :, head, :], cache_ref[1 : F + 1, head, :], cache_ref[0:1, head, :], pad]
    return jnp.concatenate([jnp.concatenate(old, axis=0), jnp.zeros((PHI_WIDE, WIDE - DH), F32)], axis=1)


def attend_part(slot, head, heads, length, q, own, state, gain_ref, pick):
    rows = q.shape[0]
    total = own + dot(phi_of(q, pick).astype(BF), state)
    square = jnp.sum(total * total, axis=-1, keepdims=True)
    gain = gain_ref[...].reshape(1, heads * DH)[:, head * DH : (head + 1) * DH]
    gain = jnp.concatenate([gain, jnp.zeros((1, WIDE - DH), F32)], axis=1)
    total = total * lax.rsqrt(square * (1.0 / DH) + 1e-05) * gain
    live = length - rows * (lax.axis_index("head") ^ slot)
    live_row = lax.broadcasted_iota(jnp.int32, (rows, WIDE), 0) < live
    return jnp.where(live_row, total, 0.0).astype(BF)


def project_part(parts, heads, w_ref, top, low):
    attended = jnp.concatenate(parts, axis=1)
    half = low.shape[0]
    w_out = out_projection(w_ref, heads)
    for out, rows in ((top, attended[:half]), (low, attended[half:])):
        out[...] = dot(rows, w_out).astype(BF)
        out.push()


def first_kernel(heads, len_ref, low, top, w_ref, sums, own, queries):
    qkv = qkv_of(heads, top, low, w_ref)
    pick = spreader()
    for head in range(heads):
        sums[head] = sums_of(0, heads, head, len_ref[0], qkv, pick)
    sums.push()
    for head in range(heads):
        own[head] = own_of(0, heads, head, len_ref[0], qkv)
    queries[...] = qkv[:, : heads * F]


def second_kernel(
    heads, len_ref, low1, top1, w_ref, low2, top2, cache, sums0, items, half_total, gain_ref, out_w_ref, cache_ref,
    sums1, qkv1, sums2, qkv2, state3, served, old, state, sem
):
    start = 2 * sem.shape[0]
    copies = slot_copies(heads, start, start, cache_ref, state, sem)
    pick = spreader()
    for slot, low, top, sums, qkv in ((1, low1, top1, sums1, qkv1), (2, low2, top2, sums2, qkv2)):
        found = qkv_of(heads, top, low, w_ref)
        if slot == 1:
            for copy in copies:
                copy.start()
        qkv[...] = found
        qkv.push()
        for head in range(heads):
            sums[head] = sums_of(slot, heads, head, len_ref[0], found, pick)
        sums.push()
    for head in range(heads):
        old[head] = old_state(cache, head)
        state3[head] = state_before(3, old[head], (sums0[head], sums1[head], sums2[head]))
    old.push()
    state3.push()
    serve_part(heads, start, items, half_total, gain_ref, out_w_ref, copies, state, served)


def state_before(slot, old, sums):
    mine = lax.axis_index("head")
    for other, part in enumerate(sums):
        if other != slot:
            old = old + ((mine ^ other) < (mine ^ slot)).astype(F32) * part
    return old.astype(BF)


def third_kernel(heads, len_ref, low, top, w_ref, state3, gain_ref, out_w_ref, top3, low3, qkv3):
    length = len_ref[0]
    qkv = qkv_of(heads, top, low, w_ref)
    qkv3[...] = qkv
    qkv3.push()
    pick = spreader()
    parts = []
    for head in range(heads):
        q = parts_of(qkv, heads, head)[0]
        own = own_of(3, heads, head, length, qkv)
        parts.append(attend_part(3, head, heads, length, q, own, state3[head], gain_ref, pick))
    project_part(parts, heads, out_w_ref, top3, low3)


def fourth_kernel(
    heads, len_ref, qkv3, qkv1, old, sums0, sums1, sums2, qkv2, gain_ref, out_w_ref, top1, low1, top2, low2, sums3
):
    pick = spreader()
    length = len_ref[0]
    for head in range(heads):
        sums3[head] = sums_of(3, heads, head, length, qkv3, pick)
    sums3.push()
    for slot, qkv, top, low in ((1, qkv1, top1, low1), (2, qkv2, top2, low2)):
        parts = []
        for head in range(heads):
            q = parts_of(qkv, heads, head)[0]
            own = own_of(slot, heads, head, length, qkv)
            state = state_before(slot, old[head], (sums0[head], sums1[head], sums2[head], sums3[head]))
            parts.append(attend_part(slot, head, heads, length, q, own, state, gain_ref, pick))
        project_part(parts, heads, out_w_ref, top, low)


def fifth_kernel(
    heads, len_ref, olds, sums0, sums1, sums2, sums3, queries, own, gain_ref, out_w_ref, top0, low0, state_next
):
    pick = spreader()
    parts = []
    for head in range(heads):
        old = olds[head]
        sums = [part[head] for part in (sums0, sums1, sums2, sums3)]
        q = queries[:, head * F : (head + 1) * F]
        state = state_before(0, old, sums)
        parts.append(attend_part(0, head, heads, len_ref[0], q, own[head], state, gain_ref, pick))
        new = (old + (sums[0] + sums[1]) + (sums[2] + sums[3]))[:, :DH]
        state_next[0, F + 1 :, head, :] = new[:QUAD]
        state_next[0, 1 : F + 1, head, :] = new[QUAD : QUAD + F]
        state_next[0, 0:1, head, :] = new[QUAD + F : QUAD + F + 1]
    project_part(parts, heads, out_w_ref, top0, low0)


def add_kernel(top2, via_x, low1, via_y, two_y, two_x):
    two_y[...] = (top2[...].astype(F32) + via_x[...].astype(F32)).astype(BF)
    two_x[...] = (low1[...].astype(F32) + via_y[...].astype(F32)).astype(BF)


def total_kernel(top0, two_y, low0, two_x, out):
    out[0] = (top0[...].astype(F32) + two_y[...].astype(F32)).astype(BF)
    out.push(0)
    out[1] = (low0[...].astype(F32) + two_x[...].astype(F32)).astype(BF)
    out.push(1)


def placing_rank(owners_row, axis):
    down = lax.broadcasted_iota(jnp.int32, (DEC, DEC), 0)
    along = lax.broadcasted_iota(jnp.int32, (DEC, DEC), 1)
    earlier = down < along if axis == 0 else along < down
    return jnp.sum(jnp.where(earlier & (column(owners_row) == owners_row), 1, 0), axis=axis, keepdims=True)


def send_kernel(heads, capacity, tokens_ref, tail_ref, gain_ref, taps_ref, owner_ref, slot_ref, w_ref, out):
    tokens, factor = unit_rows(tokens_ref[...])
    normed = (tokens * factor * gain_ref[...].reshape(1, D)).astype(BF).astype(F32)
    tail = tail_ref[...].astype(F32)
    taps = taps_ref[...]
    conved = taps[0:1, :] * tail[:, 0, :] + taps[1:2, :] * tail[:, 1, :]
    conved = (conved + taps[2:3, :] * normed).astype(BF)
    owners = owner_ref[...]
    target = owners * capacity + placing_rank(owners, 0)
    placing = lax.broadcasted_iota(jnp.int32, (out.shape[0], DEC), 0) == target
    cache_slot = jnp.sum(jnp.where(placing, slot_ref[...] + 1, 0), axis=1, keepdims=True) - 1
    qkv = dot(conved, projection(w_ref, heads), ((1,), (1,))).astype(BF)
    sent = dot(ones_where(placing), qkv)
    lane = lax.broadcasted_iota(jnp.int32, sent.shape, 1)
    mark = 2 * heads * F + DH
    out[...] = jnp.where(lane == mark, cache_slot.astype(F32), sent).astype(BF)


def cache_spreaders(heads):
    lane, entry = lanes_of(PHI * heads)
    feature = lane >> (heads.bit_length() - 1)
    quad = feature - (1 + F)
    a = jnp.where(quad < 0, feature - 1, quad >> 4)
    return ones_where(a == entry), ones_where((quad >= 0) & ((quad & (F - 1)) == entry))


def slot_features(heads, items):
    mark = 2 * heads * F + DH
    first, second = cache_spreaders(heads)
    phis = []
    for head in range(heads):
        q = items[:, head * F : head * F + F]
        a = dot(q, first)
        b = dot(q, second)
        lane = lax.broadcasted_iota(jnp.int32, a.shape, 1)
        scale = jnp.where(lane < heads * (F + 1), 1.0 / math.sqrt(math.sqrt(F)), b * (1.0 / math.sqrt(2.0 * F)))
        value = jnp.where(lane < heads, 1.0, a * scale)
        phis.append(jnp.where((lane & (heads - 1)) == head, value, 0.0).astype(BF))
    slots = jnp.concatenate([items[:, mark : mark + 1].astype(F32)] * heads, axis=0)
    return jnp.concatenate(phis, axis=0), slots


def slot_copies(heads, start, count, cache_ref, state, sem):
    size = 2 * PHI * heads
    return [
        pltpu.make_async_copy(cache_ref.at[pl.ds(start * size // 2 + n * size, size)], state.at[pl.ds(n * size, size)], sem.at[n])
        for n in range(count // 2)
    ]


def slot_totals(heads, start, phis, slots, copies, state, total):
    span = PHI * heads
    waiting = list(copies)
    done = {}
    for n in range(2 * len(copies)):
        if n % 2 == 0:
            waiting.pop(0).wait()
        shift = n * span % 8
        rows = -(-(span + shift) // 8) * 8
        block = state[n * span - shift : n * span - shift + rows, :].astype(BF)
        done.setdefault(shift, []).append((n, block))
        if len(done[shift]) == 2:
            zeros = jnp.zeros((rows, WIDE - DH), BF)
            pair = [part for _, block in done[shift] for part in (block, zeros)]
            sides = [jnp.zeros((phis.shape[0], size), BF) for size in (shift, rows - span - shift)]
            wide = [side for side in (sides[0], phis, sides[1]) if side.shape[1] > 0]
            table = dot(jnp.concatenate(wide, axis=1), jnp.concatenate(pair, axis=1))
            for side, (place, _) in enumerate(done.pop(shift)):
                here = slots == float(start + place)
                total = total + jnp.where(here, table[:, side * WIDE : (side + 1) * WIDE], 0.0)
    return total


def serve_kernel(heads, items, cache_ref, total, state, sem):
    copies = slot_copies(heads, 0, 2 * sem.shape[0], cache_ref, state, sem)
    for copy in copies:
        copy.start()
    phis, slots = slot_features(heads, items)
    total[...] = slot_totals(heads, 0, phis, slots, copies, state, jnp.zeros(total.shape, F32))


def serve_part(heads, start, items, half_total, gain_ref, w_ref, copies, state, out):
    attended = []
    count = items.shape[0]
    phis, slots = slot_features(heads, items)
    total = slot_totals(heads, start, phis, slots, copies, state, half_total[...])
    gains = gain_ref[...].reshape(1, heads * DH)
    for head in range(heads):
        q = items[:, head * F : head * F + F].astype(F32)
        k = items[:, (heads + head) * F : (heads + head) * F + F].astype(F32)
        at = 2 * heads * F + head * WIDE
        v = items[:, at : at + DH].astype(F32)
        inner = jnp.sum(q * k, axis=-1, keepdims=True) * (1.0 / math.sqrt(F))
        value = total[head * count : (head + 1) * count, :DH] + (1.0 + inner + 0.5 * inner * inner) * v
        square = jnp.sum(value * value, axis=-1, keepdims=True)
        value = value * lax.rsqrt(square * (1.0 / DH) + 1e-05) * gains[:, head * DH : (head + 1) * DH]
        attended += [value.astype(BF), jnp.zeros((count, WIDE - DH), BF)]
    out[...] = dot(jnp.concatenate(attended, axis=1), out_projection(w_ref, heads)).astype(BF)


def return_kernel(capacity, items_ref, owner_ref, top0, one_x, low0, one_y, *outs):
    top, low = outs[4:]
    owners = owner_ref[...]
    target = column(owners) * capacity + placing_rank(owners, 1)
    placing = lax.broadcasted_iota(jnp.int32, (DEC, items_ref.shape[0]), 1) == target
    row = lax.broadcasted_iota(jnp.int32, (4 * TILE, DEC), 0)
    entry = lax.broadcasted_iota(jnp.int32, (4 * TILE, DEC), 1)
    device = lax.axis_index("head") ^ (row // TILE)
    wanted = ((row % TILE) < DEC // 4) & (entry == device * (DEC // 4) + row % TILE)
    wanted = dot(ones_where(wanted), ones_where(placing)).astype(BF)
    shares = dot(wanted, items_ref[...]).astype(BF)
    for slot, out in enumerate(outs[:4]):
        out[...] = shares[slot * TILE : (slot + 1) * TILE]
        out.push()
    top[...] = (top0[...].astype(F32) + one_x[...].astype(F32)).astype(BF)
    top.push()
    low[...] = (low0[...].astype(F32) + one_y[...].astype(F32)).astype(BF)


def far_off(array):
    return pltpu.with_memory_space_constraint(array, pltpu.HBM)


def entries(ref):
    return [ref.at[n] for n in range(ref.shape[0])]


class Fetched:
    def __init__(self, copies, place):
        self.copies, self.place, self.here = copies, place, set()
        self.shape, self.dtype = place.shape, place.dtype

    def __getitem__(self, index):
        entry = index[0] if isinstance(index, tuple) else index
        wanted = [entry] if len(self.copies) > 1 and isinstance(entry, int) else range(len(self.copies))
        for n in wanted:
            self.wait(n)
        return self.place[index]

    def wait(self, n):
        if n not in self.here:
            self.copies[n].wait()
            self.here.add(n)


class Pushed:
    def __init__(self, copies, place):
        self.copies, self.place, self.gone = copies, place, set()
        self.shape, self.dtype = place.shape, place.dtype

    def __getitem__(self, index):
        return self.place[index]

    def __setitem__(self, index, value):
        self.place[index] = value

    def push(self, entry=None):
        if (entry is None) == (len(self.copies) == 1):
            self.send(entry or 0)

    def send(self, n):
        if n not in self.gone:
            self.copies[n].start()
            self.gone.add(n)


class Near:
    def __init__(self, ref):
        self.ref, self.shape, self.dtype, self.copies = ref, ref.shape, ref.dtype, []

    def __getitem__(self, index):
        return self.ref[index]

    def __setitem__(self, index, value):
        self.ref[index] = value

    def push(self, entry=None):
        pass


def hbm_call(kernel, outs, flops, size, scalars=(), picked=None, waits=(), loose=(), here=(), near=(), split=(), split_out=(), raw=(), scratch=()):
    def run(*args):
        count, many = len(args), len(outs)
        moved = [n for n in range(count) if n not in here and n not in raw]
        far = [n for n in range(many) if n not in near]

        def shape_in(n):
            return args[n].shape[2:] if n == picked else args[n].shape

        pieces = sum(shape_in(n)[0] if n in split else 1 for n in moved)
        pieces += sum(outs[n].shape[0] if n in split_out else 1 for n in far)

        def body(*refs):
            refs = list(refs)

            def take(number):
                taken = refs[:number]
                del refs[:number]
                return taken

            numbers, sources, _, targets = take(len(scalars)), take(count), take(len(waits)), take(many)
            places, results, own, (sem,) = dict(zip(moved, take(len(moved)))), dict(zip(far, take(len(far)))), take(len(scratch)), refs
            used = iter(range(pieces))

            def copies(source, target, apart):
                pairs = zip(entries(source), entries(target)) if apart else [(source, target)]
                return [pltpu.make_async_copy(a, b, sem.at[next(used)]) for a, b in pairs]

            ins = []
            for n, source in enumerate(sources):
                if n in here or n in raw:
                    ins.append(source)
                    continue
                if n == picked:
                    source = source.at[0, numbers[-1][0]]
                fetched = Fetched(copies(source, places[n], n in split), places[n])
                for copy in fetched.copies:
                    copy.start()
                ins.append(fetched)
            done = [
                Pushed(copies(results[n], target, n in split_out), results[n]) if n in far else Near(target)
                for n, target in enumerate(targets)
            ]
            kernel(*numbers[: len(scalars) - (picked is not None)], *ins, *done, *own)
            for n in far:
                for entry in range(len(done[n].copies)):
                    done[n].send(entry)
            for n in moved:
                for entry in range(len(ins[n].copies)):
                    ins[n].wait(entry)
            for n in far:
                for copy in done[n].copies:
                    copy.wait()

        hbm = pl.BlockSpec(memory_space=pltpu.HBM)
        in_vmem = pl.BlockSpec(memory_space=pltpu.VMEM)
        anywhere = pl.BlockSpec(memory_space=pl.ANY)
        free = set(loose) | set(here)
        return pl.pallas_call(
            body,
            out_shape=[o if n in near else pltpu.HBM(o.shape, o.dtype) for n, o in enumerate(outs)],
            in_specs=[pl.BlockSpec(memory_space=pltpu.SMEM)] * len(scalars)
            + [in_vmem if n in here else anywhere if n in loose else hbm for n in range(count)]
            + [hbm] * len(waits),
            out_specs=[in_vmem if n in near else hbm for n in range(many)],
            scratch_shapes=[pltpu.VMEM(shape_in(n), args[n].dtype) for n in moved]
            + [pltpu.VMEM(outs[n].shape, outs[n].dtype) for n in far]
            + list(scratch)
            + [pltpu.SemaphoreType.DMA((pieces,))],
            compiler_params=pltpu.CompilerParams(vmem_limit_bytes=40 * MIB),
            cost_estimate=pl.CostEstimate(flops=flops, bytes_accessed=size, transcendentals=0),
        )(*scalars, *[a if n in free else far_off(a) for n, a in enumerate(args)], *map(far_off, waits))

    return run


def shape(*dims, dtype=BF):
    return jax.ShapeDtypeStruct(dims, dtype)


def across(array, by):
    return lax.ppermute(array, "head", [(i, i ^ by) for i in range(4)])


def local_square(
    stretch_tokens,
    stretch_tail,
    decode_tokens,
    decode_tail,
    norm_gain,
    conv_taps,
    qkv_weight,
    out_gain,
    out_weight,
    state_cache,
    stretch_len,
    stretch_slot,
    decode_slot,
    decode_owner,
):
    heads = qkv_weight.shape[1]
    rows = stretch_tokens.shape[1]
    half = rows // 2
    wide = heads * (2 * F + WIDE)
    w_in = jnp.transpose(qkv_weight, (1, 2, 0))
    cache = jnp.transpose(state_cache, (0, 1, 4, 2, 3))
    length = stretch_len.astype(jnp.int32)
    slot = stretch_slot.astype(jnp.int32)
    hbm = pl.BlockSpec(memory_space=pltpu.HBM)
    piece = shape(half, D)
    block_flops = 2 * rows * D * wide + 6 * heads * rows * rows * WIDE
    attend_flops = 2 * rows * heads * WIDE * (D + PHI_WIDE)
    size = 4 * rows * D

    low, top, begin, end = hbm_call(conv_kernel, [piece, piece, shape(TILE, D), shape(TILE, D)], 20 * rows * D, size)(
        stretch_tokens[0], stretch_tail[0], norm_gain, conv_taps
    )
    low_x = across(low, 1)
    low_y = across(low, 2)
    end = from_behind(end, "head", 1)

    groups = lax.axis_size("tok")
    capacity = max(2, 2 * DEC // groups)
    count = groups * capacity
    owner_row = decode_owner.reshape(1, DEC)
    (sent,) = hbm_call(functools.partial(send_kernel, heads, capacity), [shape(count, wide)], 2 * DEC * D * wide, 2 * D * wide)(
        decode_tokens[0], decode_tail[0], norm_gain, conv_taps, owner_row, decode_slot, w_in
    )
    top = pl.pallas_call(
        lambda first_ref, top_ref, begin_ref, end_ref, taps_ref, wait_ref, *refs: rim_kernel(
            first_ref, top_ref, begin_ref, end_ref, taps_ref, *refs
        ),
        out_shape=pltpu.HBM((half, D), BF),
        in_specs=[pl.BlockSpec(memory_space=pltpu.SMEM), hbm, hbm, pl.BlockSpec(memory_space=pl.ANY), hbm, hbm],
        out_specs=hbm,
        scratch_shapes=[pltpu.VMEM((TILE, D), BF), pltpu.VMEM((TILE, D), BF), pltpu.VMEM((3, D), F32), pltpu.VMEM((TILE, D), BF)]
        + [pltpu.SemaphoreType.DMA((4,))],
        input_output_aliases={1: 0},
        compiler_params=pltpu.CompilerParams(vmem_limit_bytes=40 * MIB),
        cost_estimate=pl.CostEstimate(flops=16 * D, bytes_accessed=128 * D, transcendentals=0),
    )(lax.axis_index("head").reshape(1), far_off(top), far_off(begin), end, far_off(conv_taps), far_off(sent))
    top_x = across(top, 1)
    top_y = across(top, 2)
    items = lax.all_to_all(sent.reshape(groups, capacity, wide), "tok", split_axis=0, concat_axis=0, tiled=True)

    sums, own, queries = shape(heads, PHI_WIDE, WIDE, dtype=F32), shape(heads, rows, WIDE, dtype=F32), shape(rows, heads * F)
    sums0, own0, queries0 = hbm_call(
        functools.partial(first_kernel, heads),
        [sums, own, queries],
        block_flops,
        size,
        scalars=[length],
    )(low, top, w_in)
    items = items.reshape(count, wide)
    slots = cache.shape[1]
    flat = cache.reshape(slots * PHI * heads, DH)
    states = [pltpu.VMEM((slots // 2 * PHI * heads, DH), F32), pltpu.SemaphoreType.DMA((slots // 4,))]
    serve_flops = slots * heads * heads * DH * PHI * count
    (half_total,) = hbm_call(
        functools.partial(serve_kernel, heads),
        [shape(heads * count, WIDE, dtype=F32)],
        serve_flops,
        2 * slots * heads * WIDE * PHI,
        loose=(0,),
        raw=(1,),
        scratch=states,
        waits=[queries0],
    )(items, flat)
    low_y, top_x, low_x = lax.optimization_barrier((low_y, top_x, low_x, half_total))[:3]
    low_xy = across(low_y, 1)
    top_xy = across(top_x, 2)
    blocks = shape(rows, wide)
    sums1, qkv1, sums2, qkv2, state3, served, old = hbm_call(
        functools.partial(second_kernel, heads),
        [sums, blocks, sums, blocks, shape(heads, PHI_WIDE, WIDE), shape(count, D), sums],
        2 * block_flops + serve_flops,
        2 * slots * heads * WIDE * PHI,
        scalars=[length, slot],
        picked=5,
        loose=(0, 1, 3, 4, 7),
        raw=(11,),
        scratch=states,
    )(low_x, top_x, w_in, low_y, top_y, cache, sums0, items, half_total, out_gain, out_weight, flat)
    top3, low3, qkv3 = hbm_call(
        functools.partial(third_kernel, heads),
        [piece, piece, blocks],
        block_flops + attend_flops,
        size,
        scalars=[length],
        loose=(0, 1),
        near=(0, 1),
        waits=[qkv2],
    )(low_xy, top_xy, w_in, state3, out_gain, out_weight)

    via_x = across(top3, 1)
    via_y = across(low3, 2)
    served = lax.optimization_barrier((served, top3))[0]
    returned = lax.all_to_all(served.reshape(groups, capacity, D), "tok", split_axis=0, concat_axis=0, tiled=True)
    returned = returned.reshape(count, D)
    top1, low1, top2, low2, sums3 = hbm_call(
        functools.partial(fourth_kernel, heads),
        [piece] * 4 + [sums],
        2 * attend_flops,
        size,
        scalars=[length],
    )(qkv3, qkv1, old, sums0, sums1, sums2, qkv2, out_gain, out_weight)
    one_x = across(top1, 1)
    one_y = across(low2, 2)
    two_y, two_x = hbm_call(add_kernel, [piece, piece], 0, size, here=(1, 3), near=(0, 1), waits=[top1])(top2, via_x, low1, via_y)
    top0, low0, state_next = hbm_call(
        functools.partial(fifth_kernel, heads),
        [piece] * 2 + [shape(1, PHI, heads, DH, dtype=F32)],
        attend_flops,
        size,
        scalars=[length],
        waits=[two_x],
    )(old, sums0, sums1, sums2, sums3, queries0, own0, out_gain, out_weight)
    *decoded, top0, low0 = hbm_call(
        functools.partial(return_kernel, capacity),
        [shape(TILE, D)] * 4 + [piece] * 2,
        2 * DEC * count * D,
        4 * count * D,
        loose=(0, 3, 5),
    )(returned, owner_row, top0, one_x, low0, one_y)
    shares = [decoded[0]] + [across(decoded[by], by) for by in (1, 2, 3)]
    two_y = across(two_y, 2)
    two_x = across(two_x, 1)
    state_next = jnp.transpose(state_next, (0, 2, 3, 1))
    (stretch_out,) = hbm_call(
        total_kernel,
        [shape(2, half, D)],
        0,
        8 * rows * D,
        loose=(1, 3),
        split_out=(0,),
        waits=[decoded[0]],
    )(top0, two_y, low0, two_x)
    shares = lax.optimization_barrier((*shares, stretch_out))[:4]
    decode_out = sum(share[: DEC // 4].astype(F32) for share in shares).astype(BF)
    return (stretch_out.reshape(1, rows, D), decode_out[None], state_next)


def from_behind(array, axis, by):
    peers = lax.axis_size(axis)
    pairs = [(i, i + by) for i in range(peers) if 0 <= i + by < peers]
    return lax.ppermute(array, axis, pairs)


def rms_rows(values, gain):
    values = values.astype(jnp.float32)
    factor = lax.rsqrt(jnp.mean(values * values, axis=-1, keepdims=True) + 1e-05)
    return values * factor * gain


def features(vectors):
    breadth = vectors.shape[-1]
    linear = vectors / math.sqrt(math.sqrt(breadth))
    outer = vectors[..., :, None] * vectors[..., None, :] / math.sqrt(2.0 * breadth)
    outer = outer.reshape(vectors.shape[:-1] + (breadth * breadth,))
    ones = jnp.ones(vectors.shape[:-1] + (1,), vectors.dtype)
    return jnp.concatenate([ones, linear, outer], axis=-1)


def convolve(tail, normed, conv_taps):
    joined = jnp.concatenate([tail, normed], axis=-2).astype(jnp.float32)
    span_rows = normed.shape[-2]
    total = conv_taps[0] * joined[..., 0:span_rows, :]
    total = total + conv_taps[1] * joined[..., 1 : span_rows + 1, :]
    total = total + conv_taps[2] * joined[..., 2 : span_rows + 2, :]
    return total.astype(jnp.bfloat16)


def decode_items(items, slot_items, cache_own, out_gain, head_count):
    item_count = items.shape[0]
    shaped = items.reshape(item_count, head_count, 2 * F + DH).astype(jnp.float32)
    queries = shaped[:, :, :F]
    key_feats = shaped[:, :, F : 2 * F]
    values = shaped[:, :, 2 * F :]
    slot_total = cache_own.shape[0]
    table = jnp.einsum(
        "nhp,shdp->nshd", features(queries), cache_own, precision=lax.Precision.HIGHEST
    )
    picker = (slot_items[:, None] == jnp.arange(slot_total)[None, :]).astype(jnp.float32)
    carried = jnp.einsum("ns,nshd->nhd", picker, table, precision=lax.Precision.HIGHEST)
    inner = jnp.sum(queries * key_feats, axis=-1) / math.sqrt(F)
    own_term = (1.0 + inner + 0.5 * inner * inner)[..., None] * values
    attended = rms_rows(carried + own_term, out_gain.reshape(head_count, DH))
    return attended.astype(jnp.bfloat16).reshape(item_count, head_count * DH)


def local(
    stretch_tokens,
    stretch_tail,
    decode_tokens,
    decode_tail,
    norm_gain,
    conv_taps,
    qkv_weight,
    out_gain,
    out_weight,
    state_cache,
    stretch_len,
    stretch_slot,
    decode_slot,
    decode_owner,
):
    head_count = qkv_weight.shape[1]
    block_width = qkv_weight.shape[2]
    rows_own = stretch_tokens.shape[1]
    w_flat = qkv_weight.reshape(D, head_count * block_width)
    gains = out_gain.reshape(head_count, DH)
    normed = rms_rows(stretch_tokens[0], norm_gain).astype(jnp.bfloat16)
    rim_rows = from_behind(normed[rows_own - 2 :], "head", 1)
    first_dev = lax.axis_index("head") == 0
    rim_rows = jnp.where(first_dev, stretch_tail[0], rim_rows)
    conved = convolve(rim_rows, normed, conv_taps)
    grouped = jnp.dot(
        lax.all_gather(conved, "head", axis=0, tiled=True),
        w_flat,
        preferred_element_type=jnp.float32,
    ).astype(jnp.bfloat16)
    grouped = grouped.reshape(STRETCH, head_count, block_width)
    queries = grouped[:, :, :F]
    key_feats = grouped[:, :, F : 2 * F]
    values = grouped[:, :, 2 * F :]
    length = stretch_len[0]
    positions = jnp.arange(STRETCH)
    valid_rows = positions < length
    state_old = lax.dynamic_index_in_dim(state_cache[0], stretch_slot[0], 0, keepdims=False)
    carried = jnp.einsum(
        "ihp,hdp->ihd",
        features(queries.astype(jnp.float32)),
        state_old,
        precision=lax.Precision.HIGHEST,
    )
    block_rows = min(512, STRETCH)
    pieces = []
    for anchor in range(0, STRETCH, block_rows):
        finish = anchor + block_rows
        inner = jnp.einsum(
            "ihf,jhf->hij",
            queries[anchor:finish],
            key_feats[:finish],
            preferred_element_type=jnp.float32,
        ) / math.sqrt(F)
        weights = 1.0 + inner + 0.5 * inner * inner
        allowed = (positions[None, :finish] <= positions[anchor:finish, None]) & valid_rows[
            None, :finish
        ]
        weights = jnp.where(allowed[None], weights, 0.0).astype(jnp.bfloat16)
        pieces.append(
            jnp.einsum("hij,jhd->ihd", weights, values[:finish], preferred_element_type=jnp.float32)
        )
    local_sum = jnp.concatenate(pieces, axis=0)
    attended = rms_rows(carried + local_sum, gains)
    attended = (
        jnp.where(valid_rows[:, None, None], attended, 0.0)
        .astype(jnp.bfloat16)
        .reshape(STRETCH, head_count * DH)
    )
    key_phi = jnp.where(
        valid_rows[:, None, None], features(key_feats.astype(jnp.float32)), 0.0
    ).astype(jnp.bfloat16)
    state_next = state_old + jnp.einsum(
        "jhd,jhp->hdp", values, key_phi, preferred_element_type=jnp.float32
    )
    part_rows = attended
    stretch_out = lax.psum_scatter(
        jnp.dot(part_rows, out_weight, preferred_element_type=jnp.float32).astype(jnp.bfloat16),
        "head",
        scatter_dimension=0,
        tiled=True,
    )
    dec_normed = rms_rows(decode_tokens[0], norm_gain).astype(jnp.bfloat16)
    dec_conved = convolve(decode_tail[0], dec_normed[:, None, :], conv_taps)[:, 0, :]
    dec_qkv = jnp.dot(dec_conved, w_flat, preferred_element_type=jnp.float32).astype(jnp.bfloat16)
    owners = decode_owner[0, :, 0]
    slots_here = decode_slot[0]
    groups = lax.axis_size("tok")
    capacity = max(2, 2 * DEC // groups)
    earlier = jnp.arange(DEC)[None, :] < jnp.arange(DEC)[:, None]
    same_owner = owners[None, :] == owners[:, None]
    rank_in = jnp.sum(earlier & same_owner, axis=1)
    target = owners * capacity + rank_in
    placing = jnp.arange(groups * capacity)[:, None] == target[None, :]
    sent_rows = jnp.dot(
        placing.astype(jnp.bfloat16), dec_qkv, preferred_element_type=jnp.float32
    ).astype(jnp.bfloat16)
    sent_rows = sent_rows.reshape(groups, capacity, head_count * block_width)
    sent_slots = jnp.sum(jnp.where(placing, slots_here[None, :] + 1, 0), axis=1) - 1
    sent_slots = sent_slots.reshape(groups, capacity)
    item_rows = lax.all_to_all(sent_rows, "tok", split_axis=0, concat_axis=0, tiled=True)
    item_slots = lax.all_to_all(sent_slots, "tok", split_axis=0, concat_axis=0, tiled=True)
    item_count = item_rows.shape[1]
    flat_out = decode_items(
        item_rows.reshape(groups * item_count, head_count * block_width),
        item_slots.reshape(groups * item_count),
        state_cache[0],
        out_gain,
        head_count,
    )
    served = flat_out.reshape(groups, item_count, head_count * DH)
    returned = lax.all_to_all(served, "tok", split_axis=0, concat_axis=0, tiled=True)
    dec_attended = jnp.dot(
        jnp.transpose(placing).astype(jnp.bfloat16),
        returned.reshape(groups * capacity, head_count * DH),
        preferred_element_type=jnp.float32,
    ).astype(jnp.bfloat16)
    part_rows = dec_attended
    decode_out = lax.psum_scatter(
        jnp.dot(part_rows, out_weight, preferred_element_type=jnp.float32).astype(jnp.bfloat16),
        "head",
        scatter_dimension=0,
        tiled=True,
    )
    return (stretch_out[None], decode_out[None], state_next[None])


def solution(mesh):
    in_specs = (
        P("tok", "head", None),
        P("tok", None, None),
        P("tok", None, None),
        P("tok", None, None, None),
        P(),
        P(),
        P(None, "head", None),
        P("head"),
        P("head", None),
        P("tok", None, "head", None, None),
        P("tok"),
        P("tok"),
        P("tok", None),
        P("tok", None, None),
    )
    out_specs = (P("tok", "head", None), P("tok", "head", None), P("tok", "head", None, None))
    chosen = local_square if mesh.shape["head"] == 4 else local
    return jax.shard_map(chosen, mesh=mesh, in_specs=in_specs, out_specs=out_specs, check_vma=False)
```

```python
import functools
import math

import jax
import jax.numpy as jnp
import numpy as np
from jax import lax
from jax.experimental import pallas as pl
from jax.experimental.pallas import tpu as pltpu
from jax.sharding import PartitionSpec as P

D = 1792
DH = 112
F = 16
STRETCH = 1024
DEC = 32
QUAD = F * F
PHI = 1 + F + QUAD
WIDE = 128
PHI_WIDE = QUAD + 128
TILE = 16
MIB = 1 << 20
BF = jnp.bfloat16
F32 = jnp.float32


def lanes_of(size):
    return lax.broadcasted_iota(jnp.int32, (F, size), 1), lax.broadcasted_iota(jnp.int32, (F, size), 0)


def ones_where(mask):
    return jnp.where(mask, 1.0, 0.0).astype(BF)


def spreader():
    lane, entry = lanes_of(PHI_WIDE)
    return ones_where(jnp.where(lane < QUAD, lane >> 4, lane & (F - 1)) == entry)


def dot(left, right, contract=((1,), (0,))):
    return lax.dot_general(left, right, (contract, ((), ())), preferred_element_type=F32)


def phi_of(vectors, pick):
    spread = dot(vectors, pick)
    a, b = spread[:, :QUAD], spread[:, QUAD:]
    quad = a * jnp.concatenate([b] * (QUAD // 128), axis=1) * (1.0 / math.sqrt(2.0 * F))
    lane = lax.broadcasted_iota(jnp.int32, b.shape, 1)
    rest = jnp.where(lane < F, b * (1.0 / math.sqrt(math.sqrt(F))), jnp.where(lane == F, 1.0, 0.0))
    return jnp.concatenate([quad, rest], axis=1)


def unit_rows(values):
    values = values.astype(F32)
    total = jnp.sum(values * values, axis=-1, keepdims=True)
    return values, lax.rsqrt(total * (1.0 / D) + 1e-05)


def column(row):
    size = row.shape[1]
    same = lax.broadcasted_iota(jnp.int32, (size, size), 0) == lax.broadcasted_iota(jnp.int32, (size, size), 1)
    return jnp.sum(jnp.where(same, row, 0), axis=1, keepdims=True)


def projection(w_ref, heads):
    pieces = [w_ref[h, :F, :] for h in range(heads)] + [w_ref[h, F : 2 * F, :] for h in range(heads)]
    for h in range(heads):
        pieces += [w_ref[h, 2 * F :, :], jnp.zeros((WIDE - DH, D), w_ref.dtype)]
    return jnp.concatenate(pieces, axis=0)


def out_projection(w_ref, heads):
    pieces = []
    for h in range(heads):
        pieces += [w_ref[h * DH : (h + 1) * DH, :], jnp.zeros((WIDE - DH, D), w_ref.dtype)]
    return jnp.concatenate(pieces, axis=0)


def conv_kernel(tokens_ref, tail_ref, gain_ref, taps_ref, low, top, begin, end):
    rows = tokens_ref.shape[0]
    half = rows // 2
    gain = gain_ref[...].reshape(1, D)
    taps = taps_ref[...]
    _, factor = unit_rows(tokens_ref[...])
    step = 256
    row = lax.broadcasted_iota(jnp.int32, (rows, step), 0)
    for at in range(0, D, step):
        cols = slice(at, at + step)
        normed = tokens_ref[:, cols].astype(F32) * factor * gain[:, cols]
        normed = normed.astype(BF)
        begin[:, cols] = normed[:16]
        end[:, cols] = normed[rows - 16 :]
        normed = normed.astype(F32)
        tail = tail_ref[:, cols].astype(F32)
        one = jnp.where(row == 0, tail[1:2], pltpu.roll(normed, 1, 0))
        two = pltpu.roll(normed, 2, 0)
        two = jnp.where(row == 0, tail[0:1], jnp.where(row == 1, tail[1:2], two))
        total = taps[0:1, cols] * two + taps[1:2, cols] * one + taps[2:3, cols] * normed
        total = total.astype(BF)
        top[:, cols] = total[:half]
        low[:, cols] = total[half:]


def rim_kernel(first_ref, top_ref, begin_ref, end_ref, taps_ref, out_ref, begin, end, taps, rows, sem):
    copies = [
        pltpu.make_async_copy(src, place, sem.at[n])
        for n, (src, place) in enumerate([(begin_ref, begin), (end_ref, end), (taps_ref, taps)])
    ]
    for copy in copies:
        copy.start()
    for copy in copies:
        copy.wait()
    now = begin[...].astype(F32)
    last = end[...].astype(F32)
    row = lax.broadcasted_iota(jnp.int32, now.shape, 0)
    one = jnp.where(row == 0, last[15:16], pltpu.roll(now, 1, 0))
    two = jnp.where(row == 0, last[14:15], jnp.where(row == 1, last[15:16], pltpu.roll(now, 2, 0)))
    rows[...] = (taps[0:1, :] * two + taps[1:2, :] * one + taps[2:3, :] * now).astype(BF)

    @pl.when(first_ref[0] != 0)
    def _():
        back = pltpu.make_async_copy(rows, out_ref.at[:16], sem.at[3])
        back.start()
        back.wait()


def qkv_of(heads, top, low, w_ref):
    conved = jnp.concatenate([top[...], low[...]], axis=0)
    return dot(conved, projection(w_ref, heads), ((1,), (1,))).astype(BF)


def parts_of(qkv, heads, head):
    at = 2 * heads * F + head * WIDE
    return qkv[:, head * F : (head + 1) * F], qkv[:, (heads + head) * F : (heads + head + 1) * F], qkv[:, at : at + WIDE]


def sums_of(slot, heads, head, length, qkv, pick):
    _, k, v = parts_of(qkv, heads, head)
    live = length - v.shape[0] * (lax.axis_index("head") ^ slot)
    live_row = lax.broadcasted_iota(jnp.int32, v.shape, 0) < live
    v = jnp.where(live_row, v.astype(F32), 0.0).astype(BF)
    return dot(phi_of(k, pick).astype(BF), v, ((0,), (0,)))


def own_of(slot, heads, head, length, qkv):
    q, k, v = parts_of(qkv, heads, head)
    rows = v.shape[0]
    live = length - rows * (lax.axis_index("head") ^ slot)
    row = lax.broadcasted_iota(jnp.int32, (rows, rows), 0)
    col = lax.broadcasted_iota(jnp.int32, (rows, rows), 1)
    shifted = dot(q, k, ((1,), (1,))) * (1.0 / math.sqrt(F)) + 1.0
    weights = jnp.where((col <= row) & (col < live), 0.5 * shifted * shifted + 0.5, 0.0).astype(BF)
    return dot(weights, v)


def old_state(cache_ref, head):
    pad = jnp.zeros((PHI_WIDE - PHI, DH), F32)
    old = [cache_ref[F + 1 :, head, :], cache_ref[1 : F + 1, head, :], cache_ref[0:1, head, :], pad]
    return jnp.concatenate([jnp.concatenate(old, axis=0), jnp.zeros((PHI_WIDE, WIDE - DH), F32)], axis=1)


def attend_part(slot, head, heads, length, q, own, state, gain_ref, pick):
    rows = q.shape[0]
    total = own + dot(phi_of(q, pick).astype(BF), state)
    square = jnp.sum(total * total, axis=-1, keepdims=True)
    gain = gain_ref[...].reshape(1, heads * DH)[:, head * DH : (head + 1) * DH]
    gain = jnp.concatenate([gain, jnp.zeros((1, WIDE - DH), F32)], axis=1)
    total = total * lax.rsqrt(square * (1.0 / DH) + 1e-05) * gain
    live = length - rows * (lax.axis_index("head") ^ slot)
    live_row = lax.broadcasted_iota(jnp.int32, (rows, WIDE), 0) < live
    return jnp.where(live_row, total, 0.0).astype(BF)


def project_part(parts, heads, w_ref, top, low):
    attended = jnp.concatenate(parts, axis=1)
    half = low.shape[0]
    w_out = out_projection(w_ref, heads)
    for out, rows in ((top, attended[:half]), (low, attended[half:])):
        out[...] = dot(rows, w_out).astype(BF)
        out.push()


def first_kernel(heads, len_ref, low, top, w_ref, sums, own, queries):
    qkv = qkv_of(heads, top, low, w_ref)
    pick = spreader()
    for head in range(heads):
        sums[head] = sums_of(0, heads, head, len_ref[0], qkv, pick)
    sums.push()
    for head in range(heads):
        own[head] = own_of(0, heads, head, len_ref[0], qkv)
    queries[...] = qkv[:, : heads * F]


def second_kernel(
    heads, len_ref, low1, top1, w_ref, low2, top2, cache, sums0, items, half_total, gain_ref, out_w_ref, cache_ref,
    sums1, qkv1, sums2, qkv2, state3, served, old, state, sem
):
    start = 2 * sem.shape[0]
    copies = slot_copies(heads, start, start, cache_ref, state, sem)
    pick = spreader()
    for slot, low, top, sums, qkv in ((1, low1, top1, sums1, qkv1), (2, low2, top2, sums2, qkv2)):
        found = qkv_of(heads, top, low, w_ref)
        if slot == 1:
            for copy in copies:
                copy.start()
        qkv[...] = found
        qkv.push()
        for head in range(heads):
            sums[head] = sums_of(slot, heads, head, len_ref[0], found, pick)
        sums.push()
    for head in range(heads):
        old[head] = old_state(cache, head)
        state3[head] = state_before(3, old[head], (sums0[head], sums1[head], sums2[head]))
    old.push()
    state3.push()
    serve_part(heads, start, items, half_total, gain_ref, out_w_ref, copies, state, served)


def state_before(slot, old, sums):
    mine = lax.axis_index("head")
    for other, part in enumerate(sums):
        if other != slot:
            old = old + ((mine ^ other) < (mine ^ slot)).astype(F32) * part
    return old.astype(BF)


def third_kernel(heads, len_ref, low, top, w_ref, state3, gain_ref, out_w_ref, top3, low3, qkv3):
    length = len_ref[0]
    qkv = qkv_of(heads, top, low, w_ref)
    qkv3[...] = qkv
    qkv3.push()
    pick = spreader()
    parts = []
    for head in range(heads):
        q = parts_of(qkv, heads, head)[0]
        own = own_of(3, heads, head, length, qkv)
        parts.append(attend_part(3, head, heads, length, q, own, state3[head], gain_ref, pick))
    project_part(parts, heads, out_w_ref, top3, low3)


def fourth_kernel(
    heads, len_ref, qkv3, qkv1, old, sums0, sums1, sums2, qkv2, gain_ref, out_w_ref, top1, low1, top2, low2, sums3
):
    pick = spreader()
    length = len_ref[0]
    for head in range(heads):
        sums3[head] = sums_of(3, heads, head, length, qkv3, pick)
    sums3.push()
    for slot, qkv, top, low in ((1, qkv1, top1, low1), (2, qkv2, top2, low2)):
        parts = []
        for head in range(heads):
            q = parts_of(qkv, heads, head)[0]
            own = own_of(slot, heads, head, length, qkv)
            state = state_before(slot, old[head], (sums0[head], sums1[head], sums2[head], sums3[head]))
            parts.append(attend_part(slot, head, heads, length, q, own, state, gain_ref, pick))
        project_part(parts, heads, out_w_ref, top, low)


def fifth_kernel(
    heads, len_ref, olds, sums0, sums1, sums2, sums3, queries, own, gain_ref, out_w_ref, top0, low0, state_next
):
    pick = spreader()
    parts = []
    for head in range(heads):
        old = olds[head]
        sums = [part[head] for part in (sums0, sums1, sums2, sums3)]
        q = queries[:, head * F : (head + 1) * F]
        state = state_before(0, old, sums)
        parts.append(attend_part(0, head, heads, len_ref[0], q, own[head], state, gain_ref, pick))
        new = (old + (sums[0] + sums[1]) + (sums[2] + sums[3]))[:, :DH]
        state_next[0, F + 1 :, head, :] = new[:QUAD]
        state_next[0, 1 : F + 1, head, :] = new[QUAD : QUAD + F]
        state_next[0, 0:1, head, :] = new[QUAD + F : QUAD + F + 1]
    project_part(parts, heads, out_w_ref, top0, low0)


def add_kernel(top2, via_x, low1, via_y, two_y, two_x):
    two_y[...] = (top2[...].astype(F32) + via_x[...].astype(F32)).astype(BF)
    two_x[...] = (low1[...].astype(F32) + via_y[...].astype(F32)).astype(BF)


def total_kernel(top0, two_y, low0, two_x, out):
    out[0] = (top0[...].astype(F32) + two_y[...].astype(F32)).astype(BF)
    out.push(0)
    out[1] = (low0[...].astype(F32) + two_x[...].astype(F32)).astype(BF)
    out.push(1)


def placing_rank(owners_row, axis):
    down = lax.broadcasted_iota(jnp.int32, (DEC, DEC), 0)
    along = lax.broadcasted_iota(jnp.int32, (DEC, DEC), 1)
    earlier = down < along if axis == 0 else along < down
    return jnp.sum(jnp.where(earlier & (column(owners_row) == owners_row), 1, 0), axis=axis, keepdims=True)


def send_kernel(heads, capacity, tokens_ref, tail_ref, gain_ref, taps_ref, owner_ref, slot_ref, w_ref, out):
    tokens, factor = unit_rows(tokens_ref[...])
    normed = (tokens * factor * gain_ref[...].reshape(1, D)).astype(BF).astype(F32)
    tail = tail_ref[...].astype(F32)
    taps = taps_ref[...]
    conved = taps[0:1, :] * tail[:, 0, :] + taps[1:2, :] * tail[:, 1, :]
    conved = (conved + taps[2:3, :] * normed).astype(BF)
    owners = owner_ref[...]
    target = owners * capacity + placing_rank(owners, 0)
    placing = lax.broadcasted_iota(jnp.int32, (out.shape[0], DEC), 0) == target
    cache_slot = jnp.sum(jnp.where(placing, slot_ref[...] + 1, 0), axis=1, keepdims=True) - 1
    qkv = dot(conved, projection(w_ref, heads), ((1,), (1,))).astype(BF)
    sent = dot(ones_where(placing), qkv)
    lane = lax.broadcasted_iota(jnp.int32, sent.shape, 1)
    mark = 2 * heads * F + DH
    out[...] = jnp.where(lane == mark, cache_slot.astype(F32), sent).astype(BF)


def cache_spreaders(heads):
    lane, entry = lanes_of(PHI * heads)
    feature = lane >> (heads.bit_length() - 1)
    quad = feature - (1 + F)
    a = jnp.where(quad < 0, feature - 1, quad >> 4)
    return ones_where(a == entry), ones_where((quad >= 0) & ((quad & (F - 1)) == entry))


def slot_features(heads, items):
    mark = 2 * heads * F + DH
    first, second = cache_spreaders(heads)
    phis = []
    for head in range(heads):
        q = items[:, head * F : head * F + F]
        a = dot(q, first)
        b = dot(q, second)
        lane = lax.broadcasted_iota(jnp.int32, a.shape, 1)
        scale = jnp.where(lane < heads * (F + 1), 1.0 / math.sqrt(math.sqrt(F)), b * (1.0 / math.sqrt(2.0 * F)))
        value = jnp.where(lane < heads, 1.0, a * scale)
        phis.append(jnp.where((lane & (heads - 1)) == head, value, 0.0).astype(BF))
    slots = jnp.concatenate([items[:, mark : mark + 1].astype(F32)] * heads, axis=0)
    return jnp.concatenate(phis, axis=0), slots


def slot_copies(heads, start, count, cache_ref, state, sem):
    size = 2 * PHI * heads
    return [
        pltpu.make_async_copy(cache_ref.at[pl.ds(start * size // 2 + n * size, size)], state.at[pl.ds(n * size, size)], sem.at[n])
        for n in range(count // 2)
    ]


def slot_totals(heads, start, phis, slots, copies, state, total):
    span = PHI * heads
    waiting = list(copies)
    done = {}
    for n in range(2 * len(copies)):
        if n % 2 == 0:
            waiting.pop(0).wait()
        shift = n * span % 8
        rows = -(-(span + shift) // 8) * 8
        block = state[n * span - shift : n * span - shift + rows, :].astype(BF)
        done.setdefault(shift, []).append((n, block))
        if len(done[shift]) == 2:
            zeros = jnp.zeros((rows, WIDE - DH), BF)
            pair = [part for _, block in done[shift] for part in (block, zeros)]
            sides = [jnp.zeros((phis.shape[0], size), BF) for size in (shift, rows - span - shift)]
            wide = [side for side in (sides[0], phis, sides[1]) if side.shape[1] > 0]
            table = dot(jnp.concatenate(wide, axis=1), jnp.concatenate(pair, axis=1))
            for side, (place, _) in enumerate(done.pop(shift)):
                here = slots == float(start + place)
                total = total + jnp.where(here, table[:, side * WIDE : (side + 1) * WIDE], 0.0)
    return total


def serve_kernel(heads, items, cache_ref, total, state, sem):
    copies = slot_copies(heads, 0, 2 * sem.shape[0], cache_ref, state, sem)
    for copy in copies:
        copy.start()
    phis, slots = slot_features(heads, items)
    total[...] = slot_totals(heads, 0, phis, slots, copies, state, jnp.zeros(total.shape, F32))


def serve_part(heads, start, items, half_total, gain_ref, w_ref, copies, state, out):
    attended = []
    count = items.shape[0]
    phis, slots = slot_features(heads, items)
    total = slot_totals(heads, start, phis, slots, copies, state, half_total[...])
    gains = gain_ref[...].reshape(1, heads * DH)
    for head in range(heads):
        q = items[:, head * F : head * F + F].astype(F32)
        k = items[:, (heads + head) * F : (heads + head) * F + F].astype(F32)
        at = 2 * heads * F + head * WIDE
        v = items[:, at : at + DH].astype(F32)
        inner = jnp.sum(q * k, axis=-1, keepdims=True) * (1.0 / math.sqrt(F))
        value = total[head * count : (head + 1) * count, :DH] + (1.0 + inner + 0.5 * inner * inner) * v
        square = jnp.sum(value * value, axis=-1, keepdims=True)
        value = value * lax.rsqrt(square * (1.0 / DH) + 1e-05) * gains[:, head * DH : (head + 1) * DH]
        attended += [value.astype(BF), jnp.zeros((count, WIDE - DH), BF)]
    out[...] = dot(jnp.concatenate(attended, axis=1), out_projection(w_ref, heads)).astype(BF)


def return_kernel(capacity, items_ref, owner_ref, top0, one_x, low0, one_y, *outs):
    top, low = outs[4:]
    owners = owner_ref[...]
    target = column(owners) * capacity + placing_rank(owners, 1)
    placing = lax.broadcasted_iota(jnp.int32, (DEC, items_ref.shape[0]), 1) == target
    row = lax.broadcasted_iota(jnp.int32, (4 * TILE, DEC), 0)
    entry = lax.broadcasted_iota(jnp.int32, (4 * TILE, DEC), 1)
    device = lax.axis_index("head") ^ (row // TILE)
    wanted = ((row % TILE) < DEC // 4) & (entry == device * (DEC // 4) + row % TILE)
    wanted = dot(ones_where(wanted), ones_where(placing)).astype(BF)
    shares = dot(wanted, items_ref[...]).astype(BF)
    for slot, out in enumerate(outs[:4]):
        out[...] = shares[slot * TILE : (slot + 1) * TILE]
        out.push()
    top[...] = (top0[...].astype(F32) + one_x[...].astype(F32)).astype(BF)
    top.push()
    low[...] = (low0[...].astype(F32) + one_y[...].astype(F32)).astype(BF)


def far_off(array):
    return pltpu.with_memory_space_constraint(array, pltpu.HBM)


def entries(ref):
    return [ref.at[n] for n in range(ref.shape[0])]


class Fetched:
    def __init__(self, copies, place):
        self.copies, self.place, self.here = copies, place, set()
        self.shape, self.dtype = place.shape, place.dtype

    def __getitem__(self, index):
        entry = index[0] if isinstance(index, tuple) else index
        wanted = [entry] if len(self.copies) > 1 and isinstance(entry, int) else range(len(self.copies))
        for n in wanted:
            self.wait(n)
        return self.place[index]

    def wait(self, n):
        if n not in self.here:
            self.copies[n].wait()
            self.here.add(n)


class Pushed:
    def __init__(self, copies, place):
        self.copies, self.place, self.gone = copies, place, set()
        self.shape, self.dtype = place.shape, place.dtype

    def __getitem__(self, index):
        return self.place[index]

    def __setitem__(self, index, value):
        self.place[index] = value

    def push(self, entry=None):
        if (entry is None) == (len(self.copies) == 1):
            self.send(entry or 0)

    def send(self, n):
        if n not in self.gone:
            self.copies[n].start()
            self.gone.add(n)


class Near:
    def __init__(self, ref):
        self.ref, self.shape, self.dtype, self.copies = ref, ref.shape, ref.dtype, []

    def __getitem__(self, index):
        return self.ref[index]

    def __setitem__(self, index, value):
        self.ref[index] = value

    def push(self, entry=None):
        pass


def hbm_call(kernel, outs, flops, size, scalars=(), picked=None, waits=(), loose=(), here=(), near=(), split=(), split_out=(), raw=(), scratch=()):
    def run(*args):
        count, many = len(args), len(outs)
        moved = [n for n in range(count) if n not in here and n not in raw]
        far = [n for n in range(many) if n not in near]

        def shape_in(n):
            return args[n].shape[2:] if n == picked else args[n].shape

        pieces = sum(shape_in(n)[0] if n in split else 1 for n in moved)
        pieces += sum(outs[n].shape[0] if n in split_out else 1 for n in far)

        def body(*refs):
            refs = list(refs)

            def take(number):
                taken = refs[:number]
                del refs[:number]
                return taken

            numbers, sources, _, targets = take(len(scalars)), take(count), take(len(waits)), take(many)
            places, results, own, (sem,) = dict(zip(moved, take(len(moved)))), dict(zip(far, take(len(far)))), take(len(scratch)), refs
            used = iter(range(pieces))

            def copies(source, target, apart):
                pairs = zip(entries(source), entries(target)) if apart else [(source, target)]
                return [pltpu.make_async_copy(a, b, sem.at[next(used)]) for a, b in pairs]

            ins = []
            for n, source in enumerate(sources):
                if n in here or n in raw:
                    ins.append(source)
                    continue
                if n == picked:
                    source = source.at[0, numbers[-1][0]]
                fetched = Fetched(copies(source, places[n], n in split), places[n])
                for copy in fetched.copies:
                    copy.start()
                ins.append(fetched)
            done = [
                Pushed(copies(results[n], target, n in split_out), results[n]) if n in far else Near(target)
                for n, target in enumerate(targets)
            ]
            kernel(*numbers[: len(scalars) - (picked is not None)], *ins, *done, *own)
            for n in far:
                for entry in range(len(done[n].copies)):
                    done[n].send(entry)
            for n in moved:
                for entry in range(len(ins[n].copies)):
                    ins[n].wait(entry)
            for n in far:
                for copy in done[n].copies:
                    copy.wait()

        hbm = pl.BlockSpec(memory_space=pltpu.HBM)
        in_vmem = pl.BlockSpec(memory_space=pltpu.VMEM)
        anywhere = pl.BlockSpec(memory_space=pl.ANY)
        free = set(loose) | set(here)
        return pl.pallas_call(
            body,
            out_shape=[o if n in near else pltpu.HBM(o.shape, o.dtype) for n, o in enumerate(outs)],
            in_specs=[pl.BlockSpec(memory_space=pltpu.SMEM)] * len(scalars)
            + [in_vmem if n in here else anywhere if n in loose else hbm for n in range(count)]
            + [hbm] * len(waits),
            out_specs=[in_vmem if n in near else hbm for n in range(many)],
            scratch_shapes=[pltpu.VMEM(shape_in(n), args[n].dtype) for n in moved]
            + [pltpu.VMEM(outs[n].shape, outs[n].dtype) for n in far]
            + list(scratch)
            + [pltpu.SemaphoreType.DMA((pieces,))],
            compiler_params=pltpu.CompilerParams(vmem_limit_bytes=40 * MIB),
            cost_estimate=pl.CostEstimate(flops=flops, bytes_accessed=size, transcendentals=0),
        )(*scalars, *[a if n in free else far_off(a) for n, a in enumerate(args)], *map(far_off, waits))

    return run


def shape(*dims, dtype=BF):
    return jax.ShapeDtypeStruct(dims, dtype)


def across(array, by):
    return lax.ppermute(array, "head", [(i, i ^ by) for i in range(4)])


def local_square(
    stretch_tokens,
    stretch_tail,
    decode_tokens,
    decode_tail,
    norm_gain,
    conv_taps,
    qkv_weight,
    out_gain,
    out_weight,
    state_cache,
    stretch_len,
    stretch_slot,
    decode_slot,
    decode_owner,
):
    heads = qkv_weight.shape[1]
    rows = stretch_tokens.shape[1]
    half = rows // 2
    wide = heads * (2 * F + WIDE)
    w_in = jnp.transpose(qkv_weight, (1, 2, 0))
    cache = jnp.transpose(state_cache, (0, 1, 4, 2, 3))
    length = stretch_len.astype(jnp.int32)
    slot = stretch_slot.astype(jnp.int32)
    hbm = pl.BlockSpec(memory_space=pltpu.HBM)
    piece = shape(half, D)
    block_flops = 2 * rows * D * wide + 6 * heads * rows * rows * WIDE
    attend_flops = 2 * rows * heads * WIDE * (D + PHI_WIDE)
    size = 4 * rows * D

    low, top, begin, end = hbm_call(conv_kernel, [piece, piece, shape(TILE, D), shape(TILE, D)], 20 * rows * D, size)(
        stretch_tokens[0], stretch_tail[0], norm_gain, conv_taps
    )
    low_x = across(low, 1)
    low_y = across(low, 2)
    end = from_behind(end, "head", 1)

    groups = lax.axis_size("tok")
    capacity = max(2, 2 * DEC // groups)
    count = groups * capacity
    owner_row = decode_owner.reshape(1, DEC)
    (sent,) = hbm_call(functools.partial(send_kernel, heads, capacity), [shape(count, wide)], 2 * DEC * D * wide, 2 * D * wide)(
        decode_tokens[0], decode_tail[0], norm_gain, conv_taps, owner_row, decode_slot, w_in
    )
    top = pl.pallas_call(
        lambda first_ref, top_ref, begin_ref, end_ref, taps_ref, wait_ref, *refs: rim_kernel(
            first_ref, top_ref, begin_ref, end_ref, taps_ref, *refs
        ),
        out_shape=pltpu.HBM((half, D), BF),
        in_specs=[pl.BlockSpec(memory_space=pltpu.SMEM), hbm, hbm, pl.BlockSpec(memory_space=pl.ANY), hbm, hbm],
        out_specs=hbm,
        scratch_shapes=[pltpu.VMEM((TILE, D), BF), pltpu.VMEM((TILE, D), BF), pltpu.VMEM((3, D), F32), pltpu.VMEM((TILE, D), BF)]
        + [pltpu.SemaphoreType.DMA((4,))],
        input_output_aliases={1: 0},
        compiler_params=pltpu.CompilerParams(vmem_limit_bytes=40 * MIB),
        cost_estimate=pl.CostEstimate(flops=16 * D, bytes_accessed=128 * D, transcendentals=0),
    )(lax.axis_index("head").reshape(1), far_off(top), far_off(begin), end, far_off(conv_taps), far_off(sent))
    top_x = across(top, 1)
    top_y = across(top, 2)
    items = lax.all_to_all(sent.reshape(groups, capacity, wide), "tok", split_axis=0, concat_axis=0, tiled=True)

    sums, own, queries = shape(heads, PHI_WIDE, WIDE, dtype=F32), shape(heads, rows, WIDE, dtype=F32), shape(rows, heads * F)
    sums0, own0, queries0 = hbm_call(
        functools.partial(first_kernel, heads),
        [sums, own, queries],
        block_flops,
        size,
        scalars=[length],
    )(low, top, w_in)
    items = items.reshape(count, wide)
    slots = cache.shape[1]
    flat = cache.reshape(slots * PHI * heads, DH)
    states = [pltpu.VMEM((slots // 2 * PHI * heads, DH), F32), pltpu.SemaphoreType.DMA((slots // 4,))]
    serve_flops = slots * heads * heads * DH * PHI * count
    (half_total,) = hbm_call(
        functools.partial(serve_kernel, heads),
        [shape(heads * count, WIDE, dtype=F32)],
        serve_flops,
        2 * slots * heads * WIDE * PHI,
        loose=(0,),
        raw=(1,),
        scratch=states,
        waits=[queries0],
    )(items, flat)
    low_y, top_x, low_x = lax.optimization_barrier((low_y, top_x, low_x, half_total))[:3]
    low_xy = across(low_y, 1)
    top_xy = across(top_x, 2)
    blocks = shape(rows, wide)
    sums1, qkv1, sums2, qkv2, state3, served, old = hbm_call(
        functools.partial(second_kernel, heads),
        [sums, blocks, sums, blocks, shape(heads, PHI_WIDE, WIDE), shape(count, D), sums],
        2 * block_flops + serve_flops,
        2 * slots * heads * WIDE * PHI,
        scalars=[length, slot],
        picked=5,
        loose=(0, 1, 3, 4, 7),
        here=(2,),
        raw=(11,),
        scratch=states,
    )(low_x, top_x, w_in, low_y, top_y, cache, sums0, items, half_total, out_gain, out_weight, flat)
    top3, low3, qkv3 = hbm_call(
        functools.partial(third_kernel, heads),
        [piece, piece, blocks],
        block_flops + attend_flops,
        size,
        scalars=[length],
        loose=(0, 1),
        near=(0, 1),
        here=(2, 5),
        waits=[qkv2],
    )(low_xy, top_xy, w_in, state3, out_gain, out_weight)

    via_x = across(top3, 1)
    via_y = across(low3, 2)
    served = lax.optimization_barrier((served, top3))[0]
    returned = lax.all_to_all(served.reshape(groups, capacity, D), "tok", split_axis=0, concat_axis=0, tiled=True)
    returned = returned.reshape(count, D)
    top1, low1, top2, low2, sums3 = hbm_call(
        functools.partial(fourth_kernel, heads),
        [piece] * 4 + [sums],
        2 * attend_flops,
        size,
        scalars=[length],
        here=(8,),
    )(qkv3, qkv1, old, sums0, sums1, sums2, qkv2, out_gain, out_weight)
    one_x = across(top1, 1)
    one_y = across(low2, 2)
    two_y, two_x = hbm_call(add_kernel, [piece, piece], 0, size, here=(1, 3), near=(0, 1), waits=[top1])(top2, via_x, low1, via_y)
    top0, low0, state_next = hbm_call(
        functools.partial(fifth_kernel, heads),
        [piece] * 2 + [shape(1, PHI, heads, DH, dtype=F32)],
        attend_flops,
        size,
        scalars=[length],
        waits=[two_x],
    )(old, sums0, sums1, sums2, sums3, queries0, own0, out_gain, out_weight)
    *decoded, top0, low0 = hbm_call(
        functools.partial(return_kernel, capacity),
        [shape(TILE, D)] * 4 + [piece] * 2,
        2 * DEC * count * D,
        4 * count * D,
        loose=(0, 3, 5),
    )(returned, owner_row, top0, one_x, low0, one_y)
    shares = [decoded[0]] + [across(decoded[by], by) for by in (1, 2, 3)]
    two_y = across(two_y, 2)
    two_x = across(two_x, 1)
    state_next = jnp.transpose(state_next, (0, 2, 3, 1))
    (stretch_out,) = hbm_call(
        total_kernel,
        [shape(2, half, D)],
        0,
        8 * rows * D,
        loose=(1, 3),
        split_out=(0,),
        waits=[decoded[0]],
    )(top0, two_y, low0, two_x)
    shares = lax.optimization_barrier((*shares, stretch_out))[:4]
    decode_out = sum(share[: DEC // 4].astype(F32) for share in shares).astype(BF)
    return (stretch_out.reshape(1, rows, D), decode_out[None], state_next)


def from_behind(array, axis, by):
    peers = lax.axis_size(axis)
    pairs = [(i, i + by) for i in range(peers) if 0 <= i + by < peers]
    return lax.ppermute(array, axis, pairs)


def rms_rows(values, gain):
    values = values.astype(jnp.float32)
    factor = lax.rsqrt(jnp.mean(values * values, axis=-1, keepdims=True) + 1e-05)
    return values * factor * gain


def features(vectors):
    breadth = vectors.shape[-1]
    linear = vectors / math.sqrt(math.sqrt(breadth))
    outer = vectors[..., :, None] * vectors[..., None, :] / math.sqrt(2.0 * breadth)
    outer = outer.reshape(vectors.shape[:-1] + (breadth * breadth,))
    ones = jnp.ones(vectors.shape[:-1] + (1,), vectors.dtype)
    return jnp.concatenate([ones, linear, outer], axis=-1)


def convolve(tail, normed, conv_taps):
    joined = jnp.concatenate([tail, normed], axis=-2).astype(jnp.float32)
    span_rows = normed.shape[-2]
    total = conv_taps[0] * joined[..., 0:span_rows, :]
    total = total + conv_taps[1] * joined[..., 1 : span_rows + 1, :]
    total = total + conv_taps[2] * joined[..., 2 : span_rows + 2, :]
    return total.astype(jnp.bfloat16)


def decode_items(items, slot_items, cache_own, out_gain, head_count):
    item_count = items.shape[0]
    shaped = items.reshape(item_count, head_count, 2 * F + DH).astype(jnp.float32)
    queries = shaped[:, :, :F]
    key_feats = shaped[:, :, F : 2 * F]
    values = shaped[:, :, 2 * F :]
    slot_total = cache_own.shape[0]
    table = jnp.einsum(
        "nhp,shdp->nshd", features(queries), cache_own, precision=lax.Precision.HIGHEST
    )
    picker = (slot_items[:, None] == jnp.arange(slot_total)[None, :]).astype(jnp.float32)
    carried = jnp.einsum("ns,nshd->nhd", picker, table, precision=lax.Precision.HIGHEST)
    inner = jnp.sum(queries * key_feats, axis=-1) / math.sqrt(F)
    own_term = (1.0 + inner + 0.5 * inner * inner)[..., None] * values
    attended = rms_rows(carried + own_term, out_gain.reshape(head_count, DH))
    return attended.astype(jnp.bfloat16).reshape(item_count, head_count * DH)


def local(
    stretch_tokens,
    stretch_tail,
    decode_tokens,
    decode_tail,
    norm_gain,
    conv_taps,
    qkv_weight,
    out_gain,
    out_weight,
    state_cache,
    stretch_len,
    stretch_slot,
    decode_slot,
    decode_owner,
):
    head_count = qkv_weight.shape[1]
    block_width = qkv_weight.shape[2]
    rows_own = stretch_tokens.shape[1]
    w_flat = qkv_weight.reshape(D, head_count * block_width)
    gains = out_gain.reshape(head_count, DH)
    normed = rms_rows(stretch_tokens[0], norm_gain).astype(jnp.bfloat16)
    rim_rows = from_behind(normed[rows_own - 2 :], "head", 1)
    first_dev = lax.axis_index("head") == 0
    rim_rows = jnp.where(first_dev, stretch_tail[0], rim_rows)
    conved = convolve(rim_rows, normed, conv_taps)
    grouped = jnp.dot(
        lax.all_gather(conved, "head", axis=0, tiled=True),
        w_flat,
        preferred_element_type=jnp.float32,
    ).astype(jnp.bfloat16)
    grouped = grouped.reshape(STRETCH, head_count, block_width)
    queries = grouped[:, :, :F]
    key_feats = grouped[:, :, F : 2 * F]
    values = grouped[:, :, 2 * F :]
    length = stretch_len[0]
    positions = jnp.arange(STRETCH)
    valid_rows = positions < length
    state_old = lax.dynamic_index_in_dim(state_cache[0], stretch_slot[0], 0, keepdims=False)
    carried = jnp.einsum(
        "ihp,hdp->ihd",
        features(queries.astype(jnp.float32)),
        state_old,
        precision=lax.Precision.HIGHEST,
    )
    block_rows = min(512, STRETCH)
    pieces = []
    for anchor in range(0, STRETCH, block_rows):
        finish = anchor + block_rows
        inner = jnp.einsum(
            "ihf,jhf->hij",
            queries[anchor:finish],
            key_feats[:finish],
            preferred_element_type=jnp.float32,
        ) / math.sqrt(F)
        weights = 1.0 + inner + 0.5 * inner * inner
        allowed = (positions[None, :finish] <= positions[anchor:finish, None]) & valid_rows[
            None, :finish
        ]
        weights = jnp.where(allowed[None], weights, 0.0).astype(jnp.bfloat16)
        pieces.append(
            jnp.einsum("hij,jhd->ihd", weights, values[:finish], preferred_element_type=jnp.float32)
        )
    local_sum = jnp.concatenate(pieces, axis=0)
    attended = rms_rows(carried + local_sum, gains)
    attended = (
        jnp.where(valid_rows[:, None, None], attended, 0.0)
        .astype(jnp.bfloat16)
        .reshape(STRETCH, head_count * DH)
    )
    key_phi = jnp.where(
        valid_rows[:, None, None], features(key_feats.astype(jnp.float32)), 0.0
    ).astype(jnp.bfloat16)
    state_next = state_old + jnp.einsum(
        "jhd,jhp->hdp", values, key_phi, preferred_element_type=jnp.float32
    )
    part_rows = attended
    stretch_out = lax.psum_scatter(
        jnp.dot(part_rows, out_weight, preferred_element_type=jnp.float32).astype(jnp.bfloat16),
        "head",
        scatter_dimension=0,
        tiled=True,
    )
    dec_normed = rms_rows(decode_tokens[0], norm_gain).astype(jnp.bfloat16)
    dec_conved = convolve(decode_tail[0], dec_normed[:, None, :], conv_taps)[:, 0, :]
    dec_qkv = jnp.dot(dec_conved, w_flat, preferred_element_type=jnp.float32).astype(jnp.bfloat16)
    owners = decode_owner[0, :, 0]
    slots_here = decode_slot[0]
    groups = lax.axis_size("tok")
    capacity = max(2, 2 * DEC // groups)
    earlier = jnp.arange(DEC)[None, :] < jnp.arange(DEC)[:, None]
    same_owner = owners[None, :] == owners[:, None]
    rank_in = jnp.sum(earlier & same_owner, axis=1)
    target = owners * capacity + rank_in
    placing = jnp.arange(groups * capacity)[:, None] == target[None, :]
    sent_rows = jnp.dot(
        placing.astype(jnp.bfloat16), dec_qkv, preferred_element_type=jnp.float32
    ).astype(jnp.bfloat16)
    sent_rows = sent_rows.reshape(groups, capacity, head_count * block_width)
    sent_slots = jnp.sum(jnp.where(placing, slots_here[None, :] + 1, 0), axis=1) - 1
    sent_slots = sent_slots.reshape(groups, capacity)
    item_rows = lax.all_to_all(sent_rows, "tok", split_axis=0, concat_axis=0, tiled=True)
    item_slots = lax.all_to_all(sent_slots, "tok", split_axis=0, concat_axis=0, tiled=True)
    item_count = item_rows.shape[1]
    flat_out = decode_items(
        item_rows.reshape(groups * item_count, head_count * block_width),
        item_slots.reshape(groups * item_count),
        state_cache[0],
        out_gain,
        head_count,
    )
    served = flat_out.reshape(groups, item_count, head_count * DH)
    returned = lax.all_to_all(served, "tok", split_axis=0, concat_axis=0, tiled=True)
    dec_attended = jnp.dot(
        jnp.transpose(placing).astype(jnp.bfloat16),
        returned.reshape(groups * capacity, head_count * DH),
        preferred_element_type=jnp.float32,
    ).astype(jnp.bfloat16)
    part_rows = dec_attended
    decode_out = lax.psum_scatter(
        jnp.dot(part_rows, out_weight, preferred_element_type=jnp.float32).astype(jnp.bfloat16),
        "head",
        scatter_dimension=0,
        tiled=True,
    )
    return (stretch_out[None], decode_out[None], state_next[None])


def solution(mesh):
    in_specs = (
        P("tok", "head", None),
        P("tok", None, None),
        P("tok", None, None),
        P("tok", None, None, None),
        P(),
        P(),
        P(None, "head", None),
        P("head"),
        P("head", None),
        P("tok", None, "head", None, None),
        P("tok"),
        P("tok"),
        P("tok", None),
        P("tok", None, None),
    )
    out_specs = (P("tok", "head", None), P("tok", "head", None), P("tok", "head", None, None))
    chosen = local_square if mesh.shape["head"] == 4 else local
    return jax.shard_map(chosen, mesh=mesh, in_specs=in_specs, out_specs=out_specs, check_vma=False)
```

```python
import functools
import math

import jax
import jax.numpy as jnp
import numpy as np
from jax import lax
from jax.experimental import pallas as pl
from jax.experimental.pallas import tpu as pltpu
from jax.sharding import PartitionSpec as P

D = 1792
DH = 112
F = 16
STRETCH = 1024
DEC = 32
QUAD = F * F
PHI = 1 + F + QUAD
WIDE = 128
PHI_WIDE = QUAD + 128
TILE = 16
MIB = 1 << 20
BF = jnp.bfloat16
F32 = jnp.float32


def lanes_of(size):
    return lax.broadcasted_iota(jnp.int32, (F, size), 1), lax.broadcasted_iota(jnp.int32, (F, size), 0)


def ones_where(mask):
    return jnp.where(mask, 1.0, 0.0).astype(BF)


def spreader():
    lane, entry = lanes_of(PHI_WIDE)
    return ones_where(jnp.where(lane < QUAD, lane >> 4, lane & (F - 1)) == entry)


def dot(left, right, contract=((1,), (0,))):
    return lax.dot_general(left, right, (contract, ((), ())), preferred_element_type=F32)


def phi_of(vectors, pick):
    spread = dot(vectors, pick)
    a, b = spread[:, :QUAD], spread[:, QUAD:]
    quad = a * jnp.concatenate([b] * (QUAD // 128), axis=1) * (1.0 / math.sqrt(2.0 * F))
    lane = lax.broadcasted_iota(jnp.int32, b.shape, 1)
    rest = jnp.where(lane < F, b * (1.0 / math.sqrt(math.sqrt(F))), jnp.where(lane == F, 1.0, 0.0))
    return jnp.concatenate([quad, rest], axis=1)


def unit_rows(values):
    values = values.astype(F32)
    total = jnp.sum(values * values, axis=-1, keepdims=True)
    return values, lax.rsqrt(total * (1.0 / D) + 1e-05)


def column(row):
    size = row.shape[1]
    same = lax.broadcasted_iota(jnp.int32, (size, size), 0) == lax.broadcasted_iota(jnp.int32, (size, size), 1)
    return jnp.sum(jnp.where(same, row, 0), axis=1, keepdims=True)


def projection(w_ref, heads):
    pieces = [w_ref[h, :F, :] for h in range(heads)] + [w_ref[h, F : 2 * F, :] for h in range(heads)]
    for h in range(heads):
        pieces += [w_ref[h, 2 * F :, :], jnp.zeros((WIDE - DH, D), w_ref.dtype)]
    return jnp.concatenate(pieces, axis=0)


def out_projection(w_ref, heads):
    pieces = []
    for h in range(heads):
        pieces += [w_ref[h * DH : (h + 1) * DH, :], jnp.zeros((WIDE - DH, D), w_ref.dtype)]
    return jnp.concatenate(pieces, axis=0)


def conv_kernel(tokens_ref, tail_ref, gain_ref, taps_ref, low, top, begin, end):
    rows = tokens_ref.shape[0]
    half = rows // 2
    gain = gain_ref[...].reshape(1, D)
    taps = taps_ref[...]
    _, factor = unit_rows(tokens_ref[...])
    step = 256
    row = lax.broadcasted_iota(jnp.int32, (rows, step), 0)
    for at in range(0, D, step):
        cols = slice(at, at + step)
        normed = tokens_ref[:, cols].astype(F32) * factor * gain[:, cols]
        normed = normed.astype(BF)
        begin[:, cols] = normed[:16]
        end[:, cols] = normed[rows - 16 :]
        normed = normed.astype(F32)
        tail = tail_ref[:, cols].astype(F32)
        one = jnp.where(row == 0, tail[1:2], pltpu.roll(normed, 1, 0))
        two = pltpu.roll(normed, 2, 0)
        two = jnp.where(row == 0, tail[0:1], jnp.where(row == 1, tail[1:2], two))
        total = taps[0:1, cols] * two + taps[1:2, cols] * one + taps[2:3, cols] * normed
        total = total.astype(BF)
        top[:, cols] = total[:half]
        low[:, cols] = total[half:]


def rim_kernel(first_ref, top_ref, begin_ref, end_ref, taps_ref, out_ref, begin, end, taps, rows, sem):
    copies = [
        pltpu.make_async_copy(src, place, sem.at[n])
        for n, (src, place) in enumerate([(begin_ref, begin), (end_ref, end), (taps_ref, taps)])
    ]
    for copy in copies:
        copy.start()
    for copy in copies:
        copy.wait()
    now = begin[...].astype(F32)
    last = end[...].astype(F32)
    row = lax.broadcasted_iota(jnp.int32, now.shape, 0)
    one = jnp.where(row == 0, last[15:16], pltpu.roll(now, 1, 0))
    two = jnp.where(row == 0, last[14:15], jnp.where(row == 1, last[15:16], pltpu.roll(now, 2, 0)))
    rows[...] = (taps[0:1, :] * two + taps[1:2, :] * one + taps[2:3, :] * now).astype(BF)

    @pl.when(first_ref[0] != 0)
    def _():
        back = pltpu.make_async_copy(rows, out_ref.at[:16], sem.at[3])
        back.start()
        back.wait()


def qkv_of(heads, top, low, w_ref):
    conved = jnp.concatenate([top[...], low[...]], axis=0)
    return dot(conved, projection(w_ref, heads), ((1,), (1,))).astype(BF)


def parts_of(qkv, heads, head):
    at = 2 * heads * F + head * WIDE
    return qkv[:, head * F : (head + 1) * F], qkv[:, (heads + head) * F : (heads + head + 1) * F], qkv[:, at : at + WIDE]


def sums_of(slot, heads, head, length, qkv, pick):
    _, k, v = parts_of(qkv, heads, head)
    live = length - v.shape[0] * (lax.axis_index("head") ^ slot)
    live_row = lax.broadcasted_iota(jnp.int32, v.shape, 0) < live
    v = jnp.where(live_row, v.astype(F32), 0.0).astype(BF)
    return dot(phi_of(k, pick).astype(BF), v, ((0,), (0,)))


def own_of(slot, heads, head, length, qkv):
    q, k, v = parts_of(qkv, heads, head)
    rows = v.shape[0]
    live = length - rows * (lax.axis_index("head") ^ slot)
    row = lax.broadcasted_iota(jnp.int32, (rows, rows), 0)
    col = lax.broadcasted_iota(jnp.int32, (rows, rows), 1)
    shifted = dot(q, k, ((1,), (1,))) * (1.0 / math.sqrt(F)) + 1.0
    weights = jnp.where((col <= row) & (col < live), 0.5 * shifted * shifted + 0.5, 0.0).astype(BF)
    return dot(weights, v)


def old_state(cache_ref, head):
    pad = jnp.zeros((PHI_WIDE - PHI, DH), F32)
    old = [cache_ref[F + 1 :, head, :], cache_ref[1 : F + 1, head, :], cache_ref[0:1, head, :], pad]
    return jnp.concatenate([jnp.concatenate(old, axis=0), jnp.zeros((PHI_WIDE, WIDE - DH), F32)], axis=1)


def attend_part(slot, head, heads, length, q, own, state, gain_ref, pick):
    rows = q.shape[0]
    total = own + dot(phi_of(q, pick).astype(BF), state)
    square = jnp.sum(total * total, axis=-1, keepdims=True)
    gain = gain_ref[...].reshape(1, heads * DH)[:, head * DH : (head + 1) * DH]
    gain = jnp.concatenate([gain, jnp.zeros((1, WIDE - DH), F32)], axis=1)
    total = total * lax.rsqrt(square * (1.0 / DH) + 1e-05) * gain
    live = length - rows * (lax.axis_index("head") ^ slot)
    live_row = lax.broadcasted_iota(jnp.int32, (rows, WIDE), 0) < live
    return jnp.where(live_row, total, 0.0).astype(BF)


def project_part(parts, heads, w_ref, top, low):
    attended = jnp.concatenate(parts, axis=1)
    half = low.shape[0]
    w_out = out_projection(w_ref, heads)
    for out, rows in ((top, attended[:half]), (low, attended[half:])):
        out[...] = dot(rows, w_out).astype(BF)
        out.push()


def first_kernel(heads, len_ref, low, top, w_ref, sums, own, queries):
    qkv = qkv_of(heads, top, low, w_ref)
    pick = spreader()
    for head in range(heads):
        sums[head] = sums_of(0, heads, head, len_ref[0], qkv, pick)
    sums.push()
    for head in range(heads):
        own[head] = own_of(0, heads, head, len_ref[0], qkv)
    queries[...] = qkv[:, : heads * F]


def second_kernel(
    heads, len_ref, low1, top1, w_ref, low2, top2, cache, sums0, items, half_total, gain_ref, out_w_ref, cache_ref,
    sums1, qkv1, sums2, qkv2, state3, served, old, state, sem
):
    start = 2 * sem.shape[0]
    copies = slot_copies(heads, start, start, cache_ref, state, sem)
    pick = spreader()
    for slot, low, top, sums, qkv in ((1, low1, top1, sums1, qkv1), (2, low2, top2, sums2, qkv2)):
        found = qkv_of(heads, top, low, w_ref)
        if slot == 1:
            for copy in copies:
                copy.start()
        qkv[...] = found
        qkv.push()
        for head in range(heads):
            sums[head] = sums_of(slot, heads, head, len_ref[0], found, pick)
        sums.push()
    for head in range(heads):
        old[head] = old_state(cache, head)
        state3[head] = state_before(3, old[head], (sums0[head], sums1[head], sums2[head]))
    old.push()
    state3.push()
    serve_part(heads, start, items, half_total, gain_ref, out_w_ref, copies, state, served)


def state_before(slot, old, sums):
    mine = lax.axis_index("head")
    for other, part in enumerate(sums):
        if other != slot:
            old = old + ((mine ^ other) < (mine ^ slot)).astype(F32) * part
    return old.astype(BF)


def third_kernel(heads, len_ref, low, top, w_ref, state3, gain_ref, out_w_ref, top3, low3, qkv3):
    length = len_ref[0]
    qkv = qkv_of(heads, top, low, w_ref)
    qkv3[...] = qkv
    qkv3.push()
    pick = spreader()
    parts = []
    for head in range(heads):
        q = parts_of(qkv, heads, head)[0]
        own = own_of(3, heads, head, length, qkv)
        parts.append(attend_part(3, head, heads, length, q, own, state3[head], gain_ref, pick))
    project_part(parts, heads, out_w_ref, top3, low3)


def fourth_kernel(
    heads, len_ref, qkv3, qkv1, old, sums0, sums1, sums2, qkv2, gain_ref, out_w_ref, top1, low1, top2, low2, sums3
):
    pick = spreader()
    length = len_ref[0]
    for head in range(heads):
        sums3[head] = sums_of(3, heads, head, length, qkv3, pick)
    sums3.push()
    for slot, qkv, top, low in ((1, qkv1, top1, low1), (2, qkv2, top2, low2)):
        parts = []
        for head in range(heads):
            q = parts_of(qkv, heads, head)[0]
            own = own_of(slot, heads, head, length, qkv)
            state = state_before(slot, old[head], (sums0[head], sums1[head], sums2[head], sums3[head]))
            parts.append(attend_part(slot, head, heads, length, q, own, state, gain_ref, pick))
        project_part(parts, heads, out_w_ref, top, low)


def fifth_kernel(
    heads, len_ref, olds, sums0, sums1, sums2, sums3, queries, own, gain_ref, out_w_ref, top0, low0, state_next
):
    pick = spreader()
    parts = []
    for head in range(heads):
        old = olds[head]
        sums = [part[head] for part in (sums0, sums1, sums2, sums3)]
        q = queries[:, head * F : (head + 1) * F]
        state = state_before(0, old, sums)
        parts.append(attend_part(0, head, heads, len_ref[0], q, own[head], state, gain_ref, pick))
        new = (old + (sums[0] + sums[1]) + (sums[2] + sums[3]))[:, :DH]
        state_next[0, F + 1 :, head, :] = new[:QUAD]
        state_next[0, 1 : F + 1, head, :] = new[QUAD : QUAD + F]
        state_next[0, 0:1, head, :] = new[QUAD + F : QUAD + F + 1]
    project_part(parts, heads, out_w_ref, top0, low0)


def add_kernel(top2, via_x, low1, via_y, two_y, two_x):
    two_y[...] = (top2[...].astype(F32) + via_x[...].astype(F32)).astype(BF)
    two_x[...] = (low1[...].astype(F32) + via_y[...].astype(F32)).astype(BF)


def total_kernel(top0, two_y, low0, two_x, out):
    out[0] = (top0[...].astype(F32) + two_y[...].astype(F32)).astype(BF)
    out.push(0)
    out[1] = (low0[...].astype(F32) + two_x[...].astype(F32)).astype(BF)
    out.push(1)


def placing_rank(owners_row, axis):
    down = lax.broadcasted_iota(jnp.int32, (DEC, DEC), 0)
    along = lax.broadcasted_iota(jnp.int32, (DEC, DEC), 1)
    earlier = down < along if axis == 0 else along < down
    return jnp.sum(jnp.where(earlier & (column(owners_row) == owners_row), 1, 0), axis=axis, keepdims=True)


def send_kernel(heads, capacity, tokens_ref, tail_ref, gain_ref, taps_ref, owner_ref, slot_ref, w_ref, out):
    tokens, factor = unit_rows(tokens_ref[...])
    normed = (tokens * factor * gain_ref[...].reshape(1, D)).astype(BF).astype(F32)
    tail = tail_ref[...].astype(F32)
    taps = taps_ref[...]
    conved = taps[0:1, :] * tail[:, 0, :] + taps[1:2, :] * tail[:, 1, :]
    conved = (conved + taps[2:3, :] * normed).astype(BF)
    owners = owner_ref[...]
    target = owners * capacity + placing_rank(owners, 0)
    placing = lax.broadcasted_iota(jnp.int32, (out.shape[0], DEC), 0) == target
    cache_slot = jnp.sum(jnp.where(placing, slot_ref[...] + 1, 0), axis=1, keepdims=True) - 1
    qkv = dot(conved, projection(w_ref, heads), ((1,), (1,))).astype(BF)
    sent = dot(ones_where(placing), qkv)
    lane = lax.broadcasted_iota(jnp.int32, sent.shape, 1)
    mark = 2 * heads * F + DH
    out[...] = jnp.where(lane == mark, cache_slot.astype(F32), sent).astype(BF)


def cache_spreaders(heads):
    lane, entry = lanes_of(PHI * heads)
    feature = lane >> (heads.bit_length() - 1)
    quad = feature - (1 + F)
    a = jnp.where(quad < 0, feature - 1, quad >> 4)
    return ones_where(a == entry), ones_where((quad >= 0) & ((quad & (F - 1)) == entry))


def slot_features(heads, items):
    mark = 2 * heads * F + DH
    first, second = cache_spreaders(heads)
    phis = []
    for head in range(heads):
        q = items[:, head * F : head * F + F]
        a = dot(q, first)
        b = dot(q, second)
        lane = lax.broadcasted_iota(jnp.int32, a.shape, 1)
        scale = jnp.where(lane < heads * (F + 1), 1.0 / math.sqrt(math.sqrt(F)), b * (1.0 / math.sqrt(2.0 * F)))
        value = jnp.where(lane < heads, 1.0, a * scale)
        phis.append(jnp.where((lane & (heads - 1)) == head, value, 0.0).astype(BF))
    slots = jnp.concatenate([items[:, mark : mark + 1].astype(F32)] * heads, axis=0)
    return jnp.concatenate(phis, axis=0), slots


def slot_copies(heads, start, count, cache_ref, state, sem):
    size = 2 * PHI * heads
    return [
        pltpu.make_async_copy(cache_ref.at[pl.ds(start * size // 2 + n * size, size)], state.at[pl.ds(n * size, size)], sem.at[n])
        for n in range(count // 2)
    ]


def slot_totals(heads, start, phis, slots, copies, state, total):
    span = PHI * heads
    waiting = list(copies)
    done = {}
    for n in range(2 * len(copies)):
        if n % 2 == 0:
            waiting.pop(0).wait()
        shift = n * span % 8
        rows = -(-(span + shift) // 8) * 8
        block = state[n * span - shift : n * span - shift + rows, :].astype(BF)
        done.setdefault(shift, []).append((n, block))
        if len(done[shift]) == 2:
            zeros = jnp.zeros((rows, WIDE - DH), BF)
            pair = [part for _, block in done[shift] for part in (block, zeros)]
            sides = [jnp.zeros((phis.shape[0], size), BF) for size in (shift, rows - span - shift)]
            wide = [side for side in (sides[0], phis, sides[1]) if side.shape[1] > 0]
            table = dot(jnp.concatenate(wide, axis=1), jnp.concatenate(pair, axis=1))
            for side, (place, _) in enumerate(done.pop(shift)):
                here = slots == float(start + place)
                total = total + jnp.where(here, table[:, side * WIDE : (side + 1) * WIDE], 0.0)
    return total


def serve_kernel(heads, items, cache_ref, total, state, sem):
    copies = slot_copies(heads, 0, 2 * sem.shape[0], cache_ref, state, sem)
    for copy in copies:
        copy.start()
    phis, slots = slot_features(heads, items)
    total[...] = slot_totals(heads, 0, phis, slots, copies, state, jnp.zeros(total.shape, F32))


def serve_part(heads, start, items, half_total, gain_ref, w_ref, copies, state, out):
    attended = []
    count = items.shape[0]
    phis, slots = slot_features(heads, items)
    total = slot_totals(heads, start, phis, slots, copies, state, half_total[...])
    gains = gain_ref[...].reshape(1, heads * DH)
    for head in range(heads):
        q = items[:, head * F : head * F + F].astype(F32)
        k = items[:, (heads + head) * F : (heads + head) * F + F].astype(F32)
        at = 2 * heads * F + head * WIDE
        v = items[:, at : at + DH].astype(F32)
        inner = jnp.sum(q * k, axis=-1, keepdims=True) * (1.0 / math.sqrt(F))
        value = total[head * count : (head + 1) * count, :DH] + (1.0 + inner + 0.5 * inner * inner) * v
        square = jnp.sum(value * value, axis=-1, keepdims=True)
        value = value * lax.rsqrt(square * (1.0 / DH) + 1e-05) * gains[:, head * DH : (head + 1) * DH]
        attended += [value.astype(BF), jnp.zeros((count, WIDE - DH), BF)]
    out[...] = dot(jnp.concatenate(attended, axis=1), out_projection(w_ref, heads)).astype(BF)


def return_kernel(capacity, items_ref, owner_ref, top0, one_x, low0, one_y, *outs):
    top, low = outs[4:]
    owners = owner_ref[...]
    target = column(owners) * capacity + placing_rank(owners, 1)
    placing = lax.broadcasted_iota(jnp.int32, (DEC, items_ref.shape[0]), 1) == target
    row = lax.broadcasted_iota(jnp.int32, (4 * TILE, DEC), 0)
    entry = lax.broadcasted_iota(jnp.int32, (4 * TILE, DEC), 1)
    device = lax.axis_index("head") ^ (row // TILE)
    wanted = ((row % TILE) < DEC // 4) & (entry == device * (DEC // 4) + row % TILE)
    wanted = dot(ones_where(wanted), ones_where(placing)).astype(BF)
    shares = dot(wanted, items_ref[...]).astype(BF)
    for slot, out in enumerate(outs[:4]):
        out[...] = shares[slot * TILE : (slot + 1) * TILE]
        out.push()
    top[...] = (top0[...].astype(F32) + one_x[...].astype(F32)).astype(BF)
    top.push()
    low[...] = (low0[...].astype(F32) + one_y[...].astype(F32)).astype(BF)


def far_off(array):
    return pltpu.with_memory_space_constraint(array, pltpu.HBM)


def entries(ref):
    return [ref.at[n] for n in range(ref.shape[0])]


class Fetched:
    def __init__(self, copies, place):
        self.copies, self.place, self.here = copies, place, set()
        self.shape, self.dtype = place.shape, place.dtype

    def __getitem__(self, index):
        entry = index[0] if isinstance(index, tuple) else index
        wanted = [entry] if len(self.copies) > 1 and isinstance(entry, int) else range(len(self.copies))
        for n in wanted:
            self.wait(n)
        return self.place[index]

    def wait(self, n):
        if n not in self.here:
            self.copies[n].wait()
            self.here.add(n)


class Pushed:
    def __init__(self, copies, place):
        self.copies, self.place, self.gone = copies, place, set()
        self.shape, self.dtype = place.shape, place.dtype

    def __getitem__(self, index):
        return self.place[index]

    def __setitem__(self, index, value):
        self.place[index] = value

    def push(self, entry=None):
        if (entry is None) == (len(self.copies) == 1):
            self.send(entry or 0)

    def send(self, n):
        if n not in self.gone:
            self.copies[n].start()
            self.gone.add(n)


class Near:
    def __init__(self, ref):
        self.ref, self.shape, self.dtype, self.copies = ref, ref.shape, ref.dtype, []

    def __getitem__(self, index):
        return self.ref[index]

    def __setitem__(self, index, value):
        self.ref[index] = value

    def push(self, entry=None):
        pass


def hbm_call(kernel, outs, flops, size, scalars=(), picked=None, waits=(), loose=(), here=(), near=(), split=(), split_out=(), raw=(), scratch=()):
    def run(*args):
        count, many = len(args), len(outs)
        moved = [n for n in range(count) if n not in here and n not in raw]
        far = [n for n in range(many) if n not in near]

        def shape_in(n):
            return args[n].shape[2:] if n == picked else args[n].shape

        pieces = sum(shape_in(n)[0] if n in split else 1 for n in moved)
        pieces += sum(outs[n].shape[0] if n in split_out else 1 for n in far)

        def body(*refs):
            refs = list(refs)

            def take(number):
                taken = refs[:number]
                del refs[:number]
                return taken

            numbers, sources, _, targets = take(len(scalars)), take(count), take(len(waits)), take(many)
            places, results, own, (sem,) = dict(zip(moved, take(len(moved)))), dict(zip(far, take(len(far)))), take(len(scratch)), refs
            used = iter(range(pieces))

            def copies(source, target, apart):
                pairs = zip(entries(source), entries(target)) if apart else [(source, target)]
                return [pltpu.make_async_copy(a, b, sem.at[next(used)]) for a, b in pairs]

            ins = []
            for n, source in enumerate(sources):
                if n in here or n in raw:
                    ins.append(source)
                    continue
                if n == picked:
                    source = source.at[0, numbers[-1][0]]
                fetched = Fetched(copies(source, places[n], n in split), places[n])
                for copy in fetched.copies:
                    copy.start()
                ins.append(fetched)
            done = [
                Pushed(copies(results[n], target, n in split_out), results[n]) if n in far else Near(target)
                for n, target in enumerate(targets)
            ]
            kernel(*numbers[: len(scalars) - (picked is not None)], *ins, *done, *own)
            for n in far:
                for entry in range(len(done[n].copies)):
                    done[n].send(entry)
            for n in moved:
                for entry in range(len(ins[n].copies)):
                    ins[n].wait(entry)
            for n in far:
                for copy in done[n].copies:
                    copy.wait()

        hbm = pl.BlockSpec(memory_space=pltpu.HBM)
        in_vmem = pl.BlockSpec(memory_space=pltpu.VMEM)
        anywhere = pl.BlockSpec(memory_space=pl.ANY)
        free = set(loose) | set(here)
        return pl.pallas_call(
            body,
            out_shape=[o if n in near else pltpu.HBM(o.shape, o.dtype) for n, o in enumerate(outs)],
            in_specs=[pl.BlockSpec(memory_space=pltpu.SMEM)] * len(scalars)
            + [in_vmem if n in here else anywhere if n in loose else hbm for n in range(count)]
            + [hbm] * len(waits),
            out_specs=[in_vmem if n in near else hbm for n in range(many)],
            scratch_shapes=[pltpu.VMEM(shape_in(n), args[n].dtype) for n in moved]
            + [pltpu.VMEM(outs[n].shape, outs[n].dtype) for n in far]
            + list(scratch)
            + [pltpu.SemaphoreType.DMA((pieces,))],
            compiler_params=pltpu.CompilerParams(vmem_limit_bytes=40 * MIB),
            cost_estimate=pl.CostEstimate(flops=flops, bytes_accessed=size, transcendentals=0),
        )(*scalars, *[a if n in free else far_off(a) for n, a in enumerate(args)], *map(far_off, waits))

    return run


def shape(*dims, dtype=BF):
    return jax.ShapeDtypeStruct(dims, dtype)


def across(array, by):
    return lax.ppermute(array, "head", [(i, i ^ by) for i in range(4)])


def local_square(
    stretch_tokens,
    stretch_tail,
    decode_tokens,
    decode_tail,
    norm_gain,
    conv_taps,
    qkv_weight,
    out_gain,
    out_weight,
    state_cache,
    stretch_len,
    stretch_slot,
    decode_slot,
    decode_owner,
):
    heads = qkv_weight.shape[1]
    rows = stretch_tokens.shape[1]
    half = rows // 2
    wide = heads * (2 * F + WIDE)
    w_in = jnp.transpose(qkv_weight, (1, 2, 0))
    cache = jnp.transpose(state_cache, (0, 1, 4, 2, 3))
    length = stretch_len.astype(jnp.int32)
    slot = stretch_slot.astype(jnp.int32)
    hbm = pl.BlockSpec(memory_space=pltpu.HBM)
    piece = shape(half, D)
    block_flops = 2 * rows * D * wide + 6 * heads * rows * rows * WIDE
    attend_flops = 2 * rows * heads * WIDE * (D + PHI_WIDE)
    size = 4 * rows * D

    low, top, begin, end = hbm_call(conv_kernel, [piece, piece, shape(TILE, D), shape(TILE, D)], 20 * rows * D, size)(
        stretch_tokens[0], stretch_tail[0], norm_gain, conv_taps
    )
    low_x = across(low, 1)
    low_y = across(low, 2)
    end = from_behind(end, "head", 1)

    groups = lax.axis_size("tok")
    capacity = max(2, 2 * DEC // groups)
    count = groups * capacity
    owner_row = decode_owner.reshape(1, DEC)
    (sent,) = hbm_call(functools.partial(send_kernel, heads, capacity), [shape(count, wide)], 2 * DEC * D * wide, 2 * D * wide)(
        decode_tokens[0], decode_tail[0], norm_gain, conv_taps, owner_row, decode_slot, w_in
    )
    top = pl.pallas_call(
        lambda first_ref, top_ref, begin_ref, end_ref, taps_ref, wait_ref, *refs: rim_kernel(
            first_ref, top_ref, begin_ref, end_ref, taps_ref, *refs
        ),
        out_shape=pltpu.HBM((half, D), BF),
        in_specs=[pl.BlockSpec(memory_space=pltpu.SMEM), hbm, hbm, pl.BlockSpec(memory_space=pl.ANY), hbm, hbm],
        out_specs=hbm,
        scratch_shapes=[pltpu.VMEM((TILE, D), BF), pltpu.VMEM((TILE, D), BF), pltpu.VMEM((3, D), F32), pltpu.VMEM((TILE, D), BF)]
        + [pltpu.SemaphoreType.DMA((4,))],
        input_output_aliases={1: 0},
        compiler_params=pltpu.CompilerParams(vmem_limit_bytes=40 * MIB),
        cost_estimate=pl.CostEstimate(flops=16 * D, bytes_accessed=128 * D, transcendentals=0),
    )(lax.axis_index("head").reshape(1), far_off(top), far_off(begin), end, far_off(conv_taps), far_off(sent))
    top_x = across(top, 1)
    top_y = across(top, 2)
    items = lax.all_to_all(sent.reshape(groups, capacity, wide), "tok", split_axis=0, concat_axis=0, tiled=True)

    sums, own, queries = shape(heads, PHI_WIDE, WIDE, dtype=F32), shape(heads, rows, WIDE, dtype=F32), shape(rows, heads * F)
    sums0, own0, queries0 = hbm_call(
        functools.partial(first_kernel, heads),
        [sums, own, queries],
        block_flops,
        size,
        scalars=[length],
    )(low, top, w_in)
    items = items.reshape(count, wide)
    slots = cache.shape[1]
    flat = cache.reshape(slots * PHI * heads, DH)
    states = [pltpu.VMEM((slots // 2 * PHI * heads, DH), F32), pltpu.SemaphoreType.DMA((slots // 4,))]
    serve_flops = slots * heads * heads * DH * PHI * count
    (half_total,) = hbm_call(
        functools.partial(serve_kernel, heads),
        [shape(heads * count, WIDE, dtype=F32)],
        serve_flops,
        2 * slots * heads * WIDE * PHI,
        loose=(0,),
        raw=(1,),
        scratch=states,
        waits=[queries0],
    )(items, flat)
    low_y, top_x, low_x = lax.optimization_barrier((low_y, top_x, low_x, half_total))[:3]
    low_xy = across(low_y, 1)
    top_xy = across(top_x, 2)
    blocks = shape(rows, wide)
    sums1, qkv1, sums2, qkv2, state3, served, old = hbm_call(
        functools.partial(second_kernel, heads),
        [sums, blocks, sums, blocks, shape(heads, PHI_WIDE, WIDE), shape(count, D), sums],
        2 * block_flops + serve_flops,
        2 * slots * heads * WIDE * PHI,
        scalars=[length, slot],
        picked=5,
        loose=(0, 1, 3, 4, 7),
        here=(2,),
        near=(4,),
        raw=(11,),
        scratch=states,
    )(low_x, top_x, w_in, low_y, top_y, cache, sums0, items, half_total, out_gain, out_weight, flat)
    top3, low3, qkv3 = hbm_call(
        functools.partial(third_kernel, heads),
        [piece, piece, blocks],
        block_flops + attend_flops,
        size,
        scalars=[length],
        loose=(0, 1),
        near=(0, 1),
        here=(2, 3, 5),
        waits=[qkv2],
    )(low_xy, top_xy, w_in, state3, out_gain, out_weight)

    via_x = across(top3, 1)
    via_y = across(low3, 2)
    served = lax.optimization_barrier((served, top3))[0]
    returned = lax.all_to_all(served.reshape(groups, capacity, D), "tok", split_axis=0, concat_axis=0, tiled=True)
    returned = returned.reshape(count, D)
    top1, low1, top2, low2, sums3 = hbm_call(
        functools.partial(fourth_kernel, heads),
        [piece] * 4 + [sums],
        2 * attend_flops,
        size,
        scalars=[length],
        here=(8,),
    )(qkv3, qkv1, old, sums0, sums1, sums2, qkv2, out_gain, out_weight)
    one_x = across(top1, 1)
    one_y = across(low2, 2)
    two_y, two_x = hbm_call(add_kernel, [piece, piece], 0, size, here=(1, 3), near=(0, 1), waits=[top1])(top2, via_x, low1, via_y)
    top0, low0, state_next = hbm_call(
        functools.partial(fifth_kernel, heads),
        [piece] * 2 + [shape(1, PHI, heads, DH, dtype=F32)],
        attend_flops,
        size,
        scalars=[length],
        waits=[two_x],
    )(old, sums0, sums1, sums2, sums3, queries0, own0, out_gain, out_weight)
    *decoded, top0, low0 = hbm_call(
        functools.partial(return_kernel, capacity),
        [shape(TILE, D)] * 4 + [piece] * 2,
        2 * DEC * count * D,
        4 * count * D,
        loose=(0, 3, 5),
    )(returned, owner_row, top0, one_x, low0, one_y)
    shares = [decoded[0]] + [across(decoded[by], by) for by in (1, 2, 3)]
    two_y = across(two_y, 2)
    two_x = across(two_x, 1)
    state_next = jnp.transpose(state_next, (0, 2, 3, 1))
    (stretch_out,) = hbm_call(
        total_kernel,
        [shape(2, half, D)],
        0,
        8 * rows * D,
        loose=(1, 3),
        split_out=(0,),
        waits=[decoded[0]],
    )(top0, two_y, low0, two_x)
    shares = lax.optimization_barrier((*shares, stretch_out))[:4]
    decode_out = sum(share[: DEC // 4].astype(F32) for share in shares).astype(BF)
    return (stretch_out.reshape(1, rows, D), decode_out[None], state_next)


def from_behind(array, axis, by):
    peers = lax.axis_size(axis)
    pairs = [(i, i + by) for i in range(peers) if 0 <= i + by < peers]
    return lax.ppermute(array, axis, pairs)


def rms_rows(values, gain):
    values = values.astype(jnp.float32)
    factor = lax.rsqrt(jnp.mean(values * values, axis=-1, keepdims=True) + 1e-05)
    return values * factor * gain


def features(vectors):
    breadth = vectors.shape[-1]
    linear = vectors / math.sqrt(math.sqrt(breadth))
    outer = vectors[..., :, None] * vectors[..., None, :] / math.sqrt(2.0 * breadth)
    outer = outer.reshape(vectors.shape[:-1] + (breadth * breadth,))
    ones = jnp.ones(vectors.shape[:-1] + (1,), vectors.dtype)
    return jnp.concatenate([ones, linear, outer], axis=-1)


def convolve(tail, normed, conv_taps):
    joined = jnp.concatenate([tail, normed], axis=-2).astype(jnp.float32)
    span_rows = normed.shape[-2]
    total = conv_taps[0] * joined[..., 0:span_rows, :]
    total = total + conv_taps[1] * joined[..., 1 : span_rows + 1, :]
    total = total + conv_taps[2] * joined[..., 2 : span_rows + 2, :]
    return total.astype(jnp.bfloat16)


def decode_items(items, slot_items, cache_own, out_gain, head_count):
    item_count = items.shape[0]
    shaped = items.reshape(item_count, head_count, 2 * F + DH).astype(jnp.float32)
    queries = shaped[:, :, :F]
    key_feats = shaped[:, :, F : 2 * F]
    values = shaped[:, :, 2 * F :]
    slot_total = cache_own.shape[0]
    table = jnp.einsum(
        "nhp,shdp->nshd", features(queries), cache_own, precision=lax.Precision.HIGHEST
    )
    picker = (slot_items[:, None] == jnp.arange(slot_total)[None, :]).astype(jnp.float32)
    carried = jnp.einsum("ns,nshd->nhd", picker, table, precision=lax.Precision.HIGHEST)
    inner = jnp.sum(queries * key_feats, axis=-1) / math.sqrt(F)
    own_term = (1.0 + inner + 0.5 * inner * inner)[..., None] * values
    attended = rms_rows(carried + own_term, out_gain.reshape(head_count, DH))
    return attended.astype(jnp.bfloat16).reshape(item_count, head_count * DH)


def local(
    stretch_tokens,
    stretch_tail,
    decode_tokens,
    decode_tail,
    norm_gain,
    conv_taps,
    qkv_weight,
    out_gain,
    out_weight,
    state_cache,
    stretch_len,
    stretch_slot,
    decode_slot,
    decode_owner,
):
    head_count = qkv_weight.shape[1]
    block_width = qkv_weight.shape[2]
    rows_own = stretch_tokens.shape[1]
    w_flat = qkv_weight.reshape(D, head_count * block_width)
    gains = out_gain.reshape(head_count, DH)
    normed = rms_rows(stretch_tokens[0], norm_gain).astype(jnp.bfloat16)
    rim_rows = from_behind(normed[rows_own - 2 :], "head", 1)
    first_dev = lax.axis_index("head") == 0
    rim_rows = jnp.where(first_dev, stretch_tail[0], rim_rows)
    conved = convolve(rim_rows, normed, conv_taps)
    grouped = jnp.dot(
        lax.all_gather(conved, "head", axis=0, tiled=True),
        w_flat,
        preferred_element_type=jnp.float32,
    ).astype(jnp.bfloat16)
    grouped = grouped.reshape(STRETCH, head_count, block_width)
    queries = grouped[:, :, :F]
    key_feats = grouped[:, :, F : 2 * F]
    values = grouped[:, :, 2 * F :]
    length = stretch_len[0]
    positions = jnp.arange(STRETCH)
    valid_rows = positions < length
    state_old = lax.dynamic_index_in_dim(state_cache[0], stretch_slot[0], 0, keepdims=False)
    carried = jnp.einsum(
        "ihp,hdp->ihd",
        features(queries.astype(jnp.float32)),
        state_old,
        precision=lax.Precision.HIGHEST,
    )
    block_rows = min(512, STRETCH)
    pieces = []
    for anchor in range(0, STRETCH, block_rows):
        finish = anchor + block_rows
        inner = jnp.einsum(
            "ihf,jhf->hij",
            queries[anchor:finish],
            key_feats[:finish],
            preferred_element_type=jnp.float32,
        ) / math.sqrt(F)
        weights = 1.0 + inner + 0.5 * inner * inner
        allowed = (positions[None, :finish] <= positions[anchor:finish, None]) & valid_rows[
            None, :finish
        ]
        weights = jnp.where(allowed[None], weights, 0.0).astype(jnp.bfloat16)
        pieces.append(
            jnp.einsum("hij,jhd->ihd", weights, values[:finish], preferred_element_type=jnp.float32)
        )
    local_sum = jnp.concatenate(pieces, axis=0)
    attended = rms_rows(carried + local_sum, gains)
    attended = (
        jnp.where(valid_rows[:, None, None], attended, 0.0)
        .astype(jnp.bfloat16)
        .reshape(STRETCH, head_count * DH)
    )
    key_phi = jnp.where(
        valid_rows[:, None, None], features(key_feats.astype(jnp.float32)), 0.0
    ).astype(jnp.bfloat16)
    state_next = state_old + jnp.einsum(
        "jhd,jhp->hdp", values, key_phi, preferred_element_type=jnp.float32
    )
    part_rows = attended
    stretch_out = lax.psum_scatter(
        jnp.dot(part_rows, out_weight, preferred_element_type=jnp.float32).astype(jnp.bfloat16),
        "head",
        scatter_dimension=0,
        tiled=True,
    )
    dec_normed = rms_rows(decode_tokens[0], norm_gain).astype(jnp.bfloat16)
    dec_conved = convolve(decode_tail[0], dec_normed[:, None, :], conv_taps)[:, 0, :]
    dec_qkv = jnp.dot(dec_conved, w_flat, preferred_element_type=jnp.float32).astype(jnp.bfloat16)
    owners = decode_owner[0, :, 0]
    slots_here = decode_slot[0]
    groups = lax.axis_size("tok")
    capacity = max(2, 2 * DEC // groups)
    earlier = jnp.arange(DEC)[None, :] < jnp.arange(DEC)[:, None]
    same_owner = owners[None, :] == owners[:, None]
    rank_in = jnp.sum(earlier & same_owner, axis=1)
    target = owners * capacity + rank_in
    placing = jnp.arange(groups * capacity)[:, None] == target[None, :]
    sent_rows = jnp.dot(
        placing.astype(jnp.bfloat16), dec_qkv, preferred_element_type=jnp.float32
    ).astype(jnp.bfloat16)
    sent_rows = sent_rows.reshape(groups, capacity, head_count * block_width)
    sent_slots = jnp.sum(jnp.where(placing, slots_here[None, :] + 1, 0), axis=1) - 1
    sent_slots = sent_slots.reshape(groups, capacity)
    item_rows = lax.all_to_all(sent_rows, "tok", split_axis=0, concat_axis=0, tiled=True)
    item_slots = lax.all_to_all(sent_slots, "tok", split_axis=0, concat_axis=0, tiled=True)
    item_count = item_rows.shape[1]
    flat_out = decode_items(
        item_rows.reshape(groups * item_count, head_count * block_width),
        item_slots.reshape(groups * item_count),
        state_cache[0],
        out_gain,
        head_count,
    )
    served = flat_out.reshape(groups, item_count, head_count * DH)
    returned = lax.all_to_all(served, "tok", split_axis=0, concat_axis=0, tiled=True)
    dec_attended = jnp.dot(
        jnp.transpose(placing).astype(jnp.bfloat16),
        returned.reshape(groups * capacity, head_count * DH),
        preferred_element_type=jnp.float32,
    ).astype(jnp.bfloat16)
    part_rows = dec_attended
    decode_out = lax.psum_scatter(
        jnp.dot(part_rows, out_weight, preferred_element_type=jnp.float32).astype(jnp.bfloat16),
        "head",
        scatter_dimension=0,
        tiled=True,
    )
    return (stretch_out[None], decode_out[None], state_next[None])


def solution(mesh):
    in_specs = (
        P("tok", "head", None),
        P("tok", None, None),
        P("tok", None, None),
        P("tok", None, None, None),
        P(),
        P(),
        P(None, "head", None),
        P("head"),
        P("head", None),
        P("tok", None, "head", None, None),
        P("tok"),
        P("tok"),
        P("tok", None),
        P("tok", None, None),
    )
    out_specs = (P("tok", "head", None), P("tok", "head", None), P("tok", "head", None, None))
    chosen = local_square if mesh.shape["head"] == 4 else local
    return jax.shard_map(chosen, mesh=mesh, in_specs=in_specs, out_specs=out_specs, check_vma=False)
```
